32 devices in a mesh: rows: 8 (over z, y), cols: 4 (over x, core).
Axes of the slice: x: 2, y: 2, z: 4, core: 2. Of those that a mesh axis runs over, the one named last changes fastest.
Arguments:
- block_input: float32 [4, 256, 256, 256], P(None, 'rows', 'cols'), may hold values from -6 to 6
- first_kernel: float32 [3, 3, 256, 64], replicated, may hold values from -0.25 to 0.25
- first_bias: float32 [64], replicated, may hold values from -3 to 3
- second_kernel: float32 [3, 3, 64, 64], replicated, may hold values from -0.375 to 0.375
- second_bias: float32 [64], replicated, may hold values from -3 to 3
- third_kernel: float32 [3, 3, 64, 64], replicated, may hold values from -0.375 to 0.375
- third_bias: float32 [64], replicated, may hold values from -3 to 3
- out_kernel: float32 [64, 256], replicated, may hold values from -64 to 64
- out_bias: float32 [256], replicated, may hold values from -96 to 96
- output_cotangent: float32 [4, 256, 256, 256], P(None, 'rows', 'cols'), may hold values from -6 to 6
- image_heights: int32 [4], replicated, may hold values from 64 to 256, as said below
- image_widths: int32 [4], replicated, may hold values from 64 to 256, as said below
Outputs:
- block_output: float32 [4, 256, 256, 256], P(None, 'rows', 'cols')
- input_grad: float32 [4, 256, 256, 256], P(None, 'rows', 'cols')
- first_kernel_grad: float32 [3, 3, 256, 64], replicated
- first_bias_grad: float32 [64], replicated
- second_kernel_grad: float32 [3, 3, 64, 64], replicated
- second_bias_grad: float32 [64], replicated
- third_kernel_grad: float32 [3, 3, 64, 64], replicated
- third_bias_grad: float32 [64], replicated
- out_kernel_grad: float32 [64, 256], replicated
- out_bias_grad: float32 [256], replicated
The draws below stay inside these ranges and needn't reach their ends.
Inputs may be any that keep to these rules, and one draw needn't show every extreme that they name: An image's valid pixels are its top-left image_heights x image_widths rectangle; some image, chosen from the seed, has the full height 256. `image_widths`: some image, chosen from the seed, has the full width 256.
All inputs are finite; a program needn't handle non-finite values.
Results may differ from the reference program's by a relative error of at most 0.0003.
Values sent between devices are 32-bit elements; how exact they have to be, the bound alone decides.
A program may use at most 320 MiB of HBM per device.

```python
import jax
import jax.numpy as jnp
from jax import lax

CIN = 256
CMID = 64
IMAGES = 4
H = 256
W = 256


def full_image(key):
    return jax.random.randint(key, (), 0, IMAGES)


def draw_image_heights(key, part):
    chosen = full_image(key)
    key = jax.random.fold_in(key, 11)
    sampled = jax.random.randint(key, (IMAGES,), H // 4, H + 1)
    return jnp.where(jnp.arange(IMAGES) == chosen, H, sampled).astype(jnp.int32)


def draw_image_widths(key, part):
    chosen = (full_image(key) + 1) % IMAGES
    key = jax.random.fold_in(key, 12)
    sampled = jax.random.randint(key, (IMAGES,), W // 4, W + 1)
    return jnp.where(jnp.arange(IMAGES) == chosen, W, sampled).astype(jnp.int32)


def levels(own_key, dims, cuts, low, high):
    factor_of, own = 1.0, jax.random.fold_in(own_key, 6)
    for axis_at, blocks in cuts:
        steps = jnp.exp(jax.random.uniform(jax.random.fold_in(own, axis_at), (blocks,), jnp.float32, low / len(cuts), high / len(cuts)))
        factor_of = factor_of * jnp.repeat(steps, dims[axis_at] // blocks).reshape([-1 if axis == axis_at else 1 for axis in range(len(dims))])
    return factor_of


def noise(stream_key, dims, deviation, bound, split=(), held_as=jnp.bfloat16):
    values = deviation * jax.random.normal(stream_key, dims, jnp.float32)
    if split:
        values = values * levels(stream_key, dims, split, -0.22, 0.18)
    return jnp.clip(values, -bound, bound).astype(held_as)


def setup_inputs(seed: int = 0) -> dict:
    arg_keys = jax.random.split(jax.random.key(seed), 13)
    return {
        "block_input": noise(arg_keys[0], (IMAGES, H, W, CIN), 1.0, 6.0, ((1, 8), (2, 4)), jnp.float32),
        "first_kernel": noise(arg_keys[1], (3, 3, CIN, CMID), (9 * CIN // 4) ** -0.5, 0.25, (), jnp.float32),
        "first_bias": noise(arg_keys[2], (CMID,), 0.5, 3.0, (), jnp.float32),
        "second_kernel": noise(arg_keys[3], (3, 3, CMID, CMID), (9 * CMID // 2) ** -0.5, 0.375, (), jnp.float32),
        "second_bias": noise(arg_keys[4], (CMID,), 0.5, 3.0, (), jnp.float32),
        "third_kernel": noise(arg_keys[5], (3, 3, CMID, CMID), (9 * CMID // 2) ** -0.5, 0.375, (), jnp.float32),
        "third_bias": noise(arg_keys[6], (CMID,), 0.5, 3.0, (), jnp.float32),
        "out_kernel": noise(arg_keys[7], (CMID, CIN), 12.0, 64.0, (), jnp.float32),
        "out_bias": noise(arg_keys[8], (CIN,), 16.0, 96.0, (), jnp.float32),
        "output_cotangent": noise(arg_keys[9], (IMAGES, H, W, CIN), 1.0, 6.0, ((1, 8), (2, 4)), jnp.float32),
        "image_heights": draw_image_heights(jax.random.fold_in(arg_keys[12], 71), 0),
        "image_widths": draw_image_widths(jax.random.fold_in(arg_keys[12], 71), 0),
    }


@jax.custom_vjp
def low(v):
    return lax.optimization_barrier(v.astype(jnp.bfloat16)).astype(jnp.float32)

@jax.custom_vjp
def low_back(v):
    return v

def low_keep(v):
    return (low(v), None)

def low_pass(kept, grad):
    return (grad,)

def back_keep(v):
    return (v, None)

def back_low(kept, grad):
    return (low(grad),)
low.defvjp(low_keep, low_pass)
low_back.defvjp(back_keep, back_low)
post_gain = 1.0 / 64.0
layout = ('NHWC', 'HWIO', 'NHWC')

def convolve(values, kernel):
    return lax.conv_general_dilated(values, kernel, (1, 1), 'SAME', dimension_numbers=layout, precision=lax.Precision.HIGHEST)

def residual_block(block_input, first_kernel, first_bias, second_kernel, second_bias, third_kernel, third_bias, out_kernel, out_bias):
    hidden = convolve(jax.nn.silu(block_input), first_kernel) + first_bias
    hidden = convolve(jax.nn.silu(hidden), second_kernel) + second_bias
    hidden = convolve(jax.nn.silu(hidden), third_kernel) + third_bias
    branch = jnp.einsum('nhwc,cd->nhwd', jax.nn.silu(hidden), out_kernel, precision=lax.Precision.HIGHEST) + out_bias
    return block_input + post_gain * branch

def reference(block_input, first_kernel, first_bias, second_kernel, second_bias, third_kernel, third_bias, out_kernel, out_bias, output_cotangent, image_heights, image_widths):
    height = block_input.shape[1]
    breadth = block_input.shape[2]
    row_valid = jnp.arange(height, dtype=jnp.int32)[None, :, None] < image_heights[:, None, None]
    col_valid = jnp.arange(breadth, dtype=jnp.int32)[None, None, :] < image_widths[:, None, None]
    pixel_mask = jnp.logical_and(row_valid, col_valid).astype(jnp.float32)[..., None]
    result, pullback = jax.vjp(residual_block, block_input, first_kernel, first_bias, second_kernel, second_bias, third_kernel, third_bias, out_kernel, out_bias)
    gradients = pullback(output_cotangent * pixel_mask)
    return (result, gradients[0], gradients[1], gradients[2], gradients[3], gradients[4], gradients[5], gradients[6], gradients[7], gradients[8])
```

```python
import functools

import jax
import jax.numpy as jnp
from jax import lax
from jax.experimental import pallas as pl
from jax.experimental.pallas import tpu as pltpu
from jax.sharding import PartitionSpec as P

MESH = pl.DeviceIdType.MESH
bf16 = jnp.bfloat16
f32 = jnp.float32
LANES = 128
NN = (((1,), (0,)), ((), ()))
NT = (((1,), (1,)), ((), ()))
GAIN = 1.0 / 64.0
EXCHANGES = 6
GOES = ((0, 1), (0, -1), (1, 0), (-1, 0), (1, 1), (1, -1), (-1, 1), (-1, -1))


def dot(a, b, dims=NN):
    return lax.dot_general(a, b, dims, preferred_element_type=f32)


def halves(v):
    hi = v.astype(bf16)
    return hi, (v - hi.astype(f32)).astype(bf16)


def sigmoid(v):
    return 0.5 + 0.5 * jnp.tanh(0.5 * v)


def cat(parts, axis):
    return jnp.concatenate(parts, axis=axis)


def lane_column(width):
    return lax.broadcasted_iota(jnp.int32, (1, LANES), 1) % width


class Sizes:
    def __init__(self, shape, mid, rows, cols):
        self.images, self.height, self.width, self.wide = shape
        self.mid = mid
        self.rows, self.cols = rows, cols
        self.per_group = LANES // self.width
        self.groups = self.images // self.per_group
        self.block = 8
        self.blocks = self.height // self.block
        self.devices = rows * cols
        taps = 9 * mid
        self.wide_units = taps // 8 * (self.wide // LANES)
        self.used = self.wide_units + 72 + 20 + 8
        self.shard = -(-self.used // self.devices)
        self.units = self.shard * self.devices
        self.low = 2
        self.near = (cols // 2) * self.low
        self.far = rows // self.low


def kernel_a(sz, refs):
    (x_hbm, dy_hbm, heights, widths, w1, w2, w3, t3, t2, ko, bias, q_hbm, a3_hbm, sums_out) = refs["io"]
    G, H, W, M = sz.groups, sz.height, sz.width, sz.mid
    RB, NB = sz.block, sz.blocks
    me_r, me_c = lax.axis_index("rows"), lax.axis_index("cols")
    col = lane_column(W)
    first, last = col == 0, col == W - 1
    n3 = 3 * M

    def exists(dr, dc):
        ok = None
        for here, step, count in ((me_r, dr, sz.rows), (me_c, dc, sz.cols)):
            if step:
                near = (here + step >= 0) & (here + step < count)
                ok = near if ok is None else ok & near
        return ok

    buf = refs["buf"]

    def in_copy(src, which, g, k):
        n0 = g * sz.per_group
        return pltpu.make_async_copy(
            src.at[pl.ds(n0, sz.per_group), pl.ds(k * RB, RB)],
            buf.at[pl.ds(n0, sz.per_group), pl.ds(k * RB, RB)],
            refs["in_sem"].at[which, g, k],
        )

    for g in range(G):
        for k in range(NB):
            in_copy(x_hbm, 0, g, k).start()

    core, rest, low, far = me_c % 2, me_c // 2, me_r % sz.low, me_r // sz.low
    near_at = rest * sz.low + low

    def near_id(k):
        return (far * sz.low + k % sz.low, (k // sz.low) * 2 + core)

    def far_id(k):
        return (k * sz.low + low, me_c)

    pair_id = (me_r, me_c + 1 - 2 * core)
    near_ids = [near_id(lax.rem(near_at + d, sz.near)) for d in range(1, sz.near)]
    far_ids = [far_id(lax.rem(far + d, sz.far)) for d in range(1, sz.far)]

    refs["big"][...] = jnp.zeros_like(refs["big"])
    refs["corner"][...] = jnp.zeros_like(refs["corner"])

    barrier = pltpu.get_barrier_semaphore()
    count = 1 + len(near_ids) + len(far_ids)
    for dev in [pair_id] + near_ids + far_ids:
        pl.semaphore_signal(barrier, inc=1, device_id=dev, device_id_type=MESH)
    for dr, dc in GOES:
        ok = exists(dr, dc)
        count = count + jnp.where(ok, 1, 0)

        @pl.when(ok)
        def _():
            pl.semaphore_signal(barrier, inc=1, device_id=(me_r + dr, me_c + dc), device_id_type=MESH)

    pl.semaphore_wait(barrier, count)

    def message(e, g, slot):
        dr, dc = GOES[slot]
        if slot < 2:
            src, dst = refs["msg"].at[e, g], refs["big"].at[e, g, slot]
        elif slot < 4:
            src, dst = refs["rowmsg"].at[e, g, 3 - slot], refs["big"].at[e, g, slot]
        else:
            src, dst = refs["cormsg"].at[e, g, 1 if dr > 0 else 0], refs["corner"].at[e, g, slot - 4]
        return pltpu.make_async_remote_copy(
            src_ref=src,
            dst_ref=dst,
            send_sem=refs["send"].at[e, g, slot],
            recv_sem=refs["recv"].at[e, g, slot],
            device_id=(me_r + dr, me_c + dc),
            device_id_type=MESH,
        )

    def send(e, g, top, bottom, top_rim, bottom_rim):
        refs["rowmsg"][e, g, 0] = top
        refs["rowmsg"][e, g, 1] = bottom
        refs["cormsg"][e, g, 0] = pack_corner(top_rim)
        refs["cormsg"][e, g, 1] = pack_corner(bottom_rim)
        for slot in range(8):
            dr, dc = GOES[slot]

            @pl.when(exists(dr, dc))
            def _():
                message(e, g, slot).start()

    def receive(e, g):
        for slot in range(8):
            dr, dc = GOES[slot]

            @pl.when(exists(-dr, -dc))
            def _():
                message(e, g, slot).wait_recv()

    def pack(held, value, u):
        moved = pltpu.roll(value, lax.rem(LANES + 1 + 2 * u, LANES), 1)
        return jnp.where(col // 2 == u, moved, held)

    def pack_corner(value):
        held = jnp.zeros((8, LANES), f32)
        for k in range(M // 8):
            held = jnp.where(col // 2 == k, pltpu.roll(value[8 * k : 8 * k + 8], 1 + 2 * k, 1), held)
        return held

    def from_left(held, u):
        return pltpu.roll(held, LANES - W - 2 * u, 1)

    def from_right(held, u):
        return pltpu.roll(held, W - 2 - 2 * u, 1)

    def corner_left(held):
        return cat([pltpu.roll(held, LANES - W - 2 * k, 1) for k in range(M // 8)], 0)

    def corner_right(held):
        return cat([pltpu.roll(held, W - 2 - 2 * k, 1) for k in range(M // 8)], 0)

    def rows_loop(body):
        def step(b, carry):
            body(b)
            return carry

        lax.fori_loop(0, NB, step, 0)

    def conv_first(g):
        a0, z, carry = refs["a0"][g], refs["slope3"][g], refs["carry"][g]
        carry[...] = jnp.zeros_like(carry)
        refs["msg"][0, g] = jnp.zeros((M, LANES), f32)

        def emit(row, s, held):
            s0, s1, s2 = s[:M], s[M : 2 * M], s[2 * M :]
            value = s1 + jnp.where(first, 0.0, pltpu.roll(s0, 1, 1))
            value = value + jnp.where(last, 0.0, pltpu.roll(s2, LANES - 1, 1))
            z[row + 1] = value
            rim = jnp.where(first, s2, s0)
            return rim, pack(held, rim, row)

        def body(b):
            for k in range(NB):
                @pl.when(b == k)
                def _():
                    in_copy(x_hbm, 0, g, k).wait()

            held = refs["msg"][0, g]
            c0, c1 = carry[0], carry[1]
            for m in range(RB // 2):
                r = b * RB + 2 * m
                pair = []
                for i in range(2):
                    v = cat([buf[g * sz.per_group + s, r + i] for s in range(sz.per_group)], 0)
                    hi, lo = halves(v * sigmoid(v))
                    both = cat([hi, lo], 1)
                    a0[r + i] = both
                    pair.append(both)
                rhs = cat(pair, 0)
                y = dot(w1[...], cat([rhs, rhs[:, : sz.wide]], 1), NT)
                ya, yb = y[:, :LANES], y[:, LANES:]
                rim, held = emit(r - 1, c0 + ya[2 * n3 :], held)
                if m == 0:
                    refs["rim"][jnp.minimum(b, 1)] = rim
                _, held = emit(r, c1 + ya[n3 : 2 * n3] + yb[2 * n3 :], held)
                c0, c1 = ya[:n3] + yb[n3 : 2 * n3], yb[:n3]
            carry[0] = c0
            carry[1] = c1
            refs["msg"][0, g] = held

        rows_loop(body)
        _, held = emit(H - 1, carry[0], refs["msg"][0, g])
        rim, _ = emit(H, carry[1], held)
        refs["msg"][0, g] = held
        for k in range(NB):
            in_copy(dy_hbm, 1, g, k).start()
        send(0, g, z[0], z[H + 1], refs["rim"][0], rim)

    def after_first(g):
        z, act, slope = refs["slope3"][g], refs["act"][g], refs["slope1"][g]
        receive(0, g)
        big, corner = refs["big"], refs["corner"]
        for row, at in ((1, 0), (H, 2)):
            z[row] += (
                big[0, g, 2 + at // 2]
                + jnp.where(first, corner_left(corner[0, g, at]), 0.0)
                + jnp.where(last, corner_right(corner[0, g, at + 1]), 0.0)
            )
        refs["msg"][1, g] = jnp.zeros((M, LANES), f32)

        def body(b):
            held = refs["msg"][1, g]
            left, right = big[0, g, 0], big[0, g, 1]
            for k in range(RB):
                r = b * RB + k
                v = z[r + 1] + jnp.where(first, from_left(left, r), jnp.where(last, from_right(right, r), 0.0)) + bias[0]
                sig = sigmoid(v)
                a = v * sig
                slope[r] = sig + a * (1.0 - sig)
                act[r] = a
                held = pack(held, a, r)
            refs["msg"][1, g] = held

        rows_loop(body)
        send(1, g, act[0], act[H - 1], act[0], act[H - 1])

    def spread(e, g, dst):
        act, big, corner = refs["act"][g], refs["big"], refs["corner"]
        receive(e, g)

        def store(row, v, left, right):
            before = jnp.where(first, left, pltpu.roll(v, 1, 1))
            behind = jnp.where(last, right, pltpu.roll(v, LANES - 1, 1))
            for at, part in enumerate((before, v, behind)):
                hi, lo = halves(part)
                dst[row, at * M : (at + 1) * M] = hi
                dst[row, n3 + at * M : n3 + (at + 1) * M] = lo

        def body(b):
            left, right = big[e, g, 0], big[e, g, 1]
            for k in range(RB):
                r = b * RB + k
                store(r + 1, act[r], from_left(left, r), from_right(right, r))

        rows_loop(body)
        store(0, big[e, g, 2], corner_left(corner[e, g, 0]), corner_right(corner[e, g, 1]))
        store(H + 1, big[e, g, 3], corner_left(corner[e, g, 2]), corner_right(corner[e, g, 3]))

    def conv_mid(g, src, weight, emit, begin, end):
        carry = refs["carry"][g]

        def pair(m):
            rhs = cat([src[2 * m], src[2 * m + 1]], 1)
            y = dot(weight[...], cat([rhs, rhs[:n3]], 0))
            return y[:, :LANES], y[:, LANES:]

        ya, yb = pair(0)
        carry[0, :M] = ya[:M] + yb[M : 2 * M]
        carry[1, :M] = yb[:M]

        def body(b):
            state = begin(b)
            c0, c1 = carry[0, :M], carry[1, :M]
            for k in range(RB // 2):
                ya, yb = pair(1 + b * (RB // 2) + k)
                r = b * RB + 2 * k
                state = emit(r, c0 + ya[2 * M :], state)
                state = emit(r + 1, c1 + ya[M : 2 * M] + yb[2 * M :], state)
                c0, c1 = ya[:M] + yb[M : 2 * M], yb[:M]
            carry[0, :M] = c0
            carry[1, :M] = c1
            end(b, state)

        rows_loop(body)

    def second(g):
        act, slope = refs["act"][g], refs["slope2"][g]
        refs["msg"][2, g] = jnp.zeros((M, LANES), f32)

        def emit(r, v, held):
            v = v + bias[1]
            sig = sigmoid(v)
            a = v * sig
            slope[r] = sig + a * (1.0 - sig)
            act[r] = a
            return pack(held, a, r)

        def end(b, held):
            refs["msg"][2, g] = held

        conv_mid(g, refs["p1"][g], w2, emit, lambda b: refs["msg"][2, g], end)
        send(2, g, act[0], act[H - 1], act[0], act[H - 1])

    def third(g):
        a3, slope = refs["a3"][g], refs["slope3"][g]

        def emit(r, v, state):
            v = v + bias[2]
            sig = sigmoid(v)
            a = v * sig
            slope[r] = sig + a * (1.0 - sig)
            hi, lo = halves(a)
            a3[r, :M] = hi
            a3[r, M:] = lo
            return state

        conv_mid(g, refs["p2"][g], w3, emit, lambda b: 0, lambda b, s: None)
        pltpu.make_async_copy(a3, a3_hbm.at[g], refs["out_sem"].at[0, g]).start()

    def emit_grad(e, g, own, total, slope):
        act = refs["act"][g]

        def emit(r, v, state):
            held, summed = state
            d = v * slope[r]
            act[r] = d
            if own is not None:
                hi, lo = halves(d)
                own[r + 1, :M] = hi
                own[r + 1, M:] = lo
            return pack(held, d, r), summed + d

        def begin(b):
            return refs["msg"][e, g], total[...]

        def end(b, state):
            refs["msg"][e, g] = state[0]
            total[...] = state[1]

        refs["msg"][e, g] = jnp.zeros((M, LANES), f32)
        return emit, begin, end

    def out_layer(g):
        a3, act = refs["a3"][g], refs["act"][g]
        emit, begin, end = emit_grad(3, g, refs["d3"][g], refs["total"].at[2], refs["slope3"][g])
        ones = jnp.ones((16, 2 * LANES), bf16)
        start_row, start_col = me_r * H, me_c * W
        across = lax.broadcasted_iota(jnp.int32, (W, 1), 0) + start_col
        inside = [(across < widths[g * sz.per_group + s]).astype(f32) * GAIN for s in range(sz.per_group)]

        def body(b):
            for k in range(NB):
                @pl.when(b == k)
                def _():
                    in_copy(dy_hbm, 1, g, k).wait()

            state = begin(b)
            upper, lower = refs["acc_o1"][...], refs["acc_o2"][...]
            for m in range(RB // 2):
                r = b * RB + 2 * m
                parts = []
                for i in range(2):
                    for s in range(sz.per_group):
                        n = g * sz.per_group + s
                        valid = jnp.where(start_row + r + i < heights[n], 1.0, 0.0)
                        parts.append(buf[n, r + i] * (inside[s] * valid))
                hi, lo = halves(cat(parts, 0))
                y1 = dot(ko[...], hi, NT)
                y2 = dot(ko[:M], lo, NT)
                y = y1[:M] + y1[M:] + y2
                state = emit(r, y[:, :LANES], state)
                state = emit(r + 1, y[:, LANES:], state)
                act3 = cat([a3[r], a3[r + 1]], 1)
                upper = upper + dot(cat([act3, ones], 0), hi)
                lower = lower + dot(cat([act3[:M], ones], 0), lo)
            refs["acc_o1"][...] = upper
            refs["acc_o2"][...] = lower
            end(b, state)

        rows_loop(body)
        send(3, g, act[0], act[H - 1], act[0], act[H - 1])

    def back_layer(e, g, weight, own, total, slope):
        act = refs["act"][g]
        emit, begin, end = emit_grad(e, g, own, total, slope)
        conv_mid(g, refs["q"][g], weight, emit, begin, end)
        send(e, g, act[0], act[H - 1], act[0], act[H - 1])

    def mid_kernel_grad(g, src, own, acc):
        def terms(rows, own_rows):
            left = cat(rows, 1)
            right = [cat(two, 1) for two in own_rows]
            hi = cat([two[:M] for two in right], 0)
            lo = cat([two[M:] for two in right], 0)
            return cat([left[:n3], left[:n3], left[n3:]], 1), cat([hi, lo, hi], 1)

        def body(b):
            ls, rs = [], []
            for m in range(RB // 2):
                r = b * RB + 2 * m
                l, rr = terms(
                    [src[r + 1], src[r + 2]], [[own[r + 2 - p], own[r + 3 - p]] for p in range(3)]
                )
                ls.append(l)
                rs.append(rr)
            acc[...] += dot(cat(ls, 1), cat(rs, 1), NT)

        rows_loop(body)
        none = jnp.zeros((2 * M, LANES), bf16)
        l, rr = terms([src[0], src[H + 1]], [[own[1], none], [none, none], [none, own[H]]])
        acc[...] += dot(l, rr, NT)

    def first_kernel_grad(g):
        a0, q, acc = refs["a0"][g], refs["q"][g], refs["acc1"]

        def body(b):
            ls, rs = [], []
            for m in range(RB // 2):
                r = b * RB + 2 * m
                three = [cat([q[r + s], q[r + 1 + s]], 1) for s in range(3)]
                hi = cat([t[:n3] for t in three], 0)
                lo = cat([t[n3:] for t in three], 0)
                ls.append(cat([hi, hi, lo], 1))
                two = cat([a0[r], a0[r + 1]], 0)
                rs.append(cat([two[:, : sz.wide], two[:, sz.wide :], two[:, : sz.wide]], 0))
            acc[...] += dot(cat(ls, 1), cat(rs, 0))

        rows_loop(body)

    for name in ("acc1", "acc2", "acc3", "acc_o1", "acc_o2", "total"):
        refs[name][...] = jnp.zeros_like(refs[name])
    none = jnp.zeros((2 * M, LANES), bf16)
    for g in range(G):
        for name in ("d2", "d3"):
            refs[name][g][0] = none
            refs[name][g][H + 1] = none

    every = range(G)
    for g in every:
        conv_first(g)
    for g in every:
        after_first(g)
    for g in every:
        spread(1, g, refs["p1"][g])
        second(g)
    for g in every:
        spread(2, g, refs["p2"][g])
        third(g)
        out_layer(g)
    for g in every:
        spread(3, g, refs["q"][g])
        back_layer(4, g, t3, refs["d2"][g], refs["total"].at[1], refs["slope2"][g])
    for g in every:
        spread(4, g, refs["q"][g])
        back_layer(5, g, t2, None, refs["total"].at[0], refs["slope1"][g])
    for g in every:
        spread(5, g, refs["q"][g])
        pltpu.make_async_copy(refs["q"][g], q_hbm.at[g], refs["out_sem"].at[1, g]).start()
        first_kernel_grad(g)
    for g in every:
        mid_kernel_grad(g, refs["p2"][g], refs["d3"][g], refs["acc3"])
        mid_kernel_grad(g, refs["p1"][g], refs["d2"][g], refs["acc2"])

    ar = refs["ar"]

    def place(at, block):
        rows = block.shape[0] // 8
        ar[at : at + rows] = block.reshape(rows, 8, LANES)
        return at + rows

    at = 0
    for h in range(sz.wide // LANES):
        at = place(at, refs["acc1"][:, h * LANES : (h + 1) * LANES])
    g3, g2 = refs["acc3"][...], refs["acc2"][...]
    at = place(at, g3[:, :LANES])
    at = place(at, g2[:, :LANES])
    at = place(at, cat([g3[:, LANES:], g2[:, LANES:]], 1))
    upper, lower = refs["acc_o1"][...], refs["acc_o2"][...]
    outs = cat([upper[:M] + upper[M : 2 * M] + lower[:M], upper[2 * M :] + lower[M:]], 0)
    for h in range(sz.wide // LANES):
        at = place(at, outs[:, h * LANES : (h + 1) * LANES])
    lane = lax.broadcasted_iota(jnp.int32, (1, LANES), 1)
    sums = [jnp.sum(refs["total"][i], axis=1, keepdims=True) for i in range(3)]
    at = place(at, jnp.where(lane == 0, sums[0], jnp.where(lane == 1, sums[1], sums[2])))
    if at < sz.units:
        ar[at:] = jnp.zeros((sz.units - at, 8, LANES), f32)

    half = sz.units // 2
    quarter = half // sz.near

    def ship(src, dst, at, dev):
        return pltpu.make_async_remote_copy(
            src_ref=src,
            dst_ref=dst,
            send_sem=refs["ar_send"].at[at],
            recv_sem=refs["ar_recv"].at[at],
            device_id=dev,
            device_id_type=MESH,
        )

    at = 0
    mine = core * half
    copy = ship(ar.at[pl.ds((1 - core) * half, half)], refs["ar_pair"], at, pair_id)
    copy.start()
    copy.wait()
    ar[pl.ds(mine, half)] += refs["ar_pair"][...]
    copies = []
    at += 1
    for d, dev in enumerate(near_ids, 1):
        to = lax.rem(near_at + d, sz.near)
        copies.append(ship(ar.at[pl.ds(mine + to * quarter, quarter)], refs["ar_near"].at[sz.near - 1 - d], at, dev))
        at += 1
    for copy in copies:
        copy.start()
    for copy in copies:
        copy.wait()
    mine = mine + near_at * quarter
    got = ar[pl.ds(mine, quarter)]
    for d in range(sz.near - 1):
        got = got + refs["ar_near"][d]
    ar[pl.ds(mine, quarter)] = got
    copies = []
    for d, dev in enumerate(far_ids, 1):
        to = lax.rem(far + d, sz.far)
        copies.append(ship(ar.at[pl.ds(mine + to * sz.shard, sz.shard)], refs["ar_far"].at[sz.far - 1 - d], at, dev))
        at += 1
    for copy in copies:
        copy.start()
    for copy in copies:
        copy.wait()
    mine = mine + far * sz.shard
    got = ar[pl.ds(mine, sz.shard)]
    for d in range(sz.far - 1):
        got = got + refs["ar_far"][d]
    whole = refs["ar_all"]
    whole[pl.ds(mine, sz.shard)] = got
    for ids, size in ((far_ids, sz.shard), (near_ids, quarter), ([pair_id], half)):
        start = mine // size * size
        copies = []
        for dev in ids:
            copies.append(ship(whole.at[pl.ds(start, size)], whole.at[pl.ds(start, size)], at, dev))
            at += 1
        for copy in copies:
            copy.start()
        for copy in copies:
            copy.wait()
    sums_out[...] = whole[...]

    for g in every:
        pltpu.make_async_copy(refs["a3"][g], a3_hbm.at[g], refs["out_sem"].at[0, g]).wait()
        pltpu.make_async_copy(refs["q"][g], q_hbm.at[g], refs["out_sem"].at[1, g]).wait()
        for slot in range(8):
            dr, dc = GOES[slot]

            @pl.when(exists(dr, dc))
            def _():
                for e in range(EXCHANGES):
                    message(e, g, slot).wait_send()


def call_a(sz, x, dy, heights, widths, w1, w2, w3, t3, t2, ko, bias):
    G, H, W, M, N = sz.groups, sz.height, sz.width, sz.mid, LANES
    n3 = 3 * M
    names, shapes = [], []

    def add(name, *what):
        names.append((name, len(what)))
        shapes.extend(what)

    def per_group(name, shape, dtype):
        add(name, *[pltpu.VMEM(shape, dtype) for _ in range(G)])

    add("buf", pltpu.VMEM((sz.images, H, W, sz.wide), f32))
    per_group("a0", (H, N, 2 * sz.wide), bf16)
    per_group("act", (H, M, N), f32)
    per_group("carry", (2, n3, N), f32)
    for name in ("slope1", "slope2"):
        per_group(name, (H, M, N), f32)
    per_group("slope3", (H + 2, M, N), f32)
    for name in ("p1", "p2", "q"):
        per_group(name, (H + 2, 2 * n3, N), bf16)
    for name in ("d3", "d2"):
        per_group(name, (H + 2, 2 * M, N), bf16)
    per_group("a3", (H, 2 * M, N), bf16)
    E = EXCHANGES
    add("rim", pltpu.VMEM((2, M, N), f32))
    add("msg", pltpu.VMEM((E, G, M, N), f32))
    add("rowmsg", pltpu.VMEM((E, G, 2, M, N), f32))
    add("cormsg", pltpu.VMEM((E, G, 2, 8, N), f32))
    add("big", pltpu.VMEM((E, G, 4, M, N), f32))
    add("corner", pltpu.VMEM((E, G, 4, 8, N), f32))
    add("acc1", pltpu.VMEM((9 * M, sz.wide), f32))
    add("acc2", pltpu.VMEM((n3, n3), f32))
    add("acc3", pltpu.VMEM((n3, n3), f32))
    add("acc_o1", pltpu.VMEM((2 * M + 16, sz.wide), f32))
    add("acc_o2", pltpu.VMEM((M + 16, sz.wide), f32))
    add("total", pltpu.VMEM((3, M, N), f32))
    U = sz.units
    add("ar", pltpu.VMEM((U, 8, N), f32))
    add("ar_all", pltpu.VMEM((U, 8, N), f32))
    add("ar_pair", pltpu.VMEM((U // 2, 8, N), f32))
    add("ar_near", pltpu.VMEM((max(sz.near - 1, 1), U // 2 // sz.near, 8, N), f32))
    add("ar_far", pltpu.VMEM((max(sz.far - 1, 1), sz.shard, 8, N), f32))
    add("in_sem", pltpu.SemaphoreType.DMA((2, G, sz.blocks)))
    add("out_sem", pltpu.SemaphoreType.DMA((2, G)))
    add("send", pltpu.SemaphoreType.DMA((E, G, 8)))
    add("recv", pltpu.SemaphoreType.DMA((E, G, 8)))
    ships = 2 * (1 + (sz.near - 1) + (sz.far - 1))
    add("ar_send", pltpu.SemaphoreType.DMA((ships,)))
    add("ar_recv", pltpu.SemaphoreType.DMA((ships,)))
    grouped = ("a0", "act", "carry", "slope1", "slope2", "slope3", "p1", "p2", "q", "d3", "d2", "a3")

    def run(*args):
        refs = {"io": args[:14]}
        at = 14
        for name, size in names:
            held = args[at : at + size]
            refs[name] = held if name in grouped else held[0]
            at += size
        kernel_a(sz, refs)

    hbm = pl.BlockSpec(memory_space=pl.ANY)
    vmem = pl.BlockSpec(memory_space=pltpu.VMEM)
    smem = pl.BlockSpec(memory_space=pltpu.SMEM)
    return pl.pallas_call(
        run,
        out_shape=(
            jax.ShapeDtypeStruct((G, H + 2, 2 * n3, N), bf16),
            jax.ShapeDtypeStruct((G, H, 2 * M, N), bf16),
            jax.ShapeDtypeStruct((U, 8, N), f32),
        ),
        in_specs=[hbm, hbm, smem, smem] + [vmem] * 7,
        out_specs=(hbm, hbm, vmem),
        scratch_shapes=shapes,
        compiler_params=pltpu.CompilerParams(
            collective_id=0, has_side_effects=True, vmem_limit_bytes=63 * 2**20
        ),
        name="block_chain",
    )(x, dy, heights, widths, w1, w2, w3, t3, t2, ko, bias)


def kernel_b(sz, rows, x, dy, q, a3, wb, wo, bo, heights, widths, sums, out, grad, k1, k2, k3, kout, b1, b2, b3, bout):
    G, H, W, M = sz.groups, sz.height, sz.width, sz.mid
    n3 = 3 * M
    step = pl.program_id(0)
    start_row = lax.axis_index("rows") * H + step * rows
    across = lax.broadcasted_iota(jnp.int32, (W, 1), 0) + lax.axis_index("cols") * W
    inside = [(across < widths[n]).astype(f32) for n in range(sz.images)]
    for i in range(rows):
        three = [cat([q[g, i + s] for g in range(G)], 1) for s in range(3)]
        y = dot(wb[...], cat(three + [t[:n3] for t in three], 0))
        act = cat([a3[g, i] for g in range(G)], 1)
        branch = dot(wo[...], cat([act, act[:M]], 0))
        y, branch = y.T, branch.T
        for n in range(sz.images):
            at = slice(n * W, (n + 1) * W)
            v = x[n, i]
            out[n, i] = v + (branch[at] + bo[...])
            sig = sigmoid(v)
            slope = sig * (1.0 + v * (1.0 - sig))
            valid = jnp.where(start_row + i < heights[n], 1.0, 0.0)
            grad[n, i] = dy[n, i] * (inside[n] * valid) + y[at] * slope

    @pl.when(step == 0)
    def _():
        def take(at, count):
            return sums[at : at + count].reshape(count * 8, LANES)

        at = 0
        parts = []
        for h in range(sz.wide // LANES):
            parts.append(take(at, 9 * M // 8))
            at += 9 * M // 8
        for s in range(3):
            for b in range(3):
                lo = (s * 3 + b) * M
                for h, part in enumerate(parts):
                    k1[2 - s, 2 - b, h * LANES : (h + 1) * LANES] = part[lo : lo + M].T
        g3 = take(at, n3 // 8)
        g2 = take(at + n3 // 8, n3 // 8)
        mix = take(at + 2 * (n3 // 8), n3 // 8)
        at += 3 * (n3 // 8)
        for big, ref, lo in ((g3, k3, 0), (g2, k2, M)):
            for b in range(3):
                sl = slice(b * M, (b + 1) * M)
                ref[0, b] = big[sl, :M]
                ref[1, b] = big[sl, M:]
                ref[2, b] = mix[sl, lo : lo + M]
        for h in range(sz.wide // LANES):
            part = take(at, (M + 16) // 8)
            at += (M + 16) // 8
            kout[:, h * LANES : (h + 1) * LANES] = part[:M]
            bout[:, h * LANES : (h + 1) * LANES] = part[M : M + 1]
        tail = take(at, M // 8).T
        b1[...] = tail[0:1]
        b2[...] = tail[1:2]
        b3[...] = tail[2:3]


def call_b(sz, x, dy, q, a3, wb, wo, bo, heights, widths, sums):
    G, H, W, M = sz.groups, sz.height, sz.width, sz.mid
    rows = 2
    n3 = 3 * M
    big = pl.BlockSpec((sz.images, rows, W, sz.wide), lambda i: (0, i, 0, 0))
    smem = pl.BlockSpec(memory_space=pltpu.SMEM)

    def whole(*shape):
        return pl.BlockSpec(shape, lambda i: (0,) * len(shape))

    shapes = ((3, 3, sz.wide, M), (3, 3, M, M), (3, 3, M, M), (M, sz.wide), (1, M), (1, M), (1, M), (1, sz.wide))
    return pl.pallas_call(
        functools.partial(kernel_b, sz, rows),
        grid=(H // rows,),
        out_shape=tuple(
            jax.ShapeDtypeStruct(s, f32) for s in (x.shape, x.shape) + shapes
        ),
        in_specs=[
            big,
            big,
            pl.BlockSpec(
                (pl.Element(G), pl.Element(rows + 2), pl.Element(2 * n3), pl.Element(LANES)),
                lambda i: (0, i * rows, 0, 0),
            ),
            pl.BlockSpec((G, rows, 2 * M, LANES), lambda i: (0, i, 0, 0)),
            whole(*wb.shape),
            whole(*wo.shape),
            whole(*bo.shape),
            smem,
            smem,
            whole(*sums.shape),
        ],
        out_specs=(big, big) + tuple(whole(*s) for s in shapes),
        compiler_params=pltpu.CompilerParams(vmem_limit_bytes=48 * 2**20),
        name="wide_outputs",
    )(x, dy, q, a3, wb, wo, bo, heights, widths, sums)


def split(w):
    hi = lax.reduce_precision(w, 8, 7)
    return hi.astype(bf16), (w - hi).astype(bf16)


def three_passes(w):
    hi, lo = split(w)
    return cat([hi, hi, lo], 1)


def body(rows, cols, x, k1, b1, k2, b2, k3, b3, ko, bo, dy, heights, widths):
    wide, mid = k1.shape[2:]
    sz = Sizes(x.shape, mid, rows, cols)
    n3 = 3 * mid
    w1 = three_passes(k1.transpose(0, 1, 3, 2).reshape(9 * mid, wide))
    w2, w3 = [three_passes(k.transpose(0, 3, 1, 2).reshape(n3, n3)) for k in (k2, k3)]
    t2, t3 = [three_passes(k[::-1, ::-1].transpose(0, 2, 1, 3).reshape(n3, n3)) for k in (k2, k3)]
    hi, lo = split(k1[::-1, ::-1].transpose(2, 0, 1, 3).reshape(wide, 3, n3))
    wb = cat([cat([hi, hi], 2).reshape(wide, 6 * n3), lo.reshape(wide, 3 * n3)], 1)
    wo = three_passes(ko.T * GAIN)
    ko_both = cat(split(ko), 0)
    bias = jnp.broadcast_to(jnp.stack([b1, b2, b3])[:, :, None], (3, mid, LANES))
    q, a3, sums = call_a(sz, x, dy, heights, widths, w1, w2, w3, t3, t2, ko_both, bias)
    outs = call_b(sz, x, dy, q, a3, wb, wo, (bo * GAIN)[None], heights, widths, sums)
    out, grad, g1, g2, g3, go, s1, s2, s3, so = outs
    return (
        out,
        grad,
        g1,
        s1.reshape(mid),
        g2,
        s2.reshape(mid),
        g3,
        s3.reshape(mid),
        go,
        so.reshape(wide),
    )


def solution(mesh):
    tiled = P(None, "rows", "cols", None)
    return jax.shard_map(
        functools.partial(body, mesh.shape["rows"], mesh.shape["cols"]),
        mesh=mesh,
        in_specs=(tiled,) + (P(),) * 8 + (tiled, P(), P()),
        out_specs=(tiled, tiled) + (P(),) * 8,
        check_vma=False,
    )
```

```python
import functools

import jax
import jax.numpy as jnp
from jax import lax
from jax.experimental import pallas as pl
from jax.experimental.pallas import tpu as pltpu
from jax.sharding import PartitionSpec as P

MESH = pl.DeviceIdType.MESH
bf16 = jnp.bfloat16
f32 = jnp.float32
LANES = 128
NN = (((1,), (0,)), ((), ()))
NT = (((1,), (1,)), ((), ()))
GAIN = 1.0 / 64.0
EXCHANGES = 6
GOES = ((0, 1), (0, -1), (1, 0), (-1, 0), (1, 1), (1, -1), (-1, 1), (-1, -1))


def dot(a, b, dims=NN):
    return lax.dot_general(a, b, dims, preferred_element_type=f32)


def halves(v):
    hi = v.astype(bf16)
    return hi, (v - hi.astype(f32)).astype(bf16)


def sigmoid(v):
    return 0.5 + 0.5 * jnp.tanh(0.5 * v)


def cat(parts, axis):
    return jnp.concatenate(parts, axis=axis)


def lane_column(width):
    return lax.broadcasted_iota(jnp.int32, (1, LANES), 1) % width


class Sizes:
    def __init__(self, shape, mid, rows, cols):
        self.images, self.height, self.width, self.wide = shape
        self.mid = mid
        self.rows, self.cols = rows, cols
        self.per_group = LANES // self.width
        self.groups = self.images // self.per_group
        self.block = 8
        self.blocks = self.height // self.block
        self.devices = rows * cols
        self.low = min(rows, max(16 // (cols // 2), 1))
        self.near = (cols // 2) * self.low
        self.far = rows // self.low
        half = 3 * mid // 8
        self.counts = dict(
            taps=9 * mid // 8 * (self.wide // LANES) + mid // 8,
            outs=(mid + 16) // 8 * (self.wide // LANES) + half + half // 2,
            second=half + half // 2,
        )
        self.parts, at = {}, 0
        for name, used in self.counts.items():
            shard = -(-used // self.devices)
            self.parts[name] = (at, shard * self.devices, shard)
            at += shard * self.devices
        self.units = at


def kernel_a(sz, refs):
    (x_hbm, dy_hbm, heights, widths, k1, k2, k3, ko_in, b1, b2, b3, q_hbm, a3_hbm, sums_out) = refs["io"]
    w1, w2, w3, t3, t2, ko, bias = [refs[n] for n in ("w1", "w2", "w3", "t3", "t2", "ko", "bias")]
    G, H, W, M = sz.groups, sz.height, sz.width, sz.mid
    RB, NB = sz.block, sz.blocks
    me_r, me_c = lax.axis_index("rows"), lax.axis_index("cols")
    col = lane_column(W)
    first, last = col == 0, col == W - 1
    ends = first | last
    even = col % 2 == 0
    n3 = 3 * M

    def exists(dr, dc):
        ok = None
        for here, step, count in ((me_r, dr, sz.rows), (me_c, dc, sz.cols)):
            if step:
                near = (here + step >= 0) & (here + step < count)
                ok = near if ok is None else ok & near
        return ok

    buf = refs["buf"]

    def in_copy(src, which, g, k):
        n0 = g * sz.per_group
        return pltpu.make_async_copy(
            src.at[pl.ds(n0, sz.per_group), pl.ds(k * RB, RB)],
            buf.at[pl.ds(n0, sz.per_group), pl.ds(k * RB, RB)],
            refs["in_sem"].at[which, g, k],
        )

    for g in range(G):
        for k in range(NB):
            in_copy(x_hbm, 0, g, k).start()

    k1_copy = pltpu.make_async_copy(k1, refs["acc1"], refs["k1_sem"])
    k1_copy.start()

    def prepare():
        k1_copy.wait()
        hi, lo = halves(refs["acc1"][...])
        w1[...] = cat([hi, hi, lo], 1)
        for k, fwd, back in ((k2, w2, t2), (k3, w3, t3)):
            for p in range(3):
                at = slice(p * M, (p + 1) * M)
                hi, lo = halves(cat([k[p, q].T for q in range(3)], 1))
                fwd[at] = cat([hi, hi, lo], 1)
                hi, lo = halves(cat([k[2 - p, 2 - q] for q in range(3)], 1))
                back[at] = cat([hi, hi, lo], 1)
        ko[:M], ko[M:] = halves(ko_in[...])
        for i, b in enumerate((b1, b2, b3)):
            bias[i] = jnp.broadcast_to(b[...], (LANES, M)).T

    core, rest, low, far = me_c % 2, me_c // 2, me_r % sz.low, me_r // sz.low
    near_at = rest * sz.low + low

    def near_id(k):
        return (far * sz.low + k % sz.low, (k // sz.low) * 2 + core)

    def far_id(k):
        return (k * sz.low + low, me_c)

    pair_id = (me_r, me_c + 1 - 2 * core)
    near_ids = [near_id(lax.rem(near_at + d, sz.near)) for d in range(1, sz.near)]
    far_ids = [far_id(lax.rem(far + d, sz.far)) for d in range(1, sz.far)]

    refs["big"][...] = jnp.zeros_like(refs["big"])
    refs["corner"][...] = jnp.zeros_like(refs["corner"])

    barrier = pltpu.get_barrier_semaphore()
    count = 1 + len(near_ids) + len(far_ids)
    for dev in [pair_id] + near_ids + far_ids:
        pl.semaphore_signal(barrier, inc=1, device_id=dev, device_id_type=MESH)
    for dr, dc in GOES:
        ok = exists(dr, dc)
        count = count + jnp.where(ok, 1, 0)

        @pl.when(ok)
        def _():
            pl.semaphore_signal(barrier, inc=1, device_id=(me_r + dr, me_c + dc), device_id_type=MESH)

    pl.semaphore_wait(barrier, count)

    def message(e, g, slot):
        dr, dc = GOES[slot]
        if slot < 2:
            src, dst = refs["msg"].at[e % 2, g], refs["big"].at[e % 2, g, slot]
        elif slot < 4:
            src, dst = refs["rowmsg"].at[e % 2, g, 3 - slot], refs["big"].at[e % 2, g, slot]
        else:
            src, dst = refs["cormsg"].at[e % 2, g, 1 if dr > 0 else 0], refs["corner"].at[e % 2, g, slot - 4]
        return pltpu.make_async_remote_copy(
            src_ref=src,
            dst_ref=dst,
            send_sem=refs["send"].at[e, g, slot],
            recv_sem=refs["recv"].at[e, g, slot],
            device_id=(me_r + dr, me_c + dc),
            device_id_type=MESH,
        )

    def send(e, g, top, bottom, top_rim, bottom_rim):
        refs["rowmsg"][e % 2, g, 0] = top
        refs["rowmsg"][e % 2, g, 1] = bottom
        refs["cormsg"][e % 2, g, 0] = pack_corner(top_rim)
        refs["cormsg"][e % 2, g, 1] = pack_corner(bottom_rim)
        for slot in range(8):
            dr, dc = GOES[slot]

            @pl.when(exists(dr, dc))
            def _():
                message(e, g, slot).start()

    def reuse(e, g):
        if e >= 2:
            for slot in range(8):
                dr, dc = GOES[slot]

                @pl.when(exists(dr, dc))
                def _():
                    message(e - 2, g, slot).wait_send()

    def receive(e, g):
        for slot in range(8):
            dr, dc = GOES[slot]

            @pl.when(exists(-dr, -dc))
            def _():
                message(e, g, slot).wait_recv()

    def pack(held, value, u):
        moved = pltpu.roll(value, lax.rem(LANES + 1 + 2 * u, LANES), 1)
        return jnp.where(col // 2 == u, moved, held)

    def pack_corner(value):
        held = jnp.zeros((8, LANES), f32)
        for k in range(M // 8):
            held = jnp.where(col // 2 == k, pltpu.roll(value[8 * k : 8 * k + 8], 1 + 2 * k, 1), held)
        return held

    def meet(e, g):
        left, right = refs["big"][e % 2, g, 0], refs["big"][e % 2, g, 1]
        refs["met"][g] = jnp.where(even, left, pltpu.roll(right, (2 * W - 2) % LANES, 1))

    def from_sides(held, u):
        return pltpu.roll(held, LANES - W - 2 * u, 1)

    def corner_left(held):
        return cat([pltpu.roll(held, LANES - W - 2 * k, 1) for k in range(M // 8)], 0)

    def corner_right(held):
        return cat([pltpu.roll(held, W - 2 - 2 * k, 1) for k in range(M // 8)], 0)

    def nothing():
        pass

    def run(*phases, lo=0, hi=NB):
        lo, hi = min(lo, NB), min(hi, NB)
        if lo == hi:
            return
        if lo == 0:
            for before, _, _ in phases:
                before()

        def step(b, carry):
            for _, body, _ in phases:
                body(b)
            return carry

        lax.fori_loop(lo, hi, step, 0)
        if hi == NB:
            for _, _, after in phases:
                after()

    def conv_first(g):
        a0, z, carry = refs["a0"][g], refs["slope3"][g], refs["carry"][g]

        def before():
            carry[...] = jnp.zeros_like(carry)
            refs["msg"][0, g] = jnp.zeros((M, LANES), f32)

        def emit(row, s, held):
            s0, s1, s2 = s[:M], s[M : 2 * M], s[2 * M :]
            value = s1 + jnp.where(first, 0.0, pltpu.roll(s0, 1, 1))
            value = value + jnp.where(last, 0.0, pltpu.roll(s2, LANES - 1, 1))
            z[row + 1] = value
            rim = jnp.where(first, s2, s0)
            return rim, pack(held, rim, row)

        def body(b):
            in_copy(x_hbm, 0, g, b).wait()
            held = refs["msg"][0, g]
            c0, c1 = carry[0], carry[1]
            for m in range(RB // 2):
                r = b * RB + 2 * m
                pair = []
                for i in range(2):
                    v = cat([buf[g * sz.per_group + s, r + i] for s in range(sz.per_group)], 0)
                    hi, lo = halves(v * sigmoid(v))
                    both = cat([hi, lo], 1)
                    a0[r + i] = both
                    pair.append(both)
                rhs = cat(pair, 0)
                y = dot(w1[...], cat([rhs, rhs[:, : sz.wide]], 1), NT)
                ya, yb = y[:, :LANES], y[:, LANES:]
                rim, held = emit(r - 1, c0 + ya[2 * n3 :], held)
                if m == 0:
                    refs["rim"][g, jnp.minimum(b, 1)] = rim
                _, held = emit(r, c1 + ya[n3 : 2 * n3] + yb[2 * n3 :], held)
                c0, c1 = ya[:n3] + yb[n3 : 2 * n3], yb[:n3]
            carry[0] = c0
            carry[1] = c1
            refs["msg"][0, g] = held

        def after():
            _, held = emit(H - 1, carry[0], refs["msg"][0, g])
            rim, _ = emit(H, carry[1], held)
            refs["msg"][0, g] = held
            for k in range(NB):
                in_copy(dy_hbm, 1, g, k).start()
            send(0, g, z[0], z[H + 1], refs["rim"][g, 0], rim)

        return before, body, after

    def after_first(g):
        z, act, slope = refs["slope3"][g], refs["act"][g], refs["slope1"][g]
        big, corner = refs["big"], refs["corner"]

        def before():
            receive(0, g)
            for row, at in ((1, 0), (H, 2)):
                z[row] += (
                    big[0, g, 2 + at // 2]
                    + jnp.where(first, corner_left(corner[0, g, at]), 0.0)
                    + jnp.where(last, corner_right(corner[0, g, at + 1]), 0.0)
                )
            meet(0, g)
            refs["msg"][1, g] = jnp.zeros((M, LANES), f32)

        def body(b):
            held = refs["msg"][1, g]
            both = refs["met"][g]
            for k in range(RB):
                r = b * RB + k
                v = z[r + 1] + jnp.where(ends, from_sides(both, r), 0.0) + bias[0]
                sig = sigmoid(v)
                a = v * sig
                slope[r] = sig + a * (1.0 - sig)
                act[r] = a
                held = pack(held, a, r)
            refs["msg"][1, g] = held

        return before, body, lambda: send(1, g, act[0], act[H - 1], act[0], act[H - 1])

    def spread(e, g, dst):
        act, big, corner = refs["act"][g], refs["big"], refs["corner"]

        def before():
            receive(e, g)
            meet(e, g)

        def store(row, v, left, right):
            before = jnp.where(first, left, pltpu.roll(v, 1, 1))
            behind = jnp.where(last, right, pltpu.roll(v, LANES - 1, 1))
            for at, part in enumerate((before, v, behind)):
                hi, lo = halves(part)
                dst[row, at * M : (at + 1) * M] = hi
                dst[row, n3 + at * M : n3 + (at + 1) * M] = lo

        def body(b):
            both = refs["met"][g]
            for k in range(RB):
                r = b * RB + k
                sides = from_sides(both, r)
                store(r + 1, act[r], sides, sides)

        def after():
            store(0, big[e % 2, g, 2], corner_left(corner[e % 2, g, 0]), corner_right(corner[e % 2, g, 1]))
            store(H + 1, big[e % 2, g, 3], corner_left(corner[e % 2, g, 2]), corner_right(corner[e % 2, g, 3]))

        return before, body, after

    def conv_mid(g, src, weight, emit, begin, end):
        carry = refs["carry"][g]

        def pair(m):
            rhs = cat([src[2 * m], src[2 * m + 1]], 1)
            y = dot(weight[...], cat([rhs, rhs[:n3]], 0))
            return y[:, :LANES], y[:, LANES:]

        def before():
            ya, yb = pair(0)
            carry[0, :M] = ya[:M] + yb[M : 2 * M]
            carry[1, :M] = yb[:M]

        def body(b):
            state = begin(b)
            c0, c1 = carry[0, :M], carry[1, :M]
            for k in range(RB // 2):
                ya, yb = pair(1 + b * (RB // 2) + k)
                r = b * RB + 2 * k
                state = emit(r, c0 + ya[2 * M :], state)
                state = emit(r + 1, c1 + ya[M : 2 * M] + yb[2 * M :], state)
                c0, c1 = ya[:M] + yb[M : 2 * M], yb[:M]
            carry[0, :M] = c0
            carry[1, :M] = c1
            end(b, state)

        return before, body

    def second(g):
        act, slope = refs["act"][g], refs["slope2"][g]

        def clear():
            reuse(2, g)
            refs["msg"][0, g] = jnp.zeros((M, LANES), f32)

        def emit(r, v, held):
            v = v + bias[1]
            sig = sigmoid(v)
            a = v * sig
            slope[r] = sig + a * (1.0 - sig)
            act[r] = a
            return pack(held, a, r)

        def end(b, held):
            refs["msg"][0, g] = held

        before, body = conv_mid(g, refs["p1"][g], w2, emit, lambda b: refs["msg"][0, g], end)
        return (lambda: (clear(), before())), body, lambda: send(2, g, act[0], act[H - 1], act[0], act[H - 1])

    def a3_copy(g, b):
        return pltpu.make_async_copy(
            refs["a3"].at[b % 2], a3_hbm.at[g, pl.ds(b * RB, RB)], refs["out_sem"].at[g, b]
        )

    def third(g):
        a3, slope = refs["a3"], refs["slope3"][g]

        def emit(r, v, state):
            v = v + bias[2]
            sig = sigmoid(v)
            a = v * sig
            slope[r] = sig + a * (1.0 - sig)
            hi, lo = halves(a)
            k = r - state * RB
            a3[state % 2, k, :M] = hi
            a3[state % 2, k, M:] = lo
            return state

        def begin(b):
            if NB > 2:

                @pl.when(b >= 2)
                def _():
                    a3_copy(g, b - 2).wait()

            return b

        before, body = conv_mid(g, refs["p2"][g], w3, emit, begin, lambda b, s: a3_copy(g, b).start())

        def after():
            for k in range(max(NB - 2, 0), NB):
                a3_copy(g, k).wait()

        return before, body, after

    def column_masks(g, scale):
        across = lax.broadcasted_iota(jnp.int32, (W, 1), 0) + me_c * W
        return [(across < widths[g * sz.per_group + s]).astype(f32) * scale for s in range(sz.per_group)]

    def row_valid(n, r):
        return jnp.where(me_r * H + r < heights[n], 1.0, 0.0)

    def emit_grad(e, g, own, total, slope):
        act = refs["act"][g]

        def emit(r, v, state):
            held, summed = state
            d = v * slope[r]
            act[r] = d
            if own is not None:
                hi, lo = halves(d)
                own[r + 1, :M] = hi
                own[r + 1, M:] = lo
            return pack(held, d, r), summed + d

        def begin(b):
            return refs["msg"][e % 2, g], total[...]

        def end(b, state):
            refs["msg"][e % 2, g] = state[0]
            total[...] = state[1]

        def clear():
            reuse(e, g)
            refs["msg"][e % 2, g] = jnp.zeros((M, LANES), f32)

        return emit, begin, end, clear

    def out_layer(g):
        a3, act = refs["a3"], refs["act"][g]
        emit, begin, end, clear = emit_grad(3, g, refs["d3"][g], refs["total"].at[2], refs["slope3"][g])
        ones = jnp.ones((16, 2 * LANES), bf16)
        inside = column_masks(g, GAIN)

        def body(b):
            in_copy(dy_hbm, 1, g, b).wait()
            state = begin(b)
            upper, lower = refs["acc_o1"][...], refs["acc_o2"][...]
            for m in range(RB // 2):
                r = b * RB + 2 * m
                parts = []
                for i in range(2):
                    for s in range(sz.per_group):
                        n = g * sz.per_group + s
                        parts.append(buf[n, r + i] * (inside[s] * row_valid(n, r + i)))
                hi, lo = halves(cat(parts, 0))
                y1 = dot(ko[...], hi, NT)
                y2 = dot(ko[:M], lo, NT)
                y = y1[:M] + y1[M:] + y2
                state = emit(r, y[:, :LANES], state)
                state = emit(r + 1, y[:, LANES:], state)
                act3 = cat([a3[b % 2, 2 * m], a3[b % 2, 2 * m + 1]], 1)
                upper = upper + dot(cat([act3, ones], 0), hi)
                lower = lower + dot(cat([act3[:M], ones], 0), lo)
            refs["acc_o1"][...] = upper
            refs["acc_o2"][...] = lower
            end(b, state)

        return clear, body, lambda: send(3, g, act[0], act[H - 1], act[0], act[H - 1])

    def back_layer(e, g, weight, own, total, slope):
        act = refs["act"][g]
        emit, begin, end, clear = emit_grad(e, g, own, total, slope)
        before, body = conv_mid(g, refs["q"][g], weight, emit, begin, end)
        return (lambda: (clear(), before())), body, lambda: send(e, g, act[0], act[H - 1], act[0], act[H - 1])

    def mid_kernel_grad(g, src, own, acc):
        def terms(rows, own_rows):
            left = cat(rows, 1)
            right = [cat(two, 1) for two in own_rows]
            hi = cat([two[:M] for two in right], 0)
            lo = cat([two[M:] for two in right], 0)
            return cat([left[:n3], left[:n3], left[n3:]], 1), cat([hi, lo, hi], 1)

        def body(b):
            ls, rs = [], []
            for m in range(RB // 2):
                r = b * RB + 2 * m
                l, rr = terms(
                    [src[r + 1], src[r + 2]], [[own[r + 2 - p], own[r + 3 - p]] for p in range(3)]
                )
                ls.append(l)
                rs.append(rr)
            acc[...] += dot(cat(ls, 1), cat(rs, 1), NT)

        def after():
            none = jnp.zeros((2 * M, LANES), bf16)
            l, rr = terms([src[0], src[H + 1]], [[own[1], none], [none, none], [none, own[H]]])
            acc[...] += dot(l, rr, NT)

        return nothing, body, after

    def first_kernel_grad(g):
        a0, q, acc = refs["a0"][g], refs["q"][g], refs["acc1"]

        def body(b):
            ls, rs = [], []
            for m in range(RB // 2):
                r = b * RB + 2 * m
                three = [cat([q[r + s], q[r + 1 + s]], 1) for s in range(3)]
                hi = cat([t[:n3] for t in three], 0)
                lo = cat([t[n3:] for t in three], 0)
                ls.append(cat([hi, hi, lo], 1))
                two = cat([a0[r], a0[r + 1]], 0)
                rs.append(cat([two[:, : sz.wide], two[:, sz.wide :], two[:, : sz.wide]], 0))
            for m in range(0, RB // 2, 2):
                acc[...] += dot(cat(ls[m : m + 2], 1), cat(rs[m : m + 2], 0))

        return nothing, body, nothing

    def reducer(name):
        base, units, shard = sz.parts[name]
        half, quarter = units // 2, units // 2 // sz.near
        ar, whole = refs["ar"], refs["ar_all"]
        sems = list(sz.parts).index(name)
        pair_buf = refs["pair_" + name]
        near_buf = refs["near_" + name]
        far_buf = refs["far_" + name]
        flight, used = [], [0]

        def ship(src, dst, dev):
            copy = pltpu.make_async_remote_copy(
                src_ref=src,
                dst_ref=dst,
                send_sem=refs["ar_send"].at[sems, used[0]],
                recv_sem=refs["ar_recv"].at[sems, used[0]],
                device_id=dev,
                device_id_type=MESH,
            )
            used[0] += 1
            flight.append(copy)
            copy.start()

        def land():
            while flight:
                flight.pop().wait()

        mine_half = base + core * half
        mine_quarter = mine_half + near_at * quarter
        mine = mine_quarter + far * shard

        def fill(blocks):
            at = base
            for block in blocks:
                rows = block.shape[0] // 8
                ar[at : at + rows] = block.reshape(rows, 8, LANES)
                at += rows
            if at < base + units:
                ar[at : base + units] = jnp.zeros((base + units - at, 8, LANES), f32)
            ship(ar.at[pl.ds(base + (1 - core) * half, half)], pair_buf, pair_id)

        def to_near():
            land()
            ar[pl.ds(mine_half, half)] += pair_buf[...]
            for d, dev in enumerate(near_ids, 1):
                to = lax.rem(near_at + d, sz.near)
                ship(ar.at[pl.ds(mine_half + to * quarter, quarter)], near_buf.at[sz.near - 1 - d], dev)

        def to_far():
            land()
            got = ar[pl.ds(mine_quarter, quarter)]
            for d in range(sz.near - 1):
                got = got + near_buf[d]
            ar[pl.ds(mine_quarter, quarter)] = got
            for d, dev in enumerate(far_ids, 1):
                to = lax.rem(far + d, sz.far)
                ship(ar.at[pl.ds(mine_quarter + to * shard, shard)], far_buf.at[sz.far - 1 - d], dev)

        def spread_far():
            land()
            got = ar[pl.ds(mine, shard)]
            for d in range(sz.far - 1):
                got = got + far_buf[d]
            whole[pl.ds(mine, shard)] = got
            for dev in far_ids:
                ship(whole.at[pl.ds(mine, shard)], whole.at[pl.ds(mine, shard)], dev)

        def spread_near():
            land()
            at = pl.ds(mine_quarter, quarter)
            for dev in near_ids:
                ship(whole.at[at], whole.at[at], dev)

        def spread_pair():
            land()
            at = pl.ds(mine_half, half)
            ship(whole.at[at], whole.at[at], pair_id)

        def done():
            land()
            sums = pltpu.make_async_copy(
                whole.at[pl.ds(base, units)], sums_out.at[pl.ds(base, units)], refs["sum_sem"].at[sems]
            )
            sums.start()
            return sums

        def near_only():
            land()
            got = ar[pl.ds(mine, shard)]
            for d in range(sz.near - 1):
                got = got + near_buf[d]
            whole[pl.ds(mine, shard)] = got
            for dev in near_ids:
                ship(whole.at[pl.ds(mine, shard)], whole.at[pl.ds(mine, shard)], dev)

        if sz.far == 1:
            return fill, iter((to_near, near_only, spread_pair, done))
        return fill, iter((to_near, to_far, spread_far, spread_near, spread_pair, done))

    for name in ("acc2", "acc3", "acc_o1", "acc_o2", "total"):
        refs[name][...] = jnp.zeros_like(refs[name])
    none = jnp.zeros((2 * M, LANES), bf16)
    for g in range(G):
        for name in ("d2", "d3"):
            refs[name][g][0] = none
            refs[name][g][H + 1] = none

    every = range(G)
    moving, ended = {}, []

    def q_copy(g):
        return pltpu.make_async_copy(refs["q"][g], q_hbm.at[g], refs["q_sem"].at[g])

    def advance(*names):
        for name in names:
            copy = next(moving[name])()
            if copy is not None:
                ended.append(copy)
                del moving[name]

    def reduce(name, blocks):
        fill, moving[name] = reducer(name)
        fill(blocks)

    def wide_blocks(value):
        return [value[:, h * LANES : (h + 1) * LANES] for h in range(sz.wide // LANES)]

    def mid_blocks(acc):
        value = acc[...]
        rest = value[:, LANES:]
        return [value[:, :LANES], cat([rest[: n3 // 2], rest[n3 // 2 :]], 1)]

    prepare()
    refs["acc1"][...] = jnp.zeros_like(refs["acc1"])
    for g in every:
        run(conv_first(g))
    for g in every:
        run(after_first(g))
    for g in every:
        run(spread(1, g, refs["p1"][g]))
        run(second(g))
    for g in every:
        run(spread(2, g, refs["p2"][g]))
        run(third(g), out_layer(g))
    for g in every:
        run(spread(3, g, refs["q"][g]), mid_kernel_grad(g, refs["p2"][g], refs["d3"][g], refs["acc3"]))
        run(back_layer(4, g, t3, refs["d2"][g], refs["total"].at[1], refs["slope2"][g]))
    upper, lower = refs["acc_o1"][...], refs["acc_o2"][...]
    outs = cat([upper[:M] + upper[M : 2 * M] + lower[:M], upper[2 * M :] + lower[M:]], 0)
    reduce("outs", wide_blocks(outs) + mid_blocks(refs["acc3"]))
    for g in every:
        run(spread(4, g, refs["q"][g]), mid_kernel_grad(g, refs["p1"][g], refs["d2"][g], refs["acc2"]))
        if g == 0:
            advance("outs")
        run(back_layer(5, g, t2, None, refs["total"].at[0], refs["slope1"][g]))
    reduce("second", mid_blocks(refs["acc2"]))
    lane = lax.broadcasted_iota(jnp.int32, (1, LANES), 1)
    sums = [jnp.sum(refs["total"][i], axis=1, keepdims=True) for i in range(3)]
    biases = jnp.where(lane == 0, sums[0], jnp.where(lane == 1, sums[1], sums[2]))
    run(spread(5, 0, refs["q"][0]))
    advance("outs", "second")
    q_copy(0).start()
    for g in every:
        following = [spread(5, g + 1, refs["q"][g + 1])] if g < G - 1 else []
        run(first_kernel_grad(g), *following)
        if following:
            q_copy(g + 1).start()
            advance("outs", "second")
    reduce("taps", wide_blocks(refs["acc1"]) + [biases])
    if G == 1:
        advance("outs", "second")
    advance("taps", "second", "outs")
    while moving:
        advance(*list(moving))

    for copy in ended:
        copy.wait()
    for g in every:
        q_copy(g).wait()
    for g in every:
        for slot in range(8):
            dr, dc = GOES[slot]

            @pl.when(exists(dr, dc))
            def _():
                for e in range(EXCHANGES - 2, EXCHANGES):
                    message(e, g, slot).wait_send()


def call_a(sz, x, dy, heights, widths, k1, k2, k3, ko, b1, b2, b3):
    G, H, W, M, N = sz.groups, sz.height, sz.width, sz.mid, LANES
    n3 = 3 * M
    names, shapes = [], []

    def add(name, *what):
        names.append((name, len(what)))
        shapes.extend(what)

    def per_group(name, shape, dtype):
        add(name, *[pltpu.VMEM(shape, dtype) for _ in range(G)])

    add("buf", pltpu.VMEM((sz.images, H, W, sz.wide), f32))
    per_group("a0", (H, N, 2 * sz.wide), bf16)
    per_group("act", (H, M, N), f32)
    per_group("carry", (2, n3, N), f32)
    for name in ("slope1", "slope2"):
        per_group(name, (H, M, N), f32)
    per_group("slope3", (H + 2, M, N), f32)
    for name in ("p1", "p2", "q"):
        per_group(name, (H + 2, 2 * n3, N), bf16)
    for name in ("d3", "d2"):
        per_group(name, (H + 2, 2 * M, N), bf16)
    add("a3", pltpu.VMEM((2, sz.block, 2 * M, N), bf16))
    add("w1", pltpu.VMEM((9 * M, 3 * sz.wide), bf16))
    for name in ("w2", "w3", "t2", "t3"):
        add(name, pltpu.VMEM((n3, 3 * n3), bf16))
    add("ko", pltpu.VMEM((2 * M, sz.wide), bf16))
    add("met", pltpu.VMEM((G, M, N), f32))
    add("bias", pltpu.VMEM((3, M, N), f32))
    E = EXCHANGES
    add("rim", pltpu.VMEM((G, 2, M, N), f32))
    add("msg", pltpu.VMEM((2, G, M, N), f32))
    add("rowmsg", pltpu.VMEM((2, G, 2, M, N), f32))
    add("cormsg", pltpu.VMEM((2, G, 2, 8, N), f32))
    add("big", pltpu.VMEM((2, G, 4, M, N), f32))
    add("corner", pltpu.VMEM((2, G, 4, 8, N), f32))
    add("acc1", pltpu.VMEM((9 * M, sz.wide), f32))
    add("acc2", pltpu.VMEM((n3, n3), f32))
    add("acc3", pltpu.VMEM((n3, n3), f32))
    add("acc_o1", pltpu.VMEM((2 * M + 16, sz.wide), f32))
    add("acc_o2", pltpu.VMEM((M + 16, sz.wide), f32))
    add("total", pltpu.VMEM((3, M, N), f32))
    U = sz.units
    add("ar", pltpu.VMEM((U, 8, N), f32))
    add("ar_all", pltpu.VMEM((U, 8, N), f32))
    for part, (_, units, shard) in sz.parts.items():
        add("pair_" + part, pltpu.VMEM((units // 2, 8, N), f32))
        add("near_" + part, pltpu.VMEM((max(sz.near - 1, 1), units // 2 // sz.near, 8, N), f32))
        add("far_" + part, pltpu.VMEM((max(sz.far - 1, 1), shard, 8, N), f32))
    add("sum_sem", pltpu.SemaphoreType.DMA((len(sz.parts),)))
    add("in_sem", pltpu.SemaphoreType.DMA((2, G, sz.blocks)))
    add("k1_sem", pltpu.SemaphoreType.DMA)
    add("q_sem", pltpu.SemaphoreType.DMA((G,)))
    add("out_sem", pltpu.SemaphoreType.DMA((G, sz.blocks)))
    add("send", pltpu.SemaphoreType.DMA((E, G, 8)))
    add("recv", pltpu.SemaphoreType.DMA((E, G, 8)))
    ships = 2 * (1 + (sz.near - 1) + (sz.far - 1))
    add("ar_send", pltpu.SemaphoreType.DMA((len(sz.parts), ships)))
    add("ar_recv", pltpu.SemaphoreType.DMA((len(sz.parts), ships)))
    grouped = ("a0", "act", "carry", "slope1", "slope2", "slope3", "p1", "p2", "q", "d3", "d2")

    def whole_kernel(*args):
        refs = {"io": args[:14]}
        at = 14
        for name, size in names:
            held = args[at : at + size]
            refs[name] = held if name in grouped else held[0]
            at += size
        kernel_a(sz, refs)

    hbm = pl.BlockSpec(memory_space=pl.ANY)
    vmem = pl.BlockSpec(memory_space=pltpu.VMEM)
    smem = pl.BlockSpec(memory_space=pltpu.SMEM)
    return pl.pallas_call(
        whole_kernel,
        out_shape=(
            jax.ShapeDtypeStruct((G, H + 2, 2 * n3, N), bf16),
            jax.ShapeDtypeStruct((G, H, 2 * M, N), bf16),
            jax.ShapeDtypeStruct((U, 8, N), f32),
        ),
        in_specs=[hbm, hbm, smem, smem, hbm] + [vmem] * 6,
        out_specs=(hbm, hbm, hbm),
        scratch_shapes=shapes,
        compiler_params=pltpu.CompilerParams(
            collective_id=0, has_side_effects=True, vmem_limit_bytes=63 * 2**20
        ),
        name="block_chain",
    )(x, dy, heights, widths, k1, k2, k3, ko, b1, b2, b3)


def kernel_b(
    sz, rows, x_hbm, dy_hbm, q_hbm, a3_hbm, sums_hbm, k1_hbm, ko_hbm, bo, heights, widths,
    out_hbm, grad_hbm, g1, g2, g3, go, s1, s2, s3, so,
    x, dy, q, a3, sums, k1, ko, wb, wo, in_sem, out_sem,
):
    G, H, W, M = sz.groups, sz.height, sz.width, sz.mid
    n3 = 3 * M
    chunks = H // rows

    def copies_in(c):
        r = c * rows
        first = [(q_hbm.at[:, pl.ds(r + 2, rows)], q.at[:, pl.ds(r + 2, rows)])]
        first.append((a3_hbm.at[:, pl.ds(r, rows)], a3.at[:, pl.ds(r, rows)]))
        first.append((x_hbm.at[:, pl.ds(r, rows)], x.at[:, pl.ds(r, rows)]))
        first.append((dy_hbm.at[:, pl.ds(r, rows)], dy.at[:, pl.ds(r, rows)]))
        return [pltpu.make_async_copy(s, d, in_sem.at[i, c]) for i, (s, d) in enumerate(first)]

    def copies_out(c):
        at = (slice(None), pl.ds(c * rows, rows))
        return [
            pltpu.make_async_copy(x.at[at], out_hbm.at[at], out_sem.at[0, c]),
            pltpu.make_async_copy(dy.at[at], grad_hbm.at[at], out_sem.at[1, c]),
        ]

    early = [
        pltpu.make_async_copy(s, d, in_sem.at[i, chunks])
        for i, (s, d) in enumerate(((k1_hbm, k1), (ko_hbm, ko), (q_hbm.at[:, pl.ds(0, 2)], q.at[:, pl.ds(0, 2)])))
    ]
    tail = pltpu.make_async_copy(sums_hbm, sums, in_sem.at[3, chunks])
    for copy in early:
        copy.start()
    for c in range(chunks):
        for copy in copies_in(c):
            copy.start()
    tail.start()
    for copy in early:
        copy.wait()

    for p in range(3):
        hi, lo = halves(cat([k1[2 - p, 2 - b].T for b in range(3)], 1))
        wb[:, 2 * p * n3 : 2 * (p + 1) * n3] = cat([hi, hi], 1)
        wb[:, (6 + p) * n3 : (7 + p) * n3] = lo
    hi, lo = halves(ko[...].T * GAIN)
    wo[...] = cat([hi, hi, lo], 1)
    add = bo[...] * GAIN

    across = lax.broadcasted_iota(jnp.int32, (W, 1), 0) + lax.axis_index("cols") * W
    inside = [(across < widths[n]).astype(f32) for n in range(sz.images)]
    start_row = lax.axis_index("rows") * H

    def body(c, carry):
        for copy in copies_in(c):
            copy.wait()
        for k in range(rows):
            i = c * rows + k
            three = [cat([q[g, i + s] for g in range(G)], 1) for s in range(3)]
            y = dot(wb[...], cat(three + [t[:n3] for t in three], 0))
            act = cat([a3[g, i] for g in range(G)], 1)
            branch = dot(wo[...], cat([act, act[:M]], 0))
            y, branch = y.T, branch.T
            for n in range(sz.images):
                at = slice(n * W, (n + 1) * W)
                v = x[n, i]
                x[n, i] = v + (branch[at] + add)
                sig = sigmoid(v)
                slope = sig * (1.0 + v * (1.0 - sig))
                valid = jnp.where(start_row + i < heights[n], 1.0, 0.0)
                dy[n, i] = dy[n, i] * (inside[n] * valid) + y[at] * slope
        for copy in copies_out(c):
            copy.start()
        return carry

    lax.fori_loop(0, chunks, body, 0)

    tail.wait()

    def take(at, count):
        return sums[at : at + count].reshape(count * 8, LANES)

    at = sz.parts["taps"][0]
    for h in range(sz.wide // LANES):
        part = take(at, 9 * M // 8)
        at += 9 * M // 8
        for t in range(3):
            for b in range(3):
                lo = (t * 3 + b) * M
                g1[2 - t, 2 - b, :, h * LANES : (h + 1) * LANES] = part[lo : lo + M]
    rest = take(at, M // 8).T
    s1[...] = rest[0:1]
    s2[...] = rest[1:2]
    s3[...] = rest[2:3]
    at = sz.parts["outs"][0]
    for h in range(sz.wide // LANES):
        part = take(at, (M + 16) // 8)
        at += (M + 16) // 8
        go[:, h * LANES : (h + 1) * LANES] = part[:M]
        so[:, h * LANES : (h + 1) * LANES] = part[M : M + 1]
    for at, ref in ((at, g3), (sz.parts["second"][0], g2)):
        big, rest = take(at, n3 // 8), take(at + n3 // 8, n3 // 16)
        rest = cat([rest[:, :M], rest[:, M:]], 0)
        for b in range(3):
            sl = slice(b * M, (b + 1) * M)
            ref[0, b] = big[sl, :M]
            ref[1, b] = big[sl, M:]
            ref[2, b] = rest[sl]

    def finish(c, carry):
        for copy in copies_out(c):
            copy.wait()
        return carry

    lax.fori_loop(0, chunks, finish, 0)


def call_b(sz, x, dy, q, a3, sums, k1, ko, bo, heights, widths):
    G, H, W, M = sz.groups, sz.height, sz.width, sz.mid
    rows = 4
    n3 = 3 * M
    hbm = pl.BlockSpec(memory_space=pl.ANY)
    vmem = pl.BlockSpec(memory_space=pltpu.VMEM)
    smem = pl.BlockSpec(memory_space=pltpu.SMEM)
    shapes = ((3, 3, M, sz.wide), (3, 3, M, M), (3, 3, M, M), (M, sz.wide), (1, M), (1, M), (1, M), (1, sz.wide))
    return pl.pallas_call(
        functools.partial(kernel_b, sz, rows),
        out_shape=tuple(jax.ShapeDtypeStruct(s, f32) for s in (x.shape, x.shape) + shapes),
        in_specs=[hbm] * 7 + [vmem, smem, smem],
        out_specs=(hbm, hbm) + (vmem,) * 8,
        scratch_shapes=[
            pltpu.VMEM(x.shape, f32),
            pltpu.VMEM(x.shape, f32),
            pltpu.VMEM(q.shape, bf16),
            pltpu.VMEM(a3.shape, bf16),
            pltpu.VMEM(sums.shape, f32),
            pltpu.VMEM(k1.shape, f32),
            pltpu.VMEM(ko.shape, f32),
            pltpu.VMEM((sz.wide, 9 * n3), bf16),
            pltpu.VMEM((sz.wide, n3), bf16),
            pltpu.SemaphoreType.DMA((4, H // rows + 1)),
            pltpu.SemaphoreType.DMA((2, H // rows)),
        ],
        compiler_params=pltpu.CompilerParams(vmem_limit_bytes=60 * 2**20),
        name="wide_outputs",
    )(x, dy, q, a3, sums, k1, ko, bo, heights, widths)


def body(rows, cols, x, k1, b1, k2, b2, k3, b3, ko, bo, dy, heights, widths):
    wide, mid = k1.shape[2:]
    sz = Sizes(x.shape, mid, rows, cols)
    k1 = jnp.swapaxes(k1, 2, 3)
    q, a3, sums = call_a(
        sz, x, dy, heights, widths, k1.reshape(9 * mid, wide), k2, k3, ko, b1[None], b2[None], b3[None]
    )
    outs = call_b(sz, x, dy, q, a3, sums, k1, ko, bo[None], heights, widths)
    out, grad, g1, g2, g3, go, s1, s2, s3, so = outs
    return (
        out,
        grad,
        jnp.swapaxes(g1, 2, 3),
        s1.reshape(mid),
        g2,
        s2.reshape(mid),
        g3,
        s3.reshape(mid),
        go,
        so.reshape(wide),
    )


def solution(mesh):
    tiled = P(None, "rows", "cols", None)
    return jax.shard_map(
        functools.partial(body, mesh.shape["rows"], mesh.shape["cols"]),
        mesh=mesh,
        in_specs=(tiled,) + (P(),) * 8 + (tiled, P(), P()),
        out_specs=(tiled, tiled) + (P(),) * 8,
        check_vma=False,
    )
```

```python
import functools

import jax
import jax.numpy as jnp
from jax import lax
from jax.experimental import pallas as pl
from jax.experimental.pallas import tpu as pltpu
from jax.sharding import PartitionSpec as P

MESH = pl.DeviceIdType.MESH
bf16 = jnp.bfloat16
f32 = jnp.float32
LANES = 128
NN = (((1,), (0,)), ((), ()))
NT = (((1,), (1,)), ((), ()))
GAIN = 1.0 / 64.0
EXCHANGES = 6
GOES = ((0, 1), (0, -1), (1, 0), (-1, 0), (1, 1), (1, -1), (-1, 1), (-1, -1))


def dot(a, b, dims=NN):
    return lax.dot_general(a, b, dims, preferred_element_type=f32)


def halves(v):
    hi = v.astype(bf16)
    return hi, (v - hi.astype(f32)).astype(bf16)


def sigmoid(v):
    return 0.5 + 0.5 * jnp.tanh(0.5 * v)


def cat(parts, axis):
    return jnp.concatenate(parts, axis=axis)


def lane_column(width):
    return lax.broadcasted_iota(jnp.int32, (1, LANES), 1) % width


class Sizes:
    def __init__(self, shape, mid, rows, cols):
        self.images, self.height, self.width, self.wide = shape
        self.mid = mid
        self.rows, self.cols = rows, cols
        self.per_group = LANES // self.width
        self.groups = self.images // self.per_group
        self.block = min(16, self.height)
        self.blocks = self.height // self.block
        self.devices = rows * cols
        self.lows = dict(taps=min(rows, max(16 // (cols // 2), 1)), outs=2, second=2)
        half = 3 * mid // 8
        self.counts = dict(
            taps=9 * mid // 8 * (self.wide // LANES) + mid // 8,
            outs=(mid + 16) // 8 * (self.wide // LANES) + half + half // 2,
            second=half + half // 2,
        )
        self.parts, at = {}, 0
        for name, used in self.counts.items():
            shard = -(-used // self.devices)
            self.parts[name] = (at, shard * self.devices, shard)
            at += shard * self.devices
        self.units = at


def kernel_a(sz, refs):
    (x_hbm, dy_hbm, heights, widths, k1, k2, k3, ko_in, b1, b2, b3, q_hbm, a3_hbm, sums_out) = refs["io"]
    w1, w2, w3, t3, t2, ko, bias = [refs[n] for n in ("w1", "w2", "w3", "t3", "t2", "ko", "bias")]
    G, H, W, M = sz.groups, sz.height, sz.width, sz.mid
    RB, NB = sz.block, sz.blocks
    me_r, me_c = lax.axis_index("rows"), lax.axis_index("cols")
    col = lane_column(W)
    first, last = col == 0, col == W - 1
    ends = first | last
    even = col % 2 == 0
    n3 = 3 * M

    has_up, has_down = me_r > 0, me_r < sz.rows - 1
    has_left, has_right = me_c > 0, me_c < sz.cols - 1

    row_at = {d: lax.rem(me_r + d + sz.rows, sz.rows) if d else me_r for d in (-1, 0, 1)}
    col_at = {d: lax.rem(me_c + d + sz.cols, sz.cols) if d else me_c for d in (-1, 0, 1)}

    def neighbour(dr, dc):
        return row_at[dr], col_at[dc]

    buf = refs["buf"]
    half_rows = RB // 2

    def in_copy(src, which, g, k):
        n0 = g * sz.per_group
        return pltpu.make_async_copy(
            src.at[pl.ds(n0, sz.per_group), pl.ds(k * half_rows, half_rows)],
            buf.at[pl.ds(n0, sz.per_group), pl.ds(k * half_rows, half_rows)],
            refs["in_sem"].at[which, g, k],
        )

    in_copy(x_hbm, 0, 0, 0).start()

    k1_copy = pltpu.make_async_copy(k1, refs["acc1"], refs["k1_sem"])
    k1_copy.start()

    def prepare():
        k1_copy.wait()
        hi, lo = halves(refs["acc1"][...])
        w1[...] = cat([hi, hi, lo], 1)
        for i, b in enumerate((b1, b2, b3)):
            bias[i] = jnp.broadcast_to(b[...], (LANES, M)).T

    def prepare_rest():
        ko[:M], ko[M:] = halves(ko_in[...])
        for k, fwd, back in ((k2, w2, t2), (k3, w3, t3)):
            for p in range(3):
                at = slice(p * M, (p + 1) * M)
                hi, lo = halves(cat([k[p, q].T for q in range(3)], 1))
                fwd[at] = cat([hi, hi, lo], 1)
                hi, lo = halves(cat([k[2 - p, 2 - q] for q in range(3)], 1))
                back[at] = cat([hi, hi, lo], 1)

    core, rest = me_c % 2, me_c // 2
    pair_id = (me_r, me_c + 1 - 2 * core)

    def levels(name):
        low_count = sz.lows[name]
        near, far = sz.cols // 2 * low_count, sz.rows // low_count
        low, far_at = me_r % low_count, me_r // low_count
        near_at = rest * low_count + low
        near_ids = []
        for d in range(1, near):
            k = lax.rem(near_at + d, near)
            near_ids.append((far_at * low_count + k % low_count, (k // low_count) * 2 + core))
        far_ids = [(lax.rem(far_at + d, far) * low_count + low, me_c) for d in range(1, far)]
        return near, far, near_at, far_at, near_ids, far_ids

    barrier = pltpu.get_barrier_semaphore()
    partners = [pair_id] + [neighbour(dr, dc) for dr, dc in GOES]
    for name in ("taps", "outs"):
        near_ids, far_ids = levels(name)[4:]
        partners += near_ids + far_ids
    for dev in partners:
        pl.semaphore_signal(barrier, inc=1, device_id=dev, device_id_type=MESH)

    def message(e, g, slot):
        dr, dc = GOES[slot]
        at = (e % 2, g)
        if slot < 2:
            src, dst = refs["msg"].at[at], refs["sideway"].at[(*at, slot)]
        elif slot < 4:
            src = refs["rowmsg"].at[(*at, 3 - slot)]
            dst = refs["updown"].at[(*at, pl.ds((slot - 2) * M, M))]
        else:
            src = refs["cormsg"].at[(*at, 1 if dr > 0 else 0)]
            dst = refs["updown"].at[(*at, pl.ds(2 * M + 8 * (slot - 4), 8))]
        kind = 0 if slot < 2 else 1
        return pltpu.make_async_remote_copy(
            src_ref=src,
            dst_ref=dst,
            send_sem=refs["send"].at[e, g, kind],
            recv_sem=refs["recv"].at[e, g, kind],
            device_id=neighbour(dr, dc),
            device_id_type=MESH,
        )

    def landed(e, g, kind, sem):
        held = refs["updown" if kind else "sideway"].at[e % 2, g]
        pltpu.make_async_copy(held, held, refs[sem].at[e, g, kind]).wait()

    def send(e, g, top, bottom, top_rim, bottom_rim):
        for slot in (0, 1):
            message(e, g, slot).start()
        refs["rowmsg"][e % 2, g, 0] = top
        refs["rowmsg"][e % 2, g, 1] = bottom
        for slot in (2, 3):
            message(e, g, slot).start()
        refs["cormsg"][e % 2, g, 0] = pack_corner(top_rim)
        refs["cormsg"][e % 2, g, 1] = pack_corner(bottom_rim)
        for slot in (4, 5, 6, 7):
            message(e, g, slot).start()

    def reuse(e, g):
        if e >= 2:
            for kind in range(2):
                landed(e - 2, g, kind, "send")

    def receive(e, g, kind):
        landed(e, g, kind, "recv")

    def pack(held, value, u):
        moved = pltpu.roll(value, lax.rem(LANES + 1 + 2 * u, LANES), 1)
        return jnp.where(col // 2 == u, moved, held)

    def pack_corner(value):
        held = jnp.zeros((8, LANES), f32)
        for k in range(M // 8):
            held = jnp.where(col // 2 == k, pltpu.roll(value[8 * k : 8 * k + 8], 1 + 2 * k, 1), held)
        return held

    def beyond(e, g, lower):
        row = refs["updown"][e % 2, g, pl.ds(M if lower else 0, M)]
        at = 2 if lower else 0
        there = has_down if lower else has_up
        left = jnp.where(there & has_left, corner_left(refs["updown"][e % 2, g, pl.ds(2 * M + 8 * at, 8)]), 0.0)
        right = jnp.where(there & has_right, corner_right(refs["updown"][e % 2, g, pl.ds(2 * M + 8 * (at + 1), 8)]), 0.0)
        return jnp.where(there, row, 0.0), jnp.where(first, left, right)

    def meet(e, g):
        left = jnp.where(has_left, refs["sideway"][e % 2, g, 0], 0.0)
        right = jnp.where(has_right, refs["sideway"][e % 2, g, 1], 0.0)
        refs["met"][g] = jnp.where(even, left, pltpu.roll(right, (2 * W - 2) % LANES, 1))

    def from_sides(held, u):
        return pltpu.roll(held, LANES - W - 2 * u, 1)

    def corner_left(held):
        return cat([pltpu.roll(held, LANES - W - 2 * k, 1) for k in range(M // 8)], 0)

    def corner_right(held):
        return cat([pltpu.roll(held, W - 2 - 2 * k, 1) for k in range(M // 8)], 0)

    def nothing():
        pass

    def run(*phases, lo=0, hi=NB, flat=False):
        lo, hi = min(lo, NB), min(hi, NB)
        if lo == hi:
            return
        if lo == 0:
            for before, _, _ in phases:
                before()

        def step(b, carry):
            for _, body, _ in phases:
                body(b)
            return carry

        if flat:
            for b in range(lo, hi):
                step(b, 0)
        else:
            lax.fori_loop(lo, hi, step, 0)
        if hi == NB:
            for _, _, after in phases:
                after()

    def conv_first(g):
        a0, z, carry = refs["a0"][g], refs["slope3"][g], refs["carry"][g]

        def before():
            carry[...] = jnp.zeros_like(carry)
            refs["msg"][0, g] = jnp.zeros((M, LANES), f32)

        def emit(row, s, held):
            s0, s1, s2 = s[:M], s[M : 2 * M], s[2 * M :]
            value = s1 + jnp.where(first, 0.0, pltpu.roll(s0, 1, 1))
            value = value + jnp.where(last, 0.0, pltpu.roll(s2, LANES - 1, 1))
            z[row + 1] = value
            rim = jnp.where(first, s2, s0)
            return rim, pack(held, rim, row)

        def body(b):
            held = refs["msg"][0, g]
            c0, c1 = carry[0], carry[1]
            for m in range(RB // 2):
                r = b * RB + 2 * m
                if 2 * m % half_rows == 0:
                    in_copy(x_hbm, 0, g, 2 * b + 2 * m // half_rows).wait()
                pair = []
                for i in range(2):
                    v = cat([buf[g * sz.per_group + s, r + i] for s in range(sz.per_group)], 0)
                    hi, lo = halves(v * sigmoid(v))
                    both = cat([hi, lo], 1)
                    a0[r + i] = both
                    pair.append(both)
                rhs = cat(pair, 0)
                y = dot(w1[...], cat([rhs, rhs[:, : sz.wide]], 1), NT)
                ya, yb = y[:, :LANES], y[:, LANES:]
                rim, held = emit(r - 1, c0 + ya[2 * n3 :], held)
                if m == 0:
                    refs["rim"][g, jnp.minimum(b, 1)] = rim
                _, held = emit(r, c1 + ya[n3 : 2 * n3] + yb[2 * n3 :], held)
                c0, c1 = ya[:n3] + yb[n3 : 2 * n3], yb[:n3]
            carry[0] = c0
            carry[1] = c1
            refs["msg"][0, g] = held

        def after():
            _, held = emit(H - 1, carry[0], refs["msg"][0, g])
            rim, _ = emit(H, carry[1], held)
            refs["msg"][0, g] = held
            for k in range(2 * NB):
                in_copy(dy_hbm, 1, g, k).start()
            send(0, g, z[0], z[H + 1], refs["rim"][g, 0], rim)

        return before, body, after

    def after_first(g):
        z, act, slope = refs["slope3"][g], refs["act"][g], refs["slope1"][g]
        def before():
            receive(0, g, 0)
            meet(0, g)
            refs["msg"][1, g] = jnp.zeros((M, LANES), f32)

        def emit(r, v, held):
            v = v + bias[0]
            sig = sigmoid(v)
            a = v * sig
            slope[r] = sig + a * (1.0 - sig)
            act[r] = a
            return pack(held, a, r)

        def with_sides(r):
            return z[r + 1] + jnp.where(ends, from_sides(refs["met"][g], r), 0.0)

        def body(b):
            held = refs["msg"][1, g]
            for k in range(RB):
                r = b * RB + k
                held = emit(r, with_sides(r), held)
            refs["msg"][1, g] = held

        def after():
            receive(0, g, 1)
            held = refs["msg"][1, g]
            for r, lower in ((0, False), (H - 1, True)):
                row, sides = beyond(0, g, lower)
                held = emit(r, with_sides(r) + row + jnp.where(ends, sides, 0.0), held)
            refs["msg"][1, g] = held
            send(1, g, act[0], act[H - 1], act[0], act[H - 1])

        return before, body, after

    def spread(e, g, dst):
        act = refs["act"][g]

        def before():
            receive(e, g, 0)
            meet(e, g)

        def store(row, v, left, right):
            before = jnp.where(first, left, pltpu.roll(v, 1, 1))
            behind = jnp.where(last, right, pltpu.roll(v, LANES - 1, 1))
            for at, part in enumerate((before, v, behind)):
                hi, lo = halves(part)
                dst[row, at * M : (at + 1) * M] = hi
                dst[row, n3 + at * M : n3 + (at + 1) * M] = lo

        def body(b):
            both = refs["met"][g]
            for k in range(RB):
                r = b * RB + k
                sides = from_sides(both, r)
                store(r + 1, act[r], sides, sides)

        def after():
            receive(e, g, 1)
            for at, lower in ((0, False), (H + 1, True)):
                row, sides = beyond(e, g, lower)
                store(at, row, sides, sides)

        return before, body, after

    def conv_mid(g, src, weight, emit, begin, end):
        carry = refs["carry"][g]

        def pair(m):
            rhs = cat([src[2 * m], src[2 * m + 1]], 1)
            y = dot(weight[...], cat([rhs, rhs[:n3]], 0))
            return y[:, :LANES], y[:, LANES:]

        def before():
            ya, yb = pair(0)
            carry[0, :M] = ya[:M] + yb[M : 2 * M]
            carry[1, :M] = yb[:M]

        def body(b):
            state = begin(b)
            c0, c1 = carry[0, :M], carry[1, :M]
            for k in range(RB // 2):
                ya, yb = pair(1 + b * (RB // 2) + k)
                r = b * RB + 2 * k
                state = emit(r, c0 + ya[2 * M :], state)
                state = emit(r + 1, c1 + ya[M : 2 * M] + yb[2 * M :], state)
                c0, c1 = ya[:M] + yb[M : 2 * M], yb[:M]
            carry[0, :M] = c0
            carry[1, :M] = c1
            end(b, state)

        return before, body

    def second(g):
        act, slope = refs["act"][g], refs["slope2"][g]

        def clear():
            reuse(2, g)
            refs["msg"][0, g] = jnp.zeros((M, LANES), f32)

        def emit(r, v, held):
            v = v + bias[1]
            sig = sigmoid(v)
            a = v * sig
            slope[r] = sig + a * (1.0 - sig)
            act[r] = a
            return pack(held, a, r)

        def end(b, held):
            refs["msg"][0, g] = held

        before, body = conv_mid(g, refs["p1"][g], w2, emit, lambda b: refs["msg"][0, g], end)
        return (lambda: (clear(), before())), body, lambda: send(2, g, act[0], act[H - 1], act[0], act[H - 1])

    def a3_copy(g, b):
        return pltpu.make_async_copy(
            refs["a3"].at[b % 2], a3_hbm.at[g, pl.ds(b * RB, RB)], refs["out_sem"].at[g, b]
        )

    def third(g):
        a3, slope = refs["a3"], refs["slope3"][g]

        def emit(r, v, state):
            v = v + bias[2]
            sig = sigmoid(v)
            a = v * sig
            slope[r] = sig + a * (1.0 - sig)
            hi, lo = halves(a)
            k = r - state * RB
            a3[state % 2, k, :M] = hi
            a3[state % 2, k, M:] = lo
            return state

        def begin(b):
            if NB > 2:

                @pl.when(b >= 2)
                def _():
                    a3_copy(g, b - 2).wait()

            return b

        before, body = conv_mid(g, refs["p2"][g], w3, emit, begin, lambda b, s: a3_copy(g, b).start())

        def after():
            for k in range(max(NB - 2, 0), NB):
                a3_copy(g, k).wait()

        return before, body, after

    def column_masks(g, scale):
        across = lax.broadcasted_iota(jnp.int32, (W, 1), 0) + me_c * W
        return [(across < widths[g * sz.per_group + s]).astype(f32) * scale for s in range(sz.per_group)]

    def row_valid(n, r):
        return jnp.where(me_r * H + r < heights[n], 1.0, 0.0)

    def emit_grad(e, g, own, total, slope):
        act = refs["act"][g]

        def emit(r, v, state):
            held, summed = state
            d = v * slope[r]
            act[r] = d
            if own is not None:
                hi, lo = halves(d)
                own[r + 1, :M] = hi
                own[r + 1, M:] = lo
            return pack(held, d, r), summed + d

        def begin(b):
            return refs["msg"][e % 2, g], total[...]

        def end(b, state):
            refs["msg"][e % 2, g] = state[0]
            total[...] = state[1]

        def clear():
            reuse(e, g)
            refs["msg"][e % 2, g] = jnp.zeros((M, LANES), f32)

        return emit, begin, end, clear

    def out_layer(g):
        a3, act = refs["a3"], refs["act"][g]
        emit, begin, end, clear = emit_grad(3, g, refs["d3"][g], refs["total"].at[2], refs["slope3"][g])
        ones = jnp.ones((16, 2 * LANES), bf16)
        inside = column_masks(g, GAIN)

        def body(b):
            for h in range(2):
                in_copy(dy_hbm, 1, g, 2 * b + h).wait()
            state = begin(b)
            upper, lower = refs["acc_o1"][...], refs["acc_o2"][...]
            for m in range(RB // 2):
                r = b * RB + 2 * m
                parts = []
                for i in range(2):
                    for s in range(sz.per_group):
                        n = g * sz.per_group + s
                        parts.append(buf[n, r + i] * (inside[s] * row_valid(n, r + i)))
                hi, lo = halves(cat(parts, 0))
                y1 = dot(ko[...], hi, NT)
                y2 = dot(ko[:M], lo, NT)
                y = y1[:M] + y1[M:] + y2
                state = emit(r, y[:, :LANES], state)
                state = emit(r + 1, y[:, LANES:], state)
                act3 = cat([a3[b % 2, 2 * m], a3[b % 2, 2 * m + 1]], 1)
                upper = upper + dot(cat([act3, ones], 0), hi)
                lower = lower + dot(cat([act3[:M], ones], 0), lo)
            refs["acc_o1"][...] = upper
            refs["acc_o2"][...] = lower
            end(b, state)

        return clear, body, lambda: send(3, g, act[0], act[H - 1], act[0], act[H - 1])

    def back_layer(e, g, weight, own, total, slope):
        act = refs["act"][g]
        emit, begin, end, clear = emit_grad(e, g, own, total, slope)
        before, body = conv_mid(g, refs["q"][g], weight, emit, begin, end)
        return (lambda: (clear(), before())), body, lambda: send(e, g, act[0], act[H - 1], act[0], act[H - 1])

    def mid_kernel_grad(g, src, own, acc):
        def terms(rows, own_rows):
            left = cat(rows, 1)
            right = [cat(two, 1) for two in own_rows]
            hi = cat([two[:M] for two in right], 0)
            lo = cat([two[M:] for two in right], 0)
            return cat([left[:n3], left[:n3], left[n3:]], 1), cat([hi, lo, hi], 1)

        def body(b):
            ls, rs = [], []
            for m in range(RB // 2):
                r = b * RB + 2 * m
                l, rr = terms(
                    [src[r + 1], src[r + 2]], [[own[r + 2 - p], own[r + 3 - p]] for p in range(3)]
                )
                ls.append(l)
                rs.append(rr)
            acc[...] += dot(cat(ls, 1), cat(rs, 1), NT)

        def after():
            none = jnp.zeros((2 * M, LANES), bf16)
            l, rr = terms([src[0], src[H + 1]], [[own[1], none], [none, none], [none, own[H]]])
            acc[...] += dot(l, rr, NT)

        return nothing, body, after

    def first_kernel_grad(g):
        a0, q, acc = refs["a0"][g], refs["q"][g], refs["acc1"]

        def body(b):
            ls, rs = [], []
            for m in range(RB // 2):
                r = b * RB + 2 * m
                three = [cat([q[r + s], q[r + 1 + s]], 1) for s in range(3)]
                hi = cat([t[:n3] for t in three], 0)
                lo = cat([t[n3:] for t in three], 0)
                ls.append(cat([hi, hi, lo], 1))
                two = cat([a0[r], a0[r + 1]], 0)
                rs.append(cat([two[:, : sz.wide], two[:, sz.wide :], two[:, : sz.wide]], 0))
            for m in range(0, RB // 2, 2):
                acc[...] += dot(cat(ls[m : m + 2], 1), cat(rs[m : m + 2], 0))

        return nothing, body, nothing

    def reducer(name):
        base, units, shard = sz.parts[name]
        near, far, near_at, far_at, near_ids, far_ids = levels(name)
        half, quarter = units // 2, units // 2 // near
        ar, whole = refs["ar"], refs["ar_all"]
        sems = list(sz.parts).index(name)
        pair_buf = refs["pair_" + name]
        near_buf = refs["near_" + name]
        far_buf = refs["far_" + name]
        used = [0]

        def ship(src, dst, dev):
            pltpu.make_async_remote_copy(
                src_ref=src,
                dst_ref=dst,
                send_sem=refs["ar_send"].at[sems, used[0]],
                recv_sem=refs["ar_recv"].at[sems, used[0]],
                device_id=dev,
                device_id_type=MESH,
            ).start()

        def land(held):
            for sem in ("ar_recv", "ar_send"):
                pltpu.make_async_copy(held, held, refs[sem].at[sems, used[0]]).wait()
            used[0] += 1

        mine_half = base + core * half
        mine_quarter = mine_half + near_at * quarter
        mine = mine_quarter + far_at * shard

        def fill(blocks):
            at = base
            for block in blocks:
                rows = block.shape[0] // 8
                ar[at : at + rows] = block.reshape(rows, 8, LANES)
                at += rows
            if at < base + units:
                ar[at : base + units] = jnp.zeros((base + units - at, 8, LANES), f32)
            ship(ar.at[pl.ds(base + (1 - core) * half, half)], pair_buf, pair_id)

        def to_near():
            land(pair_buf)
            ar[pl.ds(mine_half, half)] += pair_buf[...]
            for d, dev in enumerate(near_ids, 1):
                to = lax.rem(near_at + d, near)
                ship(ar.at[pl.ds(mine_half + to * quarter, quarter)], near_buf.at[near - 1 - d], dev)

        def to_far():
            land(near_buf)
            got = ar[pl.ds(mine_quarter, quarter)]
            for d in range(near - 1):
                got = got + near_buf[d]
            ar[pl.ds(mine_quarter, quarter)] = got
            for d, dev in enumerate(far_ids, 1):
                to = lax.rem(far_at + d, far)
                ship(ar.at[pl.ds(mine_quarter + to * shard, shard)], far_buf.at[far - 1 - d], dev)

        def spread_far():
            land(far_buf)
            got = ar[pl.ds(mine, shard)]
            for d in range(far - 1):
                got = got + far_buf[d]
            whole[pl.ds(mine, shard)] = got
            for dev in far_ids:
                ship(whole.at[pl.ds(mine, shard)], whole.at[pl.ds(mine, shard)], dev)

        def spread_near():
            land(far_buf)
            at = pl.ds(mine_quarter, quarter)
            for dev in near_ids:
                ship(whole.at[at], whole.at[at], dev)

        def spread_pair():
            land(near_buf)
            at = pl.ds(mine_half, half)
            ship(whole.at[at], whole.at[at], pair_id)

        def done():
            land(pair_buf)
            sums = pltpu.make_async_copy(
                whole.at[pl.ds(base, units)], sums_out.at[pl.ds(base, units)], refs["sum_sem"].at[sems]
            )
            sums.start()
            return sums

        def near_only():
            land(near_buf)
            got = ar[pl.ds(mine, shard)]
            for d in range(near - 1):
                got = got + near_buf[d]
            whole[pl.ds(mine, shard)] = got
            for dev in near_ids:
                ship(whole.at[pl.ds(mine, shard)], whole.at[pl.ds(mine, shard)], dev)

        if far == 1:
            return fill, iter((to_near, near_only, spread_pair, done))
        return fill, iter((to_near, to_far, spread_far, spread_near, spread_pair, done))

    for name in ("acc2", "acc3", "acc_o1", "acc_o2", "total"):
        refs[name][...] = jnp.zeros_like(refs[name])
    none = jnp.zeros((2 * M, LANES), bf16)
    for g in range(G):
        for name in ("d2", "d3"):
            refs[name][g][0] = none
            refs[name][g][H + 1] = none

    every = range(G)
    moving, ended = {}, []

    def q_copy(g):
        return pltpu.make_async_copy(refs["q"][g], q_hbm.at[g], refs["q_sem"].at[g])

    def advance(*names):
        for name in names:
            if name not in moving:
                continue
            copy = next(moving[name])()
            if copy is not None:
                ended.append(copy)
                del moving[name]

    def reduce(name, blocks):
        fill, moving[name] = reducer(name)
        fill(blocks)

    def wide_blocks(value):
        return [value[:, h * LANES : (h + 1) * LANES] for h in range(sz.wide // LANES)]

    def mid_blocks(acc):
        value = acc[...]
        rest = value[:, LANES:]
        return [value[:, :LANES], cat([rest[: n3 // 2], rest[n3 // 2 :]], 1)]

    prepare()
    refs["acc1"][...] = jnp.zeros_like(refs["acc1"])
    for g in every:
        for k in range(2 * NB):
            if (g, k) != (0, 0):
                in_copy(x_hbm, 0, g, k).start()
    for g in every:
        before, body, after = conv_first(g)
        if g == 0:
            run((before, body, nothing))
            pl.semaphore_wait(barrier, len(partners))
            after()
        else:
            run((before, body, after))
    for g in every:
        run(after_first(g))
        if g == 0:
            prepare_rest()
    for g in every:
        run(spread(1, g, refs["p1"][g]), flat=True)
        run(second(g), flat=True)
    for g in every:
        run(spread(2, g, refs["p2"][g]), flat=True)
        run(third(g), out_layer(g))
    for g in every:
        run(spread(3, g, refs["q"][g]), mid_kernel_grad(g, refs["p2"][g], refs["d3"][g], refs["acc3"]))
        run(back_layer(4, g, t3, refs["d2"][g], refs["total"].at[1], refs["slope2"][g]), flat=True)
    upper, lower = refs["acc_o1"][...], refs["acc_o2"][...]
    outs = cat([upper[:M] + upper[M : 2 * M] + lower[:M], upper[2 * M :] + lower[M:]], 0)
    reduce("outs", wide_blocks(outs) + mid_blocks(refs["acc3"]))
    for g in every:
        run(spread(4, g, refs["q"][g]), mid_kernel_grad(g, refs["p1"][g], refs["d2"][g], refs["acc2"]))
        advance("outs")
        if g == G - 1:
            reduce("second", mid_blocks(refs["acc2"]))
        run(back_layer(5, g, t2, None, refs["total"].at[0], refs["slope1"][g]), flat=True)
    advance("second")
    lane = lax.broadcasted_iota(jnp.int32, (1, LANES), 1)
    sums = [jnp.sum(refs["total"][i], axis=1, keepdims=True) for i in range(3)]
    biases = jnp.where(lane == 0, sums[0], jnp.where(lane == 1, sums[1], sums[2]))
    for g in every:
        run(spread(5, g, refs["q"][g]), flat=True)
        q_copy(g).start()
        if g == 0:
            advance("outs")
        run(first_kernel_grad(g))
        if g < G - 1:
            advance("outs", "second")
    reduce("taps", wide_blocks(refs["acc1"]) + [biases])
    advance("second", "outs", "taps")
    while moving:
        advance(*list(moving))

    for copy in ended:
        copy.wait()
    for g in every:
        q_copy(g).wait()
    for g in every:
        for e in range(EXCHANGES - 2, EXCHANGES):
            for kind in range(2):
                landed(e, g, kind, "send")


def call_a(sz, x, dy, heights, widths, k1, k2, k3, ko, b1, b2, b3):
    G, H, W, M, N = sz.groups, sz.height, sz.width, sz.mid, LANES
    n3 = 3 * M
    names, shapes = [], []

    def add(name, *what):
        names.append((name, len(what)))
        shapes.extend(what)

    def per_group(name, shape, dtype):
        add(name, *[pltpu.VMEM(shape, dtype) for _ in range(G)])

    add("buf", pltpu.VMEM((sz.images, H, W, sz.wide), f32))
    per_group("a0", (H, N, 2 * sz.wide), bf16)
    per_group("act", (H, M, N), f32)
    per_group("carry", (2, n3, N), f32)
    for name in ("slope1", "slope2"):
        per_group(name, (H, M, N), f32)
    per_group("slope3", (H + 2, M, N), f32)
    for name in ("p1", "p2", "q"):
        per_group(name, (H + 2, 2 * n3, N), bf16)
    for name in ("d3", "d2"):
        per_group(name, (H + 2, 2 * M, N), bf16)
    add("a3", pltpu.VMEM((2, sz.block, 2 * M, N), bf16))
    add("w1", pltpu.VMEM((9 * M, 3 * sz.wide), bf16))
    for name in ("w2", "w3", "t2", "t3"):
        add(name, pltpu.VMEM((n3, 3 * n3), bf16))
    add("ko", pltpu.VMEM((2 * M, sz.wide), bf16))
    add("met", pltpu.VMEM((G, M, N), f32))
    add("bias", pltpu.VMEM((3, M, N), f32))
    E = EXCHANGES
    add("rim", pltpu.VMEM((G, 2, M, N), f32))
    add("msg", pltpu.VMEM((2, G, M, N), f32))
    add("rowmsg", pltpu.VMEM((2, G, 2, M, N), f32))
    add("cormsg", pltpu.VMEM((2, G, 2, 8, N), f32))
    add("sideway", pltpu.VMEM((2, G, 2, M, N), f32))
    add("updown", pltpu.VMEM((2, G, 2 * M + 32, N), f32))
    add("acc1", pltpu.VMEM((9 * M, sz.wide), f32))
    add("acc2", pltpu.VMEM((n3, n3), f32))
    add("acc3", pltpu.VMEM((n3, n3), f32))
    add("acc_o1", pltpu.VMEM((2 * M + 16, sz.wide), f32))
    add("acc_o2", pltpu.VMEM((M + 16, sz.wide), f32))
    add("total", pltpu.VMEM((3, M, N), f32))
    U = sz.units
    add("ar", pltpu.VMEM((U, 8, N), f32))
    add("ar_all", pltpu.VMEM((U, 8, N), f32))
    for part, (_, units, shard) in sz.parts.items():
        near = sz.cols // 2 * sz.lows[part]
        far = sz.rows // sz.lows[part]
        add("pair_" + part, pltpu.VMEM((units // 2, 8, N), f32))
        add("near_" + part, pltpu.VMEM((max(near - 1, 1), units // 2 // near, 8, N), f32))
        add("far_" + part, pltpu.VMEM((max(far - 1, 1), shard, 8, N), f32))
    add("sum_sem", pltpu.SemaphoreType.DMA((len(sz.parts),)))
    add("in_sem", pltpu.SemaphoreType.DMA((2, G, 2 * sz.blocks)))
    add("k1_sem", pltpu.SemaphoreType.DMA)
    add("q_sem", pltpu.SemaphoreType.DMA((G,)))
    add("out_sem", pltpu.SemaphoreType.DMA((G, sz.blocks)))
    add("send", pltpu.SemaphoreType.DMA((E, G, 2)))
    add("recv", pltpu.SemaphoreType.DMA((E, G, 2)))
    add("ar_send", pltpu.SemaphoreType.DMA((len(sz.parts), 6)))
    add("ar_recv", pltpu.SemaphoreType.DMA((len(sz.parts), 6)))
    grouped = ("a0", "act", "carry", "slope1", "slope2", "slope3", "p1", "p2", "q", "d3", "d2")

    def whole_kernel(*args):
        refs = {"io": args[:14]}
        at = 14
        for name, size in names:
            held = args[at : at + size]
            refs[name] = held if name in grouped else held[0]
            at += size
        kernel_a(sz, refs)

    hbm = pl.BlockSpec(memory_space=pl.ANY)
    vmem = pl.BlockSpec(memory_space=pltpu.VMEM)
    smem = pl.BlockSpec(memory_space=pltpu.SMEM)
    return pl.pallas_call(
        whole_kernel,
        out_shape=(
            jax.ShapeDtypeStruct((G, H + 2, 2 * n3, N), bf16),
            jax.ShapeDtypeStruct((G, H, 2 * M, N), bf16),
            jax.ShapeDtypeStruct((U, 8, N), f32),
        ),
        in_specs=[hbm, hbm, smem, smem, hbm] + [vmem] * 6,
        out_specs=(hbm, hbm, hbm),
        scratch_shapes=shapes,
        compiler_params=pltpu.CompilerParams(
            collective_id=0, has_side_effects=True, vmem_limit_bytes=63 * 2**20
        ),
        name="block_chain",
    )(x, dy, heights, widths, k1, k2, k3, ko, b1, b2, b3)


def kernel_b(
    sz, rows, x_hbm, dy_hbm, q_hbm, a3_hbm, sums_hbm, k1_hbm, ko_hbm, bo, heights, widths,
    out_hbm, grad_hbm, g1, g2, g3, go, s1, s2, s3, so,
    x, dy, q, a3, sums, k1, ko, wb, wo, in_sem, out_sem,
):
    G, H, W, M = sz.groups, sz.height, sz.width, sz.mid
    n3 = 3 * M
    chunks = H // rows

    def copies_in(c):
        r = c * rows
        first = [(q_hbm.at[:, pl.ds(r + 2, rows)], q.at[:, pl.ds(r + 2, rows)])]
        first.append((a3_hbm.at[:, pl.ds(r, rows)], a3.at[:, pl.ds(r, rows)]))
        first.append((x_hbm.at[:, pl.ds(r, rows)], x.at[:, pl.ds(r, rows)]))
        first.append((dy_hbm.at[:, pl.ds(r, rows)], dy.at[:, pl.ds(r, rows)]))
        return [pltpu.make_async_copy(s, d, in_sem.at[i, c]) for i, (s, d) in enumerate(first)]

    def copies_out(c):
        at = (slice(None), pl.ds(c * rows, rows))
        return [
            pltpu.make_async_copy(x.at[at], out_hbm.at[at], out_sem.at[0, c]),
            pltpu.make_async_copy(dy.at[at], grad_hbm.at[at], out_sem.at[1, c]),
        ]

    early = [
        pltpu.make_async_copy(s, d, in_sem.at[i, chunks])
        for i, (s, d) in enumerate(((k1_hbm, k1), (ko_hbm, ko), (q_hbm.at[:, pl.ds(0, 2)], q.at[:, pl.ds(0, 2)])))
    ]
    tail = pltpu.make_async_copy(sums_hbm, sums, in_sem.at[3, chunks])
    for copy in early:
        copy.start()
    for c in range(chunks):
        for copy in copies_in(c):
            copy.start()
    tail.start()
    for copy in early:
        copy.wait()

    for p in range(3):
        hi, lo = halves(cat([k1[2 - p, 2 - b].T for b in range(3)], 1))
        wb[:, 2 * p * n3 : 2 * (p + 1) * n3] = cat([hi, hi], 1)
        wb[:, (6 + p) * n3 : (7 + p) * n3] = lo
    hi, lo = halves(ko[...].T * GAIN)
    wo[...] = cat([hi, hi, lo], 1)
    add = bo[...] * GAIN

    across = lax.broadcasted_iota(jnp.int32, (W, 1), 0) + lax.axis_index("cols") * W
    inside = [(across < widths[n]).astype(f32) for n in range(sz.images)]
    start_row = lax.axis_index("rows") * H

    def body(c, carry):
        for copy in copies_in(c):
            copy.wait()
        for k in range(rows):
            i = c * rows + k
            three = [cat([q[g, i + s] for g in range(G)], 1) for s in range(3)]
            y = dot(wb[...], cat(three + [t[:n3] for t in three], 0))
            act = cat([a3[g, i] for g in range(G)], 1)
            branch = dot(wo[...], cat([act, act[:M]], 0))
            y, branch = y.T, branch.T
            for n in range(sz.images):
                at = slice(n * W, (n + 1) * W)
                v = x[n, i]
                x[n, i] = v + (branch[at] + add)
                sig = sigmoid(v)
                slope = sig * (1.0 + v * (1.0 - sig))
                valid = jnp.where(start_row + i < heights[n], 1.0, 0.0)
                dy[n, i] = dy[n, i] * (inside[n] * valid) + y[at] * slope
        for copy in copies_out(c):
            copy.start()
        return carry

    lax.fori_loop(0, chunks, body, 0)

    tail.wait()

    def take(at, count):
        return sums[at : at + count].reshape(count * 8, LANES)

    at = sz.parts["taps"][0]
    for h in range(sz.wide // LANES):
        part = take(at, 9 * M // 8)
        at += 9 * M // 8
        for t in range(3):
            for b in range(3):
                lo = (t * 3 + b) * M
                g1[2 - t, 2 - b, :, h * LANES : (h + 1) * LANES] = part[lo : lo + M]
    rest = take(at, M // 8).T
    s1[...] = rest[0:1]
    s2[...] = rest[1:2]
    s3[...] = rest[2:3]
    at = sz.parts["outs"][0]
    for h in range(sz.wide // LANES):
        part = take(at, (M + 16) // 8)
        at += (M + 16) // 8
        go[:, h * LANES : (h + 1) * LANES] = part[:M]
        so[:, h * LANES : (h + 1) * LANES] = part[M : M + 1]
    for at, ref in ((at, g3), (sz.parts["second"][0], g2)):
        big, rest = take(at, n3 // 8), take(at + n3 // 8, n3 // 16)
        rest = cat([rest[:, :M], rest[:, M:]], 0)
        for b in range(3):
            sl = slice(b * M, (b + 1) * M)
            ref[0, b] = big[sl, :M]
            ref[1, b] = big[sl, M:]
            ref[2, b] = rest[sl]

    def finish(c, carry):
        for copy in copies_out(c):
            copy.wait()
        return carry

    lax.fori_loop(0, chunks, finish, 0)


def call_b(sz, x, dy, q, a3, sums, k1, ko, bo, heights, widths):
    G, H, W, M = sz.groups, sz.height, sz.width, sz.mid
    rows = 4
    n3 = 3 * M
    hbm = pl.BlockSpec(memory_space=pl.ANY)
    vmem = pl.BlockSpec(memory_space=pltpu.VMEM)
    smem = pl.BlockSpec(memory_space=pltpu.SMEM)
    shapes = ((3, 3, M, sz.wide), (3, 3, M, M), (3, 3, M, M), (M, sz.wide), (1, M), (1, M), (1, M), (1, sz.wide))
    return pl.pallas_call(
        functools.partial(kernel_b, sz, rows),
        out_shape=tuple(jax.ShapeDtypeStruct(s, f32) for s in (x.shape, x.shape) + shapes),
        in_specs=[hbm] * 7 + [vmem, smem, smem],
        out_specs=(hbm, hbm) + (vmem,) * 8,
        scratch_shapes=[
            pltpu.VMEM(x.shape, f32),
            pltpu.VMEM(x.shape, f32),
            pltpu.VMEM(q.shape, bf16),
            pltpu.VMEM(a3.shape, bf16),
            pltpu.VMEM(sums.shape, f32),
            pltpu.VMEM(k1.shape, f32),
            pltpu.VMEM(ko.shape, f32),
            pltpu.VMEM((sz.wide, 9 * n3), bf16),
            pltpu.VMEM((sz.wide, n3), bf16),
            pltpu.SemaphoreType.DMA((4, H // rows + 1)),
            pltpu.SemaphoreType.DMA((2, H // rows)),
        ],
        compiler_params=pltpu.CompilerParams(vmem_limit_bytes=60 * 2**20),
        name="wide_outputs",
    )(x, dy, q, a3, sums, k1, ko, bo, heights, widths)


def body(rows, cols, x, k1, b1, k2, b2, k3, b3, ko, bo, dy, heights, widths):
    wide, mid = k1.shape[2:]
    sz = Sizes(x.shape, mid, rows, cols)
    k1 = jnp.swapaxes(k1, 2, 3)
    q, a3, sums = call_a(
        sz, x, dy, heights, widths, k1.reshape(9 * mid, wide), k2, k3, ko, b1[None], b2[None], b3[None]
    )
    outs = call_b(sz, x, dy, q, a3, sums, k1, ko, bo[None], heights, widths)
    out, grad, g1, g2, g3, go, s1, s2, s3, so = outs
    return (
        out,
        grad,
        jnp.swapaxes(g1, 2, 3),
        s1.reshape(mid),
        g2,
        s2.reshape(mid),
        g3,
        s3.reshape(mid),
        go,
        so.reshape(wide),
    )


def solution(mesh):
    tiled = P(None, "rows", "cols", None)
    return jax.shard_map(
        functools.partial(body, mesh.shape["rows"], mesh.shape["cols"]),
        mesh=mesh,
        in_specs=(tiled,) + (P(),) * 8 + (tiled, P(), P()),
        out_specs=(tiled, tiled) + (P(),) * 8,
        check_vma=False,
    )
```

```python
import functools

import jax
import jax.numpy as jnp
from jax import lax
from jax.experimental import pallas as pl
from jax.experimental.pallas import tpu as pltpu
from jax.sharding import PartitionSpec as P

MESH = pl.DeviceIdType.MESH
bf16 = jnp.bfloat16
f32 = jnp.float32
LANES = 128
NN = (((1,), (0,)), ((), ()))
NT = (((1,), (1,)), ((), ()))
GAIN = 1.0 / 64.0
EXCHANGES = 6
GOES = ((0, 1), (0, -1), (1, 0), (-1, 0), (1, 1), (1, -1), (-1, 1), (-1, -1))


def dot(a, b, dims=NN):
    return lax.dot_general(a, b, dims, preferred_element_type=f32)


def halves(v):
    hi = v.astype(bf16)
    return hi, (v - hi.astype(f32)).astype(bf16)


def sigmoid(v):
    return 0.5 + 0.5 * jnp.tanh(0.5 * v)


def cat(parts, axis):
    return jnp.concatenate(parts, axis=axis)


def lane_column(width):
    return lax.broadcasted_iota(jnp.int32, (1, LANES), 1) % width


class Sizes:
    def __init__(self, shape, mid, rows, cols):
        self.images, self.height, self.width, self.wide = shape
        self.mid = mid
        self.rows, self.cols = rows, cols
        self.per_group = LANES // self.width
        self.groups = self.images // self.per_group
        self.block = min(16, self.height)
        self.blocks = self.height // self.block
        self.devices = rows * cols
        self.lows = dict(taps=min(rows, max(16 // (cols // 2), 1)), rest=2)
        half = 3 * mid // 8
        self.counts = dict(
            taps=9 * mid // 8 * (self.wide // LANES) + mid // 8,
            rest=(mid + 16) // 8 * (self.wide // LANES) + 2 * (half + half // 2),
        )
        self.parts, at = {}, 0
        for name, used in self.counts.items():
            shard = -(-used // self.devices)
            self.parts[name] = (at, shard * self.devices, shard)
            at += shard * self.devices
        self.units = at


def kernel_a(sz, refs):
    (x_hbm, dy_hbm, heights, widths, k1, k2, k3, ko_in, b1, b2, b3, grad_hbm, a3_hbm, sums_out) = refs["io"]
    w1, w2, w3, t3, t2, ko, bias = [refs[n] for n in ("w1", "w2", "w3", "t3", "t2", "ko", "bias")]
    G, H, W, M = sz.groups, sz.height, sz.width, sz.mid
    RB, NB = sz.block, sz.blocks
    me_r, me_c = lax.axis_index("rows"), lax.axis_index("cols")
    col = lane_column(W)
    first, last = col == 0, col == W - 1
    ends = first | last
    even = col % 2 == 0
    n3 = 3 * M

    has_up, has_down = me_r > 0, me_r < sz.rows - 1
    has_left, has_right = me_c > 0, me_c < sz.cols - 1

    row_at = {d: lax.rem(me_r + d + sz.rows, sz.rows) if d else me_r for d in (-1, 0, 1)}
    col_at = {d: lax.rem(me_c + d + sz.cols, sz.cols) if d else me_c for d in (-1, 0, 1)}

    def neighbour(dr, dc):
        return row_at[dr], col_at[dc]

    buf = refs["buf"]
    half_rows = RB // 2

    def in_copy(src, which, g, k):
        n0 = g * sz.per_group
        return pltpu.make_async_copy(
            src.at[pl.ds(n0, sz.per_group), pl.ds(k * half_rows, half_rows)],
            buf.at[pl.ds(n0, sz.per_group), pl.ds(k * half_rows, half_rows)],
            refs["in_sem"].at[which, g, k],
        )

    in_copy(x_hbm, 0, 0, 0).start()

    k1_copy = pltpu.make_async_copy(k1, refs["acc1"], refs["k1_sem"])
    k1_copy.start()

    def prepare():
        k1_copy.wait()
        hi, lo = halves(refs["acc1"][...])
        w1[...] = cat([hi, hi, lo], 1)
        for i, b in enumerate((b1, b2, b3)):
            bias[i] = jnp.broadcast_to(b[...], (LANES, M)).T

    def prepare_rest():
        back = refs["acc1"][...].reshape(3, 3, M, sz.wide)
        for p in range(3):
            hi, lo = halves(cat([back[2 - p, 2 - b].T for b in range(3)], 1))
            refs["wb"][:, 2 * p * n3 : 2 * (p + 1) * n3] = cat([hi, hi], 1)
            refs["wb"][:, (6 + p) * n3 : (7 + p) * n3] = lo
        across = lax.broadcasted_iota(jnp.int32, (W, LANES), 0) + me_c * W
        for n in range(sz.images):
            refs["inside"][n] = jnp.where(across < widths[n], 1.0, 0.0)
        ko[:M], ko[M:] = halves(ko_in[...])
        for k, fwd, back in ((k2, w2, t2), (k3, w3, t3)):
            for p in range(3):
                at = slice(p * M, (p + 1) * M)
                hi, lo = halves(cat([k[p, q].T for q in range(3)], 1))
                fwd[at] = cat([hi, hi, lo], 1)
                hi, lo = halves(cat([k[2 - p, 2 - q] for q in range(3)], 1))
                back[at] = cat([hi, hi, lo], 1)

    core, rest = me_c % 2, me_c // 2
    pair_id = (me_r, me_c + 1 - 2 * core)

    def levels(name):
        low_count = sz.lows[name]
        near, far = sz.cols // 2 * low_count, sz.rows // low_count
        low, far_at = me_r % low_count, me_r // low_count
        near_at = rest * low_count + low
        near_ids = []
        for d in range(1, near):
            k = lax.rem(near_at + d, near)
            near_ids.append((far_at * low_count + k % low_count, (k // low_count) * 2 + core))
        far_ids = [(lax.rem(far_at + d, far) * low_count + low, me_c) for d in range(1, far)]
        return near, far, near_at, far_at, near_ids, far_ids

    barrier = pltpu.get_barrier_semaphore()
    partners = [pair_id] + [neighbour(dr, dc) for dr, dc in GOES]
    for name in ("taps", "rest"):
        near_ids, far_ids = levels(name)[4:]
        partners += near_ids + far_ids
    for dev in partners:
        pl.semaphore_signal(barrier, inc=1, device_id=dev, device_id_type=MESH)

    def message(e, g, slot):
        dr, dc = GOES[slot]
        at = (e % 2, g)
        if slot < 2:
            src, dst = refs["msg"].at[at], refs["sideway"].at[(*at, slot)]
        elif slot < 4:
            src = refs["rowmsg"].at[(*at, 3 - slot)]
            dst = refs["updown"].at[(*at, pl.ds((slot - 2) * M, M))]
        else:
            src = refs["cormsg"].at[(*at, 1 if dr > 0 else 0)]
            dst = refs["updown"].at[(*at, pl.ds(2 * M + 8 * (slot - 4), 8))]
        kind = 0 if slot < 2 else 1
        return pltpu.make_async_remote_copy(
            src_ref=src,
            dst_ref=dst,
            send_sem=refs["send"].at[e, g, kind],
            recv_sem=refs["recv"].at[e, g, kind],
            device_id=neighbour(dr, dc),
            device_id_type=MESH,
        )

    def landed(e, g, kind, sem):
        held = refs["updown" if kind else "sideway"].at[e % 2, g]
        pltpu.make_async_copy(held, held, refs[sem].at[e, g, kind]).wait()

    def send(e, g, top, bottom, top_rim, bottom_rim):
        for slot in (0, 1):
            message(e, g, slot).start()
        refs["rowmsg"][e % 2, g, 0] = top
        refs["rowmsg"][e % 2, g, 1] = bottom
        for slot in (2, 3):
            message(e, g, slot).start()
        refs["cormsg"][e % 2, g, 0] = pack_corner(top_rim)
        refs["cormsg"][e % 2, g, 1] = pack_corner(bottom_rim)
        for slot in (4, 5, 6, 7):
            message(e, g, slot).start()

    def reuse(e, g):
        if e >= 2:
            for kind in range(2):
                landed(e - 2, g, kind, "send")

    def receive(e, g, kind):
        landed(e, g, kind, "recv")

    def pack(held, value, u):
        moved = pltpu.roll(value, lax.rem(LANES + 1 + 2 * u, LANES), 1)
        return jnp.where(col // 2 == u, moved, held)

    def pack_corner(value):
        held = jnp.zeros((8, LANES), f32)
        for k in range(M // 8):
            held = jnp.where(col // 2 == k, pltpu.roll(value[8 * k : 8 * k + 8], 1 + 2 * k, 1), held)
        return held

    def beyond(e, g, lower):
        row = refs["updown"][e % 2, g, pl.ds(M if lower else 0, M)]
        at = 2 if lower else 0
        there = has_down if lower else has_up
        left = jnp.where(there & has_left, corner_left(refs["updown"][e % 2, g, pl.ds(2 * M + 8 * at, 8)]), 0.0)
        right = jnp.where(there & has_right, corner_right(refs["updown"][e % 2, g, pl.ds(2 * M + 8 * (at + 1), 8)]), 0.0)
        return jnp.where(there, row, 0.0), jnp.where(first, left, right)

    def meet(e, g):
        left = jnp.where(has_left, refs["sideway"][e % 2, g, 0], 0.0)
        right = jnp.where(has_right, refs["sideway"][e % 2, g, 1], 0.0)
        refs["met"][g] = jnp.where(even, left, pltpu.roll(right, (2 * W - 2) % LANES, 1))

    def from_sides(held, u):
        return pltpu.roll(held, LANES - W - 2 * u, 1)

    def corner_left(held):
        return cat([pltpu.roll(held, LANES - W - 2 * k, 1) for k in range(M // 8)], 0)

    def corner_right(held):
        return cat([pltpu.roll(held, W - 2 - 2 * k, 1) for k in range(M // 8)], 0)

    def nothing():
        pass

    def run(*phases, lo=0, hi=NB, flat=False):
        lo, hi = min(lo, NB), min(hi, NB)
        if lo == hi:
            return
        if lo == 0:
            for before, _, _ in phases:
                before()

        def step(b, carry):
            for _, body, _ in phases:
                body(b)
            return carry

        if flat:
            for b in range(lo, hi):
                step(b, 0)
        else:
            lax.fori_loop(lo, hi, step, 0)
        if hi == NB:
            for _, _, after in phases:
                after()

    def conv_first(g):
        a0, z, carry = refs["a0"][g], refs["slope3"][g], refs["carry"][g]

        def before():
            carry[...] = jnp.zeros_like(carry)
            refs["msg"][0, g] = jnp.zeros((M, LANES), f32)

        def emit(row, s, held):
            s0, s1, s2 = s[:M], s[M : 2 * M], s[2 * M :]
            value = s1 + jnp.where(first, 0.0, pltpu.roll(s0, 1, 1))
            value = value + jnp.where(last, 0.0, pltpu.roll(s2, LANES - 1, 1))
            z[row + 1] = value
            rim = jnp.where(first, s2, s0)
            return rim, pack(held, rim, row)

        def body(b):
            held = refs["msg"][0, g]
            c0, c1 = carry[0], carry[1]
            for m in range(RB // 2):
                r = b * RB + 2 * m
                if 2 * m % half_rows == 0:
                    in_copy(x_hbm, 0, g, 2 * b + 2 * m // half_rows).wait()
                pair = []
                for i in range(2):
                    v = cat([buf[g * sz.per_group + s, r + i] for s in range(sz.per_group)], 0)
                    hi, lo = halves(v * sigmoid(v))
                    both = cat([hi, lo], 1)
                    a0[r + i] = both
                    pair.append(both)
                rhs = cat(pair, 0)
                y = dot(w1[...], cat([rhs, rhs[:, : sz.wide]], 1), NT)
                ya, yb = y[:, :LANES], y[:, LANES:]
                rim, held = emit(r - 1, c0 + ya[2 * n3 :], held)
                if m == 0:
                    refs["rim"][g, jnp.minimum(b, 1)] = rim
                _, held = emit(r, c1 + ya[n3 : 2 * n3] + yb[2 * n3 :], held)
                c0, c1 = ya[:n3] + yb[n3 : 2 * n3], yb[:n3]
            carry[0] = c0
            carry[1] = c1
            refs["msg"][0, g] = held

        def after():
            _, held = emit(H - 1, carry[0], refs["msg"][0, g])
            rim, _ = emit(H, carry[1], held)
            refs["msg"][0, g] = held
            for k in range(2 * NB):
                in_copy(dy_hbm, 1, g, k).start()
            send(0, g, z[0], z[H + 1], refs["rim"][g, 0], rim)

        return before, body, after

    def after_first(g):
        z, act, slope = refs["slope3"][g], refs["act"][g], refs["slope1"][g]
        def before():
            receive(0, g, 0)
            meet(0, g)
            refs["msg"][1, g] = jnp.zeros((M, LANES), f32)

        def emit(r, v, held):
            v = v + bias[0]
            sig = sigmoid(v)
            a = v * sig
            slope[r] = sig + a * (1.0 - sig)
            act[r] = a
            return pack(held, a, r)

        def with_sides(r):
            return z[r + 1] + jnp.where(ends, from_sides(refs["met"][g], r), 0.0)

        def body(b):
            held = refs["msg"][1, g]
            for k in range(RB):
                r = b * RB + k
                held = emit(r, with_sides(r), held)
            refs["msg"][1, g] = held

        def after():
            receive(0, g, 1)
            held = refs["msg"][1, g]
            for r, lower in ((0, False), (H - 1, True)):
                row, sides = beyond(0, g, lower)
                held = emit(r, with_sides(r) + row + jnp.where(ends, sides, 0.0), held)
            refs["msg"][1, g] = held
            send(1, g, act[0], act[H - 1], act[0], act[H - 1])

        return before, body, after

    def spread(e, g, dst):
        act = refs["act"][g]

        def before():
            receive(e, g, 0)
            meet(e, g)

        def store(row, v, left, right):
            before = jnp.where(first, left, pltpu.roll(v, 1, 1))
            behind = jnp.where(last, right, pltpu.roll(v, LANES - 1, 1))
            for at, part in enumerate((before, v, behind)):
                hi, lo = halves(part)
                dst[row, at * M : (at + 1) * M] = hi
                dst[row, n3 + at * M : n3 + (at + 1) * M] = lo

        def body(b):
            both = refs["met"][g]
            for k in range(RB):
                r = b * RB + k
                sides = from_sides(both, r)
                store(r + 1, act[r], sides, sides)

        def after():
            receive(e, g, 1)
            for at, lower in ((0, False), (H + 1, True)):
                row, sides = beyond(e, g, lower)
                store(at, row, sides, sides)

        return before, body, after

    def conv_mid(g, src, weight, emit, begin, end):
        carry = refs["carry"][g]

        def pair(m):
            rhs = cat([src[2 * m], src[2 * m + 1]], 1)
            y = dot(weight[...], cat([rhs, rhs[:n3]], 0))
            return y[:, :LANES], y[:, LANES:]

        def before():
            ya, yb = pair(0)
            carry[0, :M] = ya[:M] + yb[M : 2 * M]
            carry[1, :M] = yb[:M]

        def body(b):
            state = begin(b)
            c0, c1 = carry[0, :M], carry[1, :M]
            for k in range(RB // 2):
                ya, yb = pair(1 + b * (RB // 2) + k)
                r = b * RB + 2 * k
                state = emit(r, c0 + ya[2 * M :], state)
                state = emit(r + 1, c1 + ya[M : 2 * M] + yb[2 * M :], state)
                c0, c1 = ya[:M] + yb[M : 2 * M], yb[:M]
            carry[0, :M] = c0
            carry[1, :M] = c1
            end(b, state)

        return before, body

    def second(g):
        act, slope = refs["act"][g], refs["slope2"][g]

        def clear():
            reuse(2, g)
            refs["msg"][0, g] = jnp.zeros((M, LANES), f32)

        def emit(r, v, held):
            v = v + bias[1]
            sig = sigmoid(v)
            a = v * sig
            slope[r] = sig + a * (1.0 - sig)
            act[r] = a
            return pack(held, a, r)

        def end(b, held):
            refs["msg"][0, g] = held

        before, body = conv_mid(g, refs["p1"][g], w2, emit, lambda b: refs["msg"][0, g], end)
        return (lambda: (clear(), before())), body, lambda: send(2, g, act[0], act[H - 1], act[0], act[H - 1])

    def a3_copy(g, b):
        return pltpu.make_async_copy(
            refs["a3"].at[b % 2], a3_hbm.at[g, pl.ds(b * RB, RB)], refs["out_sem"].at[g, b]
        )

    def third(g):
        a3, slope = refs["a3"], refs["slope3"][g]

        def emit(r, v, state):
            v = v + bias[2]
            sig = sigmoid(v)
            a = v * sig
            slope[r] = sig + a * (1.0 - sig)
            hi, lo = halves(a)
            k = r - state * RB
            a3[state % 2, k, :M] = hi
            a3[state % 2, k, M:] = lo
            return state

        def begin(b):
            if NB > 2:

                @pl.when(b >= 2)
                def _():
                    a3_copy(g, b - 2).wait()

            return b

        before, body = conv_mid(g, refs["p2"][g], w3, emit, begin, lambda b, s: a3_copy(g, b).start())

        def after():
            for k in range(max(NB - 2, 0), NB):
                a3_copy(g, k).wait()

        return before, body, after

    ring_rows = 4
    ring_count = H // ring_rows

    def again(g, k):
        at = (pl.ds(g * sz.per_group, sz.per_group), pl.ds(k * half_rows, half_rows))
        return (
            pltpu.make_async_copy(x_hbm.at[at], buf.at[at], refs["again_sem"].at[0, g, k]),
            pltpu.make_async_copy(buf.at[at], grad_hbm.at[at], refs["again_sem"].at[1, g, k]),
        )

    def cotangent(t, slot):
        t = lax.rem(t, G * ring_count)
        at = (
            pl.ds(t // ring_count * sz.per_group, sz.per_group),
            pl.ds(lax.rem(t, ring_count) * ring_rows, ring_rows),
        )
        return pltpu.make_async_copy(dy_hbm.at[at], refs["ring"].at[slot], refs["ring_sem"].at[slot])

    def masked(value, s, n, r):
        keep = refs["inside"][n] * jnp.where(me_r * H + r < heights[n], 1.0, 0.0)
        return value * cat([keep] * (sz.wide // LANES), 1)

    def input_grad(g):
        q, wb = refs["q"][g], refs["wb"]

        def body(b):
            for m in range(RB // 2):
                r = b * RB + 2 * m
                if 2 * m % half_rows == 0:
                    again(g, 2 * b + 2 * m // half_rows)[0].wait()
                t = g * ring_count + b * (RB // ring_rows) + 2 * m // ring_rows
                slot, at_row = 2 * m // ring_rows % 2, 2 * m % ring_rows
                if at_row == 0:
                    cotangent(t, slot).wait()
                dy = refs["ring"].at[slot]
                three = [cat([q[r + s], q[r + 1 + s]], 1) for s in range(3)]
                y = dot(wb[...], cat(three + [t3[:n3] for t3 in three], 0)).T
                for i in range(2):
                    for s in range(sz.per_group):
                        n = g * sz.per_group + s
                        at = i * LANES + s * W
                        v = buf[n, r + i]
                        sig = sigmoid(v)
                        slope = sig * (1.0 + v * (1.0 - sig))
                        buf[n, r + i] = masked(dy[s, at_row + i], s, n, r + i) + y[at : at + W] * slope
                if at_row == ring_rows - 2:
                    cotangent(t + 2, slot).start()
                if (2 * m + 2) % half_rows == 0:
                    again(g, 2 * b + 2 * m // half_rows)[1].start()

        return nothing, body, nothing

    def emit_grad(e, g, own, total, slope):
        act = refs["act"][g]

        def emit(r, v, state):
            held, summed = state
            d = v * slope[r]
            act[r] = d
            if own is not None:
                hi, lo = halves(d)
                own[r + 1, :M] = hi
                own[r + 1, M:] = lo
            return pack(held, d, r), summed + d

        def begin(b):
            return refs["msg"][e % 2, g], total[...]

        def end(b, state):
            refs["msg"][e % 2, g] = state[0]
            total[...] = state[1]

        def clear():
            reuse(e, g)
            refs["msg"][e % 2, g] = jnp.zeros((M, LANES), f32)

        return emit, begin, end, clear

    def out_layer(g):
        a3, act = refs["a3"], refs["act"][g]
        emit, begin, end, clear = emit_grad(3, g, refs["d3"][g], refs["total"].at[2], refs["slope3"][g])
        ones = jnp.ones((16, 2 * LANES), bf16)

        def body(b):
            for h in range(2):
                in_copy(dy_hbm, 1, g, 2 * b + h).wait()
            state = begin(b)
            upper, lower = refs["acc_o1"][...], refs["acc_o2"][...]
            for m in range(RB // 2):
                r = b * RB + 2 * m
                parts = []
                for i in range(2):
                    for s in range(sz.per_group):
                        n = g * sz.per_group + s
                        parts.append(masked(buf[n, r + i], s, n, r + i) * GAIN)
                hi, lo = halves(cat(parts, 0))
                y1 = dot(ko[...], hi, NT)
                y2 = dot(ko[:M], lo, NT)
                y = y1[:M] + y1[M:] + y2
                state = emit(r, y[:, :LANES], state)
                state = emit(r + 1, y[:, LANES:], state)
                act3 = cat([a3[b % 2, 2 * m], a3[b % 2, 2 * m + 1]], 1)
                upper = upper + dot(cat([act3, ones], 0), hi)
                lower = lower + dot(cat([act3[:M], ones], 0), lo)
            refs["acc_o1"][...] = upper
            refs["acc_o2"][...] = lower
            end(b, state)

        def after():
            send(3, g, act[0], act[H - 1], act[0], act[H - 1])
            for k in range(2 * NB):
                again(g, k)[0].start()
            if g == 0:
                for slot in range(2):
                    cotangent(slot, slot).start()

        return clear, body, after

    def back_layer(e, g, weight, own, total, slope):
        act = refs["act"][g]
        emit, begin, end, clear = emit_grad(e, g, own, total, slope)
        before, body = conv_mid(g, refs["q"][g], weight, emit, begin, end)
        return (lambda: (clear(), before())), body, lambda: send(e, g, act[0], act[H - 1], act[0], act[H - 1])

    def mid_kernel_grad(g, src, own, acc):
        def terms(rows, own_rows):
            left = cat(rows, 1)
            right = [cat(two, 1) for two in own_rows]
            hi = cat([two[:M] for two in right], 0)
            lo = cat([two[M:] for two in right], 0)
            return cat([left[:n3], left[:n3], left[n3:]], 1), cat([hi, lo, hi], 1)

        def body(b):
            ls, rs = [], []
            for m in range(RB // 2):
                r = b * RB + 2 * m
                l, rr = terms(
                    [src[r + 1], src[r + 2]], [[own[r + 2 - p], own[r + 3 - p]] for p in range(3)]
                )
                ls.append(l)
                rs.append(rr)
            acc[...] += dot(cat(ls, 1), cat(rs, 1), NT)

        def after():
            none = jnp.zeros((2 * M, LANES), bf16)
            l, rr = terms([src[0], src[H + 1]], [[own[1], none], [none, none], [none, own[H]]])
            acc[...] += dot(l, rr, NT)

        return nothing, body, after

    def first_kernel_grad(g):
        a0, q, acc = refs["a0"][g], refs["q"][g], refs["acc1"]

        def body(b):
            ls, rs = [], []
            for m in range(RB // 2):
                r = b * RB + 2 * m
                three = [cat([q[r + s], q[r + 1 + s]], 1) for s in range(3)]
                hi = cat([t[:n3] for t in three], 0)
                lo = cat([t[n3:] for t in three], 0)
                ls.append(cat([hi, hi, lo], 1))
                two = cat([a0[r], a0[r + 1]], 0)
                rs.append(cat([two[:, : sz.wide], two[:, sz.wide :], two[:, : sz.wide]], 0))
            for m in range(0, RB // 2, 2):
                acc[...] += dot(cat(ls[m : m + 2], 1), cat(rs[m : m + 2], 0))

        return nothing, body, nothing

    def reducer(name):
        base, units, shard = sz.parts[name]
        near, far, near_at, far_at, near_ids, far_ids = levels(name)
        half, quarter = units // 2, units // 2 // near
        ar, whole = refs["ar"], refs["ar_all"]
        sems = list(sz.parts).index(name)
        pair_buf = refs["pair_" + name]
        near_buf = refs["near_" + name]
        far_buf = refs["far_" + name]
        used = [0]

        def ship(src, dst, dev):
            pltpu.make_async_remote_copy(
                src_ref=src,
                dst_ref=dst,
                send_sem=refs["ar_send"].at[sems, used[0]],
                recv_sem=refs["ar_recv"].at[sems, used[0]],
                device_id=dev,
                device_id_type=MESH,
            ).start()

        def land(held):
            for sem in ("ar_recv", "ar_send"):
                pltpu.make_async_copy(held, held, refs[sem].at[sems, used[0]]).wait()
            used[0] += 1

        mine_half = base + core * half
        mine_quarter = mine_half + near_at * quarter
        mine = mine_quarter + far_at * shard

        def fill(blocks):
            at = base
            for block in blocks:
                rows = block.shape[0] // 8
                ar[at : at + rows] = block.reshape(rows, 8, LANES)
                at += rows
            if at < base + units:
                ar[at : base + units] = jnp.zeros((base + units - at, 8, LANES), f32)
            ship(ar.at[pl.ds(base + (1 - core) * half, half)], pair_buf, pair_id)

        def to_near():
            land(pair_buf)
            ar[pl.ds(mine_half, half)] += pair_buf[...]
            for d, dev in enumerate(near_ids, 1):
                to = lax.rem(near_at + d, near)
                ship(ar.at[pl.ds(mine_half + to * quarter, quarter)], near_buf.at[near - 1 - d], dev)

        def to_far():
            land(near_buf)
            got = ar[pl.ds(mine_quarter, quarter)]
            for d in range(near - 1):
                got = got + near_buf[d]
            ar[pl.ds(mine_quarter, quarter)] = got
            for d, dev in enumerate(far_ids, 1):
                to = lax.rem(far_at + d, far)
                ship(ar.at[pl.ds(mine_quarter + to * shard, shard)], far_buf.at[far - 1 - d], dev)

        def spread_far():
            land(far_buf)
            got = ar[pl.ds(mine, shard)]
            for d in range(far - 1):
                got = got + far_buf[d]
            whole[pl.ds(mine, shard)] = got
            for dev in far_ids:
                ship(whole.at[pl.ds(mine, shard)], whole.at[pl.ds(mine, shard)], dev)

        def spread_near():
            land(far_buf)
            at = pl.ds(mine_quarter, quarter)
            for dev in near_ids:
                ship(whole.at[at], whole.at[at], dev)

        def spread_pair():
            land(near_buf)
            at = pl.ds(mine_half, half)
            ship(whole.at[at], whole.at[at], pair_id)

        def done():
            land(pair_buf)
            sums = pltpu.make_async_copy(
                whole.at[pl.ds(base, units)], sums_out.at[pl.ds(base, units)], refs["sum_sem"].at[sems]
            )
            sums.start()
            return sums

        def near_only():
            land(near_buf)
            got = ar[pl.ds(mine, shard)]
            for d in range(near - 1):
                got = got + near_buf[d]
            whole[pl.ds(mine, shard)] = got
            for dev in near_ids:
                ship(whole.at[pl.ds(mine, shard)], whole.at[pl.ds(mine, shard)], dev)

        if far == 1:
            return fill, iter((to_near, near_only, spread_pair, done))
        return fill, iter((to_near, to_far, spread_far, spread_near, spread_pair, done))

    for name in ("acc2", "acc3", "acc_o1", "acc_o2", "total"):
        refs[name][...] = jnp.zeros_like(refs[name])
    none = jnp.zeros((2 * M, LANES), bf16)
    for g in range(G):
        for name in ("d2", "d3"):
            refs[name][g][0] = none
            refs[name][g][H + 1] = none

    every = range(G)
    moving, ended = {}, []

    def advance(*names):
        for name in names:
            if name not in moving:
                continue
            copy = next(moving[name])()
            if copy is not None:
                ended.append(copy)
                del moving[name]

    def reduce(name, blocks):
        fill, moving[name] = reducer(name)
        fill(blocks)

    def wide_blocks(value):
        return [value[:, h * LANES : (h + 1) * LANES] for h in range(sz.wide // LANES)]

    def mid_blocks(acc):
        value = acc[...]
        rest = value[:, LANES:]
        return [value[:, :LANES], cat([rest[: n3 // 2], rest[n3 // 2 :]], 1)]

    prepare()
    for g in every:
        for k in range(2 * NB):
            if (g, k) != (0, 0):
                in_copy(x_hbm, 0, g, k).start()
    for g in every:
        before, body, after = conv_first(g)
        if g == 0:
            run((before, body, nothing))
            pl.semaphore_wait(barrier, len(partners))
            after()
        else:
            run((before, body, after))
    for g in every:
        run(after_first(g))
        if g == 0:
            prepare_rest()
            refs["acc1"][...] = jnp.zeros_like(refs["acc1"])
    for g in every:
        run(spread(1, g, refs["p1"][g]), flat=True)
        run(second(g), flat=True)
    for g in every:
        run(spread(2, g, refs["p2"][g]), flat=True)
        run(third(g), out_layer(g))
    for g in every:
        run(spread(3, g, refs["q"][g]), mid_kernel_grad(g, refs["p2"][g], refs["d3"][g], refs["acc3"]))
        run(back_layer(4, g, t3, refs["d2"][g], refs["total"].at[1], refs["slope2"][g]), flat=True)
    for g in every:
        run(spread(4, g, refs["q"][g]), mid_kernel_grad(g, refs["p1"][g], refs["d2"][g], refs["acc2"]))
        if g == G - 1:
            upper, lower = refs["acc_o1"][...], refs["acc_o2"][...]
            outs = cat([upper[:M] + upper[M : 2 * M] + lower[:M], upper[2 * M :] + lower[M:]], 0)
            reduce("rest", wide_blocks(outs) + mid_blocks(refs["acc3"]) + mid_blocks(refs["acc2"]))
        run(back_layer(5, g, t2, None, refs["total"].at[0], refs["slope1"][g]), flat=True)
    advance("rest")
    lane = lax.broadcasted_iota(jnp.int32, (1, LANES), 1)
    sums = [jnp.sum(refs["total"][i], axis=1, keepdims=True) for i in range(3)]
    biases = jnp.where(lane == 0, sums[0], jnp.where(lane == 1, sums[1], sums[2]))
    for g in every:
        run(spread(5, g, refs["q"][g]), flat=True)
        run(first_kernel_grad(g))
        if g < G - 1:
            advance("rest")
    reduce("taps", wide_blocks(refs["acc1"]) + [biases])
    advance("rest", "taps")
    for g in every:
        run(input_grad(g))
        advance("taps", "rest")
    while moving:
        advance(*list(moving))

    for copy in ended:
        copy.wait()
    for slot in range(2):
        cotangent(slot, slot).wait()
    for g in every:
        for k in range(2 * NB):
            again(g, k)[1].wait()
    for g in every:
        for e in range(EXCHANGES - 2, EXCHANGES):
            for kind in range(2):
                landed(e, g, kind, "send")


def call_a(sz, x, dy, heights, widths, k1, k2, k3, ko, b1, b2, b3):
    G, H, W, M, N = sz.groups, sz.height, sz.width, sz.mid, LANES
    n3 = 3 * M
    names, shapes = [], []

    def add(name, *what):
        names.append((name, len(what)))
        shapes.extend(what)

    def per_group(name, shape, dtype):
        add(name, *[pltpu.VMEM(shape, dtype) for _ in range(G)])

    add("buf", pltpu.VMEM((sz.images, H, W, sz.wide), f32))
    per_group("a0", (H, N, 2 * sz.wide), bf16)
    per_group("act", (H, M, N), f32)
    per_group("carry", (2, n3, N), f32)
    for name in ("slope1", "slope2"):
        per_group(name, (H, M, N), f32)
    per_group("slope3", (H + 2, M, N), f32)
    for name in ("p1", "p2", "q"):
        per_group(name, (H + 2, 2 * n3, N), bf16)
    for name in ("d3", "d2"):
        per_group(name, (H + 2, 2 * M, N), bf16)
    add("a3", pltpu.VMEM((2, sz.block, 2 * M, N), bf16))
    add("w1", pltpu.VMEM((9 * M, 3 * sz.wide), bf16))
    for name in ("w2", "w3", "t2", "t3"):
        add(name, pltpu.VMEM((n3, 3 * n3), bf16))
    add("ko", pltpu.VMEM((2 * M, sz.wide), bf16))
    add("met", pltpu.VMEM((G, M, N), f32))
    add("bias", pltpu.VMEM((3, M, N), f32))
    E = EXCHANGES
    add("rim", pltpu.VMEM((G, 2, M, N), f32))
    add("msg", pltpu.VMEM((2, G, M, N), f32))
    add("rowmsg", pltpu.VMEM((2, G, 2, M, N), f32))
    add("cormsg", pltpu.VMEM((2, G, 2, 8, N), f32))
    add("sideway", pltpu.VMEM((2, G, 2, M, N), f32))
    add("updown", pltpu.VMEM((2, G, 2 * M + 32, N), f32))
    add("acc1", pltpu.VMEM((9 * M, sz.wide), f32))
    add("acc2", pltpu.VMEM((n3, n3), f32))
    add("acc3", pltpu.VMEM((n3, n3), f32))
    add("acc_o1", pltpu.VMEM((2 * M + 16, sz.wide), f32))
    add("acc_o2", pltpu.VMEM((M + 16, sz.wide), f32))
    add("total", pltpu.VMEM((3, M, N), f32))
    U = sz.units
    add("ar", pltpu.VMEM((U, 8, N), f32))
    add("ar_all", pltpu.VMEM((U, 8, N), f32))
    for part, (_, units, shard) in sz.parts.items():
        near = sz.cols // 2 * sz.lows[part]
        far = sz.rows // sz.lows[part]
        add("pair_" + part, pltpu.VMEM((units // 2, 8, N), f32))
        add("near_" + part, pltpu.VMEM((max(near - 1, 1), units // 2 // near, 8, N), f32))
        add("far_" + part, pltpu.VMEM((max(far - 1, 1), shard, 8, N), f32))
    add("sum_sem", pltpu.SemaphoreType.DMA((len(sz.parts),)))
    add("in_sem", pltpu.SemaphoreType.DMA((2, G, 2 * sz.blocks)))
    add("k1_sem", pltpu.SemaphoreType.DMA)
    add("again_sem", pltpu.SemaphoreType.DMA((2, G, 2 * sz.blocks)))
    add("ring_sem", pltpu.SemaphoreType.DMA((2,)))
    add("ring", pltpu.VMEM((2, sz.per_group, 4, W, sz.wide), f32))
    add("inside", pltpu.VMEM((sz.images, W, N), f32))
    add("wb", pltpu.VMEM((sz.wide, 9 * n3), bf16))
    add("out_sem", pltpu.SemaphoreType.DMA((G, sz.blocks)))
    add("send", pltpu.SemaphoreType.DMA((E, G, 2)))
    add("recv", pltpu.SemaphoreType.DMA((E, G, 2)))
    add("ar_send", pltpu.SemaphoreType.DMA((len(sz.parts), 6)))
    add("ar_recv", pltpu.SemaphoreType.DMA((len(sz.parts), 6)))
    grouped = ("a0", "act", "carry", "slope1", "slope2", "slope3", "p1", "p2", "q", "d3", "d2")

    def whole_kernel(*args):
        refs = {"io": args[:14]}
        at = 14
        for name, size in names:
            held = args[at : at + size]
            refs[name] = held if name in grouped else held[0]
            at += size
        kernel_a(sz, refs)

    hbm = pl.BlockSpec(memory_space=pl.ANY)
    vmem = pl.BlockSpec(memory_space=pltpu.VMEM)
    smem = pl.BlockSpec(memory_space=pltpu.SMEM)
    return pl.pallas_call(
        whole_kernel,
        out_shape=(
            jax.ShapeDtypeStruct(x.shape, f32),
            jax.ShapeDtypeStruct((G, H, 2 * M, N), bf16),
            jax.ShapeDtypeStruct((U, 8, N), f32),
        ),
        in_specs=[hbm, hbm, smem, smem, hbm] + [vmem] * 6,
        out_specs=(hbm, hbm, hbm),
        scratch_shapes=shapes,
        compiler_params=pltpu.CompilerParams(
            collective_id=0, has_side_effects=True, vmem_limit_bytes=63 * 2**20
        ),
        name="block_chain",
    )(x, dy, heights, widths, k1, k2, k3, ko, b1, b2, b3)


def kernel_b(
    sz, rows, x_hbm, g_hbm, a3_hbm, sums_hbm, ko_hbm, bo, out_hbm, grad_hbm, g1, g2, g3, go, s1, s2, s3, so,
    x, grad, a3, sums, ko, wo, in_sem, out_sem,
):
    G, W, M = sz.groups, sz.width, sz.mid
    n3 = 3 * M
    chunks = sz.height // rows

    def copies_in(c):
        at = (slice(None), pl.ds(c * rows, rows))
        pairs = ((a3_hbm, a3), (x_hbm, x), (g_hbm, grad))
        return [pltpu.make_async_copy(s.at[at], d.at[at], in_sem.at[i, c]) for i, (s, d) in enumerate(pairs)]

    def copies_out(c):
        at = (slice(None), pl.ds(c * rows, rows))
        return [
            pltpu.make_async_copy(grad.at[at], grad_hbm.at[at], out_sem.at[0, c]),
            pltpu.make_async_copy(x.at[at], out_hbm.at[at], out_sem.at[1, c]),
        ]

    early = pltpu.make_async_copy(ko_hbm, ko, in_sem.at[0, chunks])
    tail = pltpu.make_async_copy(sums_hbm, sums, in_sem.at[1, chunks])
    early.start()
    for c in range(chunks):
        for copy in copies_in(c):
            copy.start()
    tail.start()
    early.wait()
    hi, lo = halves(ko[...].T * GAIN)
    wo[...] = cat([hi, hi, lo], 1)
    add = bo[...] * GAIN

    def body(c, carry):
        for copy in copies_in(c):
            copy.wait()
        copies_out(c)[0].start()
        for k in range(rows):
            i = c * rows + k
            act = cat([a3[g, i] for g in range(G)], 1)
            branch = dot(wo[...], cat([act, act[:M]], 0)).T
            for n in range(sz.images):
                x[n, i] = x[n, i] + (branch[n * W : (n + 1) * W] + add)
        copies_out(c)[1].start()
        return carry

    lax.fori_loop(0, chunks, body, 0)

    tail.wait()

    def take(at, count):
        return sums[at : at + count].reshape(count * 8, LANES)

    at = sz.parts["taps"][0]
    for h in range(sz.wide // LANES):
        part = take(at, 9 * M // 8)
        at += 9 * M // 8
        for t in range(3):
            for b in range(3):
                lo = (t * 3 + b) * M
                g1[2 - t, 2 - b, :, h * LANES : (h + 1) * LANES] = part[lo : lo + M]
    rest = take(at, M // 8).T
    s1[...] = rest[0:1]
    s2[...] = rest[1:2]
    s3[...] = rest[2:3]
    at = sz.parts["rest"][0]
    for h in range(sz.wide // LANES):
        part = take(at, (M + 16) // 8)
        at += (M + 16) // 8
        go[:, h * LANES : (h + 1) * LANES] = part[:M]
        so[:, h * LANES : (h + 1) * LANES] = part[M : M + 1]
    for ref in (g3, g2):
        big, rest = take(at, n3 // 8), take(at + n3 // 8, n3 // 16)
        at += n3 // 8 + n3 // 16
        rest = cat([rest[:, :M], rest[:, M:]], 0)
        for b in range(3):
            sl = slice(b * M, (b + 1) * M)
            ref[0, b] = big[sl, :M]
            ref[1, b] = big[sl, M:]
            ref[2, b] = rest[sl]

    def finish(c, carry):
        for copy in copies_out(c):
            copy.wait()
        return carry

    lax.fori_loop(0, chunks, finish, 0)


def call_b(sz, x, grad, a3, sums, ko, bo):
    M = sz.mid
    rows = 4
    hbm = pl.BlockSpec(memory_space=pl.ANY)
    vmem = pl.BlockSpec(memory_space=pltpu.VMEM)
    shapes = ((3, 3, M, sz.wide), (3, 3, M, M), (3, 3, M, M), (M, sz.wide), (1, M), (1, M), (1, M), (1, sz.wide))
    return pl.pallas_call(
        functools.partial(kernel_b, sz, rows),
        out_shape=tuple(jax.ShapeDtypeStruct(s, f32) for s in (x.shape, x.shape) + shapes),
        in_specs=[hbm] * 5 + [vmem],
        out_specs=(hbm, hbm) + (vmem,) * 8,
        scratch_shapes=[
            pltpu.VMEM(x.shape, f32),
            pltpu.VMEM(x.shape, f32),
            pltpu.VMEM(a3.shape, bf16),
            pltpu.VMEM(sums.shape, f32),
            pltpu.VMEM(ko.shape, f32),
            pltpu.VMEM((sz.wide, 3 * M), bf16),
            pltpu.SemaphoreType.DMA((3, sz.height // rows + 1)),
            pltpu.SemaphoreType.DMA((2, sz.height // rows)),
        ],
        compiler_params=pltpu.CompilerParams(vmem_limit_bytes=60 * 2**20),
        name="wide_outputs",
    )(x, grad, a3, sums, ko, bo)


def body(rows, cols, x, k1, b1, k2, b2, k3, b3, ko, bo, dy, heights, widths):
    wide, mid = k1.shape[2:]
    sz = Sizes(x.shape, mid, rows, cols)
    k1 = jnp.swapaxes(k1, 2, 3)
    grad, a3, sums = call_a(
        sz, x, dy, heights, widths, k1.reshape(9 * mid, wide), k2, k3, ko, b1[None], b2[None], b3[None]
    )
    out, grad, g1, g2, g3, go, s1, s2, s3, so = call_b(sz, x, grad, a3, sums, ko, bo[None])
    return (
        out,
        grad,
        jnp.swapaxes(g1, 2, 3),
        s1.reshape(mid),
        g2,
        s2.reshape(mid),
        g3,
        s3.reshape(mid),
        go,
        so.reshape(wide),
    )


def solution(mesh):
    tiled = P(None, "rows", "cols", None)
    return jax.shard_map(
        functools.partial(body, mesh.shape["rows"], mesh.shape["cols"]),
        mesh=mesh,
        in_specs=(tiled,) + (P(),) * 8 + (tiled, P(), P()),
        out_specs=(tiled, tiled) + (P(),) * 8,
        check_vma=False,
    )
```

```python
import functools

import jax
import jax.numpy as jnp
from jax import lax
from jax.experimental import pallas as pl
from jax.experimental.pallas import tpu as pltpu
from jax.sharding import PartitionSpec as P

MESH = pl.DeviceIdType.MESH
bf16 = jnp.bfloat16
f32 = jnp.float32
LANES = 128
NN = (((1,), (0,)), ((), ()))
NT = (((1,), (1,)), ((), ()))
GAIN = 1.0 / 64.0
EXCHANGES = 6
GOES = ((0, 1), (0, -1), (1, 0), (-1, 0), (1, 1), (1, -1), (-1, 1), (-1, -1))


SMALL = ("k2", "k3", "ko_in", "b1", "b2", "b3")


def dot(a, b, dims=NN):
    return lax.dot_general(a, b, dims, preferred_element_type=f32)


def halves(v):
    hi = v.astype(bf16)
    return hi, (v - hi.astype(f32)).astype(bf16)


def sigmoid(v):
    return 0.5 + 0.5 * jnp.tanh(0.5 * v)


def cat(parts, axis):
    return jnp.concatenate(parts, axis=axis)


def lane_column(width):
    return lax.broadcasted_iota(jnp.int32, (1, LANES), 1) % width


class Sizes:
    def __init__(self, shape, mid, rows, cols):
        self.images, self.height, self.width, self.wide = shape
        self.mid = mid
        self.rows, self.cols = rows, cols
        self.per_group = LANES // self.width
        self.groups = self.images // self.per_group
        self.block = min(16, self.height)
        self.blocks = self.height // self.block
        self.devices = rows * cols
        self.lows = dict(taps=min(rows, max(16 // (cols // 2), 1)), rest=2)
        half = 3 * mid // 8
        self.counts = dict(
            taps=9 * mid // 8 * (self.wide // LANES) + mid // 8,
            rest=(mid + 16) // 8 * (self.wide // LANES) + 2 * (half + half // 2),
        )
        self.parts, at = {}, 0
        for name, used in self.counts.items():
            shard = -(-used // self.devices)
            self.parts[name] = (at, shard * self.devices, shard)
            at += shard * self.devices
        self.units = at


def kernel_a(sz, refs):
    x_hbm, dy_hbm, heights, widths, k1 = refs["io"][:5]
    grad_hbm, a3_hbm, sums_out = refs["io"][11:]
    k2, k3, ko_in, b1, b2, b3 = [refs[n] for n in SMALL]
    w1, w2, w3, t3, t2, ko, bias = [refs[n] for n in ("w1", "w2", "w3", "t3", "t2", "ko", "bias")]
    G, H, W, M = sz.groups, sz.height, sz.width, sz.mid
    RB, NB = sz.block, sz.blocks
    me_r, me_c = lax.axis_index("rows"), lax.axis_index("cols")
    col = lane_column(W)
    first, last = col == 0, col == W - 1
    ends = first | last
    even = col % 2 == 0
    n3 = 3 * M

    has_up, has_down = me_r > 0, me_r < sz.rows - 1
    has_left, has_right = me_c > 0, me_c < sz.cols - 1

    row_at = {d: lax.rem(me_r + d + sz.rows, sz.rows) if d else me_r for d in (-1, 0, 1)}
    col_at = {d: lax.rem(me_c + d + sz.cols, sz.cols) if d else me_c for d in (-1, 0, 1)}

    def neighbour(dr, dc):
        return row_at[dr], col_at[dc]

    buf = refs["buf"]
    half_rows = RB // 2

    def in_copy(src, which, g, k):
        n0 = g * sz.per_group
        return pltpu.make_async_copy(
            src.at[pl.ds(n0, sz.per_group), pl.ds(k * half_rows, half_rows)],
            buf.at[pl.ds(n0, sz.per_group), pl.ds(k * half_rows, half_rows)],
            refs["in_sem"].at[which, g, k],
        )

    in_copy(x_hbm, 0, 0, 0).start()

    k1_copy = pltpu.make_async_copy(k1, refs["acc1"], refs["k1_sem"])
    k1_copy.start()
    small_copies = [
        pltpu.make_async_copy(src, refs[n], refs["small_sem"].at[i])
        for i, (n, src) in enumerate(zip(SMALL, refs["io"][5:11]))
    ]
    for copy in small_copies:
        copy.start()

    def prepare():
        k1_copy.wait()
        hi, lo = halves(refs["acc1"][...])
        w1[...] = cat([hi, hi, lo], 1)
        for copy in small_copies:
            copy.wait()
        for i, b in enumerate((b1, b2, b3)):
            bias[i] = jnp.broadcast_to(b[...], (LANES, M)).T

    def prepare_rest():
        back = refs["acc1"][...].reshape(3, 3, M, sz.wide)
        for p in range(3):
            hi, lo = halves(cat([back[2 - p, 2 - b].T for b in range(3)], 1))
            refs["wb"][:, 2 * p * n3 : 2 * (p + 1) * n3] = cat([hi, hi], 1)
            refs["wb"][:, (6 + p) * n3 : (7 + p) * n3] = lo
        across = lax.broadcasted_iota(jnp.int32, (W, LANES), 0) + me_c * W
        for n in range(sz.images):
            refs["inside"][n] = jnp.where(across < widths[n], 1.0, 0.0)
        ko[:M], ko[M:] = halves(ko_in[...])
        for k, fwd, back in ((k2, w2, t2), (k3, w3, t3)):
            for p in range(3):
                at = slice(p * M, (p + 1) * M)
                hi, lo = halves(cat([k[p, q].T for q in range(3)], 1))
                fwd[at] = cat([hi, hi, lo], 1)
                hi, lo = halves(cat([k[2 - p, 2 - q] for q in range(3)], 1))
                back[at] = cat([hi, hi, lo], 1)

    core, rest = me_c % 2, me_c // 2
    pair_id = (me_r, me_c + 1 - 2 * core)

    def levels(name):
        low_count = sz.lows[name]
        near, far = sz.cols // 2 * low_count, sz.rows // low_count
        low, far_at = me_r % low_count, me_r // low_count
        near_at = rest * low_count + low
        near_ids = []
        for d in range(1, near):
            k = lax.rem(near_at + d, near)
            near_ids.append((far_at * low_count + k % low_count, (k // low_count) * 2 + core))
        far_ids = [(lax.rem(far_at + d, far) * low_count + low, me_c) for d in range(1, far)]
        return near, far, near_at, far_at, near_ids, far_ids

    barrier = pltpu.get_barrier_semaphore()
    partners = [pair_id] + [neighbour(dr, dc) for dr, dc in GOES]
    for name in ("taps", "rest"):
        near_ids, far_ids = levels(name)[4:]
        partners += near_ids + far_ids
    for dev in partners:
        pl.semaphore_signal(barrier, inc=1, device_id=dev, device_id_type=MESH)

    def message(e, g, slot):
        dr, dc = GOES[slot]
        at = (e % 2, g)
        if slot < 2:
            src, dst = refs["msg"].at[at], refs["sideway"].at[(*at, slot)]
        elif slot < 4:
            src = refs["rowmsg"].at[(*at, 3 - slot)]
            dst = refs["updown"].at[(*at, pl.ds((slot - 2) * M, M))]
        else:
            src = refs["cormsg"].at[(*at, 1 if dr > 0 else 0)]
            dst = refs["updown"].at[(*at, pl.ds(2 * M + 8 * (slot - 4), 8))]
        kind = 0 if slot < 2 else 1
        return pltpu.make_async_remote_copy(
            src_ref=src,
            dst_ref=dst,
            send_sem=refs["send"].at[e, g, kind],
            recv_sem=refs["recv"].at[e, g, kind],
            device_id=neighbour(dr, dc),
            device_id_type=MESH,
        )

    def landed(e, g, kind, sem):
        held = refs["updown" if kind else "sideway"].at[e % 2, g]
        pltpu.make_async_copy(held, held, refs[sem].at[e, g, kind]).wait()

    def send(e, g, top, bottom, top_rim, bottom_rim):
        for slot in (0, 1):
            message(e, g, slot).start()
        refs["rowmsg"][e % 2, g, 0] = top
        refs["rowmsg"][e % 2, g, 1] = bottom
        for slot in (2, 3):
            message(e, g, slot).start()
        refs["cormsg"][e % 2, g, 0] = pack_corner(top_rim)
        refs["cormsg"][e % 2, g, 1] = pack_corner(bottom_rim)
        for slot in (4, 5, 6, 7):
            message(e, g, slot).start()

    def reuse(e, g):
        if e >= 2:
            for kind in range(2):
                landed(e - 2, g, kind, "send")

    def receive(e, g, kind):
        landed(e, g, kind, "recv")

    def pack(held, value, u):
        moved = pltpu.roll(value, lax.rem(LANES + 1 + 2 * u, LANES), 1)
        return jnp.where(col // 2 == u, moved, held)

    def pack_corner(value):
        held = jnp.zeros((8, LANES), f32)
        for k in range(M // 8):
            held = jnp.where(col // 2 == k, pltpu.roll(value[8 * k : 8 * k + 8], 1 + 2 * k, 1), held)
        return held

    def beyond(e, g, lower):
        row = refs["updown"][e % 2, g, pl.ds(M if lower else 0, M)]
        at = 2 if lower else 0
        there = has_down if lower else has_up
        left = jnp.where(there & has_left, corner_left(refs["updown"][e % 2, g, pl.ds(2 * M + 8 * at, 8)]), 0.0)
        right = jnp.where(there & has_right, corner_right(refs["updown"][e % 2, g, pl.ds(2 * M + 8 * (at + 1), 8)]), 0.0)
        return jnp.where(there, row, 0.0), jnp.where(first, left, right)

    def meet(e, g):
        left = jnp.where(has_left, refs["sideway"][e % 2, g, 0], 0.0)
        right = jnp.where(has_right, refs["sideway"][e % 2, g, 1], 0.0)
        refs["met"][g] = jnp.where(even, left, pltpu.roll(right, (2 * W - 2) % LANES, 1))

    def from_sides(held, u):
        return pltpu.roll(held, LANES - W - 2 * u, 1)

    def corner_left(held):
        return cat([pltpu.roll(held, LANES - W - 2 * k, 1) for k in range(M // 8)], 0)

    def corner_right(held):
        return cat([pltpu.roll(held, W - 2 - 2 * k, 1) for k in range(M // 8)], 0)

    def nothing():
        pass

    def run(*phases, steps=NB, flat=False):
        for before, _, _ in phases:
            before()

        def step(b, carry):
            for _, body, _ in phases:
                body(b)
            return carry

        if flat:
            for b in range(steps):
                step(b, 0)
        else:
            lax.fori_loop(0, steps, step, 0)
        for _, _, after in phases:
            after()

    def conv_first(g):
        a0, z, carry = refs["a0"][g], refs["slope3"][g], refs["carry"][g]

        def before():
            carry[...] = jnp.zeros_like(carry)
            refs["msg"][0, g] = jnp.zeros((M, LANES), f32)

        def emit(row, s, held):
            s0, s1, s2 = s[:M], s[M : 2 * M], s[2 * M :]
            value = s1 + jnp.where(first, 0.0, pltpu.roll(s0, 1, 1))
            value = value + jnp.where(last, 0.0, pltpu.roll(s2, LANES - 1, 1))
            z[row + 1] = value
            rim = jnp.where(first, s2, s0)
            return rim, pack(held, rim, row)

        def body(b):
            held = refs["msg"][0, g]
            c0, c1 = carry[0], carry[1]
            for m in range(RB // 2):
                r = b * RB + 2 * m
                if 2 * m % half_rows == 0:
                    in_copy(x_hbm, 0, g, 2 * b + 2 * m // half_rows).wait()
                pair = []
                for i in range(2):
                    v = cat([buf[g * sz.per_group + s, r + i] for s in range(sz.per_group)], 0)
                    hi, lo = halves(v * sigmoid(v))
                    both = cat([hi, lo], 1)
                    a0[r + i] = both
                    pair.append(both)
                rhs = cat(pair, 0)
                y = dot(w1[...], cat([rhs, rhs[:, : sz.wide]], 1), NT)
                ya, yb = y[:, :LANES], y[:, LANES:]
                rim, held = emit(r - 1, c0 + ya[2 * n3 :], held)
                if m == 0:
                    refs["rim"][g, jnp.minimum(b, 1)] = rim
                _, held = emit(r, c1 + ya[n3 : 2 * n3] + yb[2 * n3 :], held)
                c0, c1 = ya[:n3] + yb[n3 : 2 * n3], yb[:n3]
            carry[0] = c0
            carry[1] = c1
            refs["msg"][0, g] = held

        def after():
            _, held = emit(H - 1, carry[0], refs["msg"][0, g])
            rim, _ = emit(H, carry[1], held)
            refs["msg"][0, g] = held
            for k in range(2 * NB):
                in_copy(dy_hbm, 1, g, k).start()
            send(0, g, z[0], z[H + 1], refs["rim"][g, 0], rim)

        return before, body, after

    def after_first(g):
        z, act, slope = refs["slope3"][g], refs["act"][g], refs["slope1"][g]
        def before():
            receive(0, g, 0)
            meet(0, g)
            refs["msg"][1, g] = jnp.zeros((M, LANES), f32)

        def emit(r, v, held):
            v = v + bias[0]
            sig = sigmoid(v)
            a = v * sig
            slope[r] = sig + a * (1.0 - sig)
            act[r] = a
            return pack(held, a, r)

        def with_sides(r):
            return z[r + 1] + jnp.where(ends, from_sides(refs["met"][g], r), 0.0)

        def body(b):
            held = refs["msg"][1, g]
            for k in range(RB):
                r = b * RB + k
                held = emit(r, with_sides(r), held)
            refs["msg"][1, g] = held

        def after():
            receive(0, g, 1)
            held = refs["msg"][1, g]
            for r, lower in ((0, False), (H - 1, True)):
                row, sides = beyond(0, g, lower)
                held = emit(r, with_sides(r) + row + jnp.where(ends, sides, 0.0), held)
            refs["msg"][1, g] = held
            send(1, g, act[0], act[H - 1], act[0], act[H - 1])

        return before, body, after

    def spread(e, g, dst):
        act = refs["act"][g]

        def before():
            receive(e, g, 0)
            meet(e, g)

        def store(row, v, left, right):
            before = jnp.where(first, left, pltpu.roll(v, 1, 1))
            behind = jnp.where(last, right, pltpu.roll(v, LANES - 1, 1))
            for at, part in enumerate((before, v, behind)):
                hi, lo = halves(part)
                dst[row, at * M : (at + 1) * M] = hi
                dst[row, n3 + at * M : n3 + (at + 1) * M] = lo

        def body(b):
            both = refs["met"][g]
            for k in range(RB):
                r = b * RB + k
                sides = from_sides(both, r)
                store(r + 1, act[r], sides, sides)

        def after():
            receive(e, g, 1)
            for at, lower in ((0, False), (H + 1, True)):
                row, sides = beyond(e, g, lower)
                store(at, row, sides, sides)

        return before, body, after

    def conv_mid(g, src, weight, emit, begin, end):
        carry = refs["carry"][g]

        def pair(m):
            rhs = cat([src[2 * m], src[2 * m + 1]], 1)
            y = dot(weight[...], cat([rhs, rhs[:n3]], 0))
            return y[:, :LANES], y[:, LANES:]

        def before():
            ya, yb = pair(0)
            carry[0, :M] = ya[:M] + yb[M : 2 * M]
            carry[1, :M] = yb[:M]

        def body(b):
            state = begin(b)
            c0, c1 = carry[0, :M], carry[1, :M]
            for k in range(RB // 2):
                ya, yb = pair(1 + b * (RB // 2) + k)
                r = b * RB + 2 * k
                state = emit(r, c0 + ya[2 * M :], state)
                state = emit(r + 1, c1 + ya[M : 2 * M] + yb[2 * M :], state)
                c0, c1 = ya[:M] + yb[M : 2 * M], yb[:M]
            carry[0, :M] = c0
            carry[1, :M] = c1
            end(b, state)

        return before, body

    def second(g):
        act, slope = refs["act"][g], refs["slope2"][g]

        def clear():
            reuse(2, g)
            refs["msg"][0, g] = jnp.zeros((M, LANES), f32)

        def emit(r, v, held):
            v = v + bias[1]
            sig = sigmoid(v)
            a = v * sig
            slope[r] = sig + a * (1.0 - sig)
            act[r] = a
            return pack(held, a, r)

        def end(b, held):
            refs["msg"][0, g] = held

        before, body = conv_mid(g, refs["p1"][g], w2, emit, lambda b: refs["msg"][0, g], end)
        return (lambda: (clear(), before())), body, lambda: send(2, g, act[0], act[H - 1], act[0], act[H - 1])

    def a3_copy(g, b):
        return pltpu.make_async_copy(
            refs["a3"].at[b % 2], a3_hbm.at[g, pl.ds(b * RB, RB)], refs["out_sem"].at[g, b]
        )

    def third(g):
        a3, slope = refs["a3"], refs["slope3"][g]

        def emit(r, v, state):
            v = v + bias[2]
            sig = sigmoid(v)
            a = v * sig
            slope[r] = sig + a * (1.0 - sig)
            hi, lo = halves(a)
            k = r - state * RB
            a3[state % 2, k, :M] = hi
            a3[state % 2, k, M:] = lo
            return state

        def begin(b):
            if NB > 2:

                @pl.when(b >= 2)
                def _():
                    a3_copy(g, b - 2).wait()

            return b

        before, body = conv_mid(g, refs["p2"][g], w3, emit, begin, lambda b, s: a3_copy(g, b).start())

        def after():
            for k in range(max(NB - 2, 0), NB):
                a3_copy(g, k).wait()

        return before, body, after

    ring_rows = half_rows // 2
    ring_count = H // ring_rows

    def again(g, k):
        at = (pl.ds(g * sz.per_group, sz.per_group), pl.ds(k * half_rows, half_rows))
        return (
            pltpu.make_async_copy(x_hbm.at[at], buf.at[at], refs["again_sem"].at[0, g, k]),
            pltpu.make_async_copy(buf.at[at], grad_hbm.at[at], refs["again_sem"].at[1, g, k]),
        )

    def cotangent(t, slot):
        t = lax.rem(t, G * ring_count)
        at = (
            pl.ds(t // ring_count * sz.per_group, sz.per_group),
            pl.ds(lax.rem(t, ring_count) * ring_rows, ring_rows),
        )
        return pltpu.make_async_copy(dy_hbm.at[at], refs["ring"].at[slot], refs["ring_sem"].at[slot])

    def masked(value, s, n, r):
        keep = refs["inside"][n] * jnp.where(me_r * H + r < heights[n], 1.0, 0.0)
        return value * cat([keep] * (sz.wide // LANES), 1)

    def input_grad(g):
        q, wb = refs["q"][g], refs["wb"]

        def body(b):
            again(g, b)[0].wait()
            for m in range(half_rows // 2):
                r = b * half_rows + 2 * m
                t = g * ring_count + 2 * b + 2 * m // ring_rows
                slot, at_row = 2 * m // ring_rows, 2 * m % ring_rows
                if at_row == 0:
                    cotangent(t, slot).wait()
                dy = refs["ring"].at[slot]
                three = [cat([q[r + s], q[r + 1 + s]], 1) for s in range(3)]
                y = dot(wb[...], cat(three + [t3[:n3] for t3 in three], 0)).T
                for i in range(2):
                    for s in range(sz.per_group):
                        n = g * sz.per_group + s
                        at = i * LANES + s * W
                        v = buf[n, r + i]
                        sig = sigmoid(v)
                        slope = sig * (1.0 + v * (1.0 - sig))
                        buf[n, r + i] = masked(dy[s, at_row + i], s, n, r + i) + y[at : at + W] * slope
                if at_row == ring_rows - 2:
                    cotangent(t + 2, slot).start()
            again(g, b)[1].start()

        return nothing, body, nothing

    def emit_grad(e, g, own, total, slope):
        act = refs["act"][g]

        def emit(r, v, state):
            held, summed = state
            d = v * slope[r]
            act[r] = d
            if own is not None:
                hi, lo = halves(d)
                own[r + 1, :M] = hi
                own[r + 1, M:] = lo
            return pack(held, d, r), summed + d

        def begin(b):
            return refs["msg"][e % 2, g], total[...]

        def end(b, state):
            refs["msg"][e % 2, g] = state[0]
            total[...] = state[1]

        def clear():
            reuse(e, g)
            refs["msg"][e % 2, g] = jnp.zeros((M, LANES), f32)

        return emit, begin, end, clear

    def out_layer(g):
        a3, act = refs["a3"], refs["act"][g]
        emit, begin, end, clear = emit_grad(3, g, refs["d3"][g], refs["total"].at[2], refs["slope3"][g])
        ones = jnp.ones((16, 2 * LANES), bf16)

        def body(b):
            for h in range(2):
                in_copy(dy_hbm, 1, g, 2 * b + h).wait()
            state = begin(b)
            upper, lower = refs["acc_o1"][...], refs["acc_o2"][...]
            for m in range(RB // 2):
                r = b * RB + 2 * m
                parts = []
                for i in range(2):
                    for s in range(sz.per_group):
                        n = g * sz.per_group + s
                        parts.append(masked(buf[n, r + i], s, n, r + i) * GAIN)
                hi, lo = halves(cat(parts, 0))
                y1 = dot(ko[...], hi, NT)
                y2 = dot(ko[:M], lo, NT)
                y = y1[:M] + y1[M:] + y2
                state = emit(r, y[:, :LANES], state)
                state = emit(r + 1, y[:, LANES:], state)
                act3 = cat([a3[b % 2, 2 * m], a3[b % 2, 2 * m + 1]], 1)
                upper = upper + dot(cat([act3, ones], 0), hi)
                lower = lower + dot(cat([act3[:M], ones], 0), lo)
            refs["acc_o1"][...] = upper
            refs["acc_o2"][...] = lower
            end(b, state)

        def after():
            send(3, g, act[0], act[H - 1], act[0], act[H - 1])
            for k in range(2 * NB):
                again(g, k)[0].start()
            if g == 0:
                for slot in range(2):
                    cotangent(slot, slot).start()

        return clear, body, after

    def back_layer(e, g, weight, own, total, slope):
        act = refs["act"][g]
        emit, begin, end, clear = emit_grad(e, g, own, total, slope)
        before, body = conv_mid(g, refs["q"][g], weight, emit, begin, end)
        return (lambda: (clear(), before())), body, lambda: send(e, g, act[0], act[H - 1], act[0], act[H - 1])

    def mid_kernel_grad(g, src, own, acc):
        def terms(rows, own_rows):
            left = cat(rows, 1)
            right = [cat(two, 1) for two in own_rows]
            hi = cat([two[:M] for two in right], 0)
            lo = cat([two[M:] for two in right], 0)
            return cat([left[:n3], left[:n3], left[n3:]], 1), cat([hi, lo, hi], 1)

        def body(b):
            ls, rs = [], []
            for m in range(RB // 2):
                r = b * RB + 2 * m
                l, rr = terms(
                    [src[r + 1], src[r + 2]], [[own[r + 2 - p], own[r + 3 - p]] for p in range(3)]
                )
                ls.append(l)
                rs.append(rr)
            acc[...] += dot(cat(ls, 1), cat(rs, 1), NT)

        def after():
            none = jnp.zeros((2 * M, LANES), bf16)
            l, rr = terms([src[0], src[H + 1]], [[own[1], none], [none, none], [none, own[H]]])
            acc[...] += dot(l, rr, NT)

        return nothing, body, after

    def first_kernel_grad(g):
        a0, q, acc = refs["a0"][g], refs["q"][g], refs["acc1"]

        def body(b):
            ls, rs = [], []
            for m in range(RB // 2):
                r = b * RB + 2 * m
                three = [cat([q[r + s], q[r + 1 + s]], 1) for s in range(3)]
                hi = cat([t[:n3] for t in three], 0)
                lo = cat([t[n3:] for t in three], 0)
                ls.append(cat([hi, hi, lo], 1))
                two = cat([a0[r], a0[r + 1]], 0)
                rs.append(cat([two[:, : sz.wide], two[:, sz.wide :], two[:, : sz.wide]], 0))
            for m in range(0, RB // 2, 2):
                acc[...] += dot(cat(ls[m : m + 2], 1), cat(rs[m : m + 2], 0))

        return nothing, body, nothing

    def reducer(name):
        base, units, shard = sz.parts[name]
        near, far, near_at, far_at, near_ids, far_ids = levels(name)
        half, quarter = units // 2, units // 2 // near
        ar, whole = refs["ar"], refs["ar_all"]
        sems = list(sz.parts).index(name)
        pair_buf = refs["pair_" + name]
        near_buf = refs["near_" + name]
        far_buf = refs["far_" + name]
        used = [0]

        def ship(src, dst, dev):
            pltpu.make_async_remote_copy(
                src_ref=src,
                dst_ref=dst,
                send_sem=refs["ar_send"].at[sems, used[0]],
                recv_sem=refs["ar_recv"].at[sems, used[0]],
                device_id=dev,
                device_id_type=MESH,
            ).start()

        def land(held):
            for sem in ("ar_recv", "ar_send"):
                pltpu.make_async_copy(held, held, refs[sem].at[sems, used[0]]).wait()
            used[0] += 1

        mine_half = base + core * half
        mine_quarter = mine_half + near_at * quarter
        mine = mine_quarter + far_at * shard

        def fill(blocks):
            at = base
            for block in blocks:
                rows = block.shape[0] // 8
                ar[at : at + rows] = block.reshape(rows, 8, LANES)
                at += rows
            if at < base + units:
                ar[at : base + units] = jnp.zeros((base + units - at, 8, LANES), f32)
            ship(ar.at[pl.ds(base + (1 - core) * half, half)], pair_buf, pair_id)

        def to_near():
            land(pair_buf)
            ar[pl.ds(mine_half, half)] += pair_buf[...]
            for d, dev in enumerate(near_ids, 1):
                to = lax.rem(near_at + d, near)
                ship(ar.at[pl.ds(mine_half + to * quarter, quarter)], near_buf.at[near - 1 - d], dev)

        def to_far():
            land(near_buf)
            got = ar[pl.ds(mine_quarter, quarter)]
            for d in range(near - 1):
                got = got + near_buf[d]
            ar[pl.ds(mine_quarter, quarter)] = got
            for d, dev in enumerate(far_ids, 1):
                to = lax.rem(far_at + d, far)
                ship(ar.at[pl.ds(mine_quarter + to * shard, shard)], far_buf.at[far - 1 - d], dev)

        def spread_far():
            land(far_buf)
            got = ar[pl.ds(mine, shard)]
            for d in range(far - 1):
                got = got + far_buf[d]
            whole[pl.ds(mine, shard)] = got
            for dev in far_ids:
                ship(whole.at[pl.ds(mine, shard)], whole.at[pl.ds(mine, shard)], dev)

        def spread_near():
            land(far_buf)
            at = pl.ds(mine_quarter, quarter)
            for dev in near_ids:
                ship(whole.at[at], whole.at[at], dev)

        def spread_pair():
            land(near_buf)
            at = pl.ds(mine_half, half)
            ship(whole.at[at], whole.at[at], pair_id)

        def done():
            land(pair_buf)
            sums = pltpu.make_async_copy(
                whole.at[pl.ds(base, units)], sums_out.at[pl.ds(base, units)], refs["sum_sem"].at[sems]
            )
            sums.start()
            return sums

        def near_only():
            land(near_buf)
            got = ar[pl.ds(mine, shard)]
            for d in range(near - 1):
                got = got + near_buf[d]
            whole[pl.ds(mine, shard)] = got
            for dev in near_ids:
                ship(whole.at[pl.ds(mine, shard)], whole.at[pl.ds(mine, shard)], dev)

        if far == 1:
            return fill, iter((to_near, near_only, spread_pair, done))
        return fill, iter((to_near, to_far, spread_far, spread_near, spread_pair, done))

    for name in ("acc2", "acc3", "acc_o1", "acc_o2", "total"):
        refs[name][...] = jnp.zeros_like(refs[name])
    none = jnp.zeros((2 * M, LANES), bf16)
    for g in range(G):
        for name in ("d2", "d3"):
            refs[name][g][0] = none
            refs[name][g][H + 1] = none

    every = range(G)
    moving, ended = {}, []

    def advance(*names):
        for name in names:
            if name not in moving:
                continue
            copy = next(moving[name])()
            if copy is not None:
                ended.append(copy)
                del moving[name]

    def reduce(name, blocks):
        fill, moving[name] = reducer(name)
        fill(blocks)

    def wide_blocks(value):
        return [value[:, h * LANES : (h + 1) * LANES] for h in range(sz.wide // LANES)]

    def mid_blocks(acc):
        value = acc[...]
        rest = value[:, LANES:]
        return [value[:, :LANES], cat([rest[: n3 // 2], rest[n3 // 2 :]], 1)]

    prepare()
    for g in every:
        for k in range(2 * NB):
            if (g, k) != (0, 0):
                in_copy(x_hbm, 0, g, k).start()
    for g in every:
        before, body, after = conv_first(g)
        if g == 0:
            run((before, body, nothing))
            pl.semaphore_wait(barrier, len(partners))
            after()
        else:
            run((before, body, after))
    for g in every:
        run(after_first(g))
        if g == 0:
            prepare_rest()
            refs["acc1"][...] = jnp.zeros_like(refs["acc1"])
    for g in every:
        run(spread(1, g, refs["p1"][g]))
        run(second(g), flat=True)
    for g in every:
        run(spread(2, g, refs["p2"][g]))
        run(third(g), out_layer(g))
    for g in every:
        run(spread(3, g, refs["q"][g]), mid_kernel_grad(g, refs["p2"][g], refs["d3"][g], refs["acc3"]))
        run(back_layer(4, g, t3, refs["d2"][g], refs["total"].at[1], refs["slope2"][g]), flat=True)
    for g in every:
        run(spread(4, g, refs["q"][g]), mid_kernel_grad(g, refs["p1"][g], refs["d2"][g], refs["acc2"]))
        if g == G - 1:
            upper, lower = refs["acc_o1"][...], refs["acc_o2"][...]
            outs = cat([upper[:M] + upper[M : 2 * M] + lower[:M], upper[2 * M :] + lower[M:]], 0)
            reduce("rest", wide_blocks(outs) + mid_blocks(refs["acc3"]) + mid_blocks(refs["acc2"]))
        run(back_layer(5, g, t2, None, refs["total"].at[0], refs["slope1"][g]), flat=True)
    advance("rest")
    lane = lax.broadcasted_iota(jnp.int32, (1, LANES), 1)
    sums = [jnp.sum(refs["total"][i], axis=1, keepdims=True) for i in range(3)]
    biases = jnp.where(lane == 0, sums[0], jnp.where(lane == 1, sums[1], sums[2]))
    for g in every:
        run(spread(5, g, refs["q"][g]), flat=True)
        run(first_kernel_grad(g))
        if g < G - 1:
            advance("rest")
    reduce("taps", wide_blocks(refs["acc1"]) + [biases])
    advance("rest", "taps")
    for g in every:
        run(input_grad(g), steps=2 * NB)
        advance("taps", "rest")
    while moving:
        advance(*list(moving))

    for copy in ended:
        copy.wait()
    for slot in range(2):
        cotangent(slot, slot).wait()
    for g in every:
        for k in range(2 * NB):
            again(g, k)[1].wait()
    for g in every:
        for e in range(EXCHANGES - 2, EXCHANGES):
            for kind in range(2):
                landed(e, g, kind, "send")


def call_a(sz, x, dy, heights, widths, k1, k2, k3, ko, b1, b2, b3):
    G, H, W, M, N = sz.groups, sz.height, sz.width, sz.mid, LANES
    n3 = 3 * M
    names, shapes = [], []

    def add(name, *what):
        names.append((name, len(what)))
        shapes.extend(what)

    def per_group(name, shape, dtype):
        add(name, *[pltpu.VMEM(shape, dtype) for _ in range(G)])

    add("buf", pltpu.VMEM((sz.images, H, W, sz.wide), f32))
    per_group("a0", (H, N, 2 * sz.wide), bf16)
    per_group("act", (H, M, N), f32)
    per_group("carry", (2, n3, N), f32)
    for name in ("slope1", "slope2"):
        per_group(name, (H, M, N), f32)
    per_group("slope3", (H + 2, M, N), f32)
    for name in ("p1", "p2", "q"):
        per_group(name, (H + 2, 2 * n3, N), bf16)
    for name in ("d3", "d2"):
        per_group(name, (H + 2, 2 * M, N), bf16)
    add("a3", pltpu.VMEM((2, sz.block, 2 * M, N), bf16))
    add("w1", pltpu.VMEM((9 * M, 3 * sz.wide), bf16))
    for name in ("w2", "w3", "t2", "t3"):
        add(name, pltpu.VMEM((n3, 3 * n3), bf16))
    add("ko", pltpu.VMEM((2 * M, sz.wide), bf16))
    add("met", pltpu.VMEM((G, M, N), f32))
    add("bias", pltpu.VMEM((3, M, N), f32))
    E = EXCHANGES
    add("rim", pltpu.VMEM((G, 2, M, N), f32))
    add("msg", pltpu.VMEM((2, G, M, N), f32))
    add("rowmsg", pltpu.VMEM((2, G, 2, M, N), f32))
    add("cormsg", pltpu.VMEM((2, G, 2, 8, N), f32))
    add("sideway", pltpu.VMEM((2, G, 2, M, N), f32))
    add("updown", pltpu.VMEM((2, G, 2 * M + 32, N), f32))
    add("acc1", pltpu.VMEM((9 * M, sz.wide), f32))
    add("acc2", pltpu.VMEM((n3, n3), f32))
    add("acc3", pltpu.VMEM((n3, n3), f32))
    add("acc_o1", pltpu.VMEM((2 * M + 16, sz.wide), f32))
    add("acc_o2", pltpu.VMEM((M + 16, sz.wide), f32))
    add("total", pltpu.VMEM((3, M, N), f32))
    U = sz.units
    add("ar", pltpu.VMEM((U, 8, N), f32))
    add("ar_all", pltpu.VMEM((U, 8, N), f32))
    for part, (_, units, shard) in sz.parts.items():
        near = sz.cols // 2 * sz.lows[part]
        far = sz.rows // sz.lows[part]
        add("pair_" + part, pltpu.VMEM((units // 2, 8, N), f32))
        add("near_" + part, pltpu.VMEM((max(near - 1, 1), units // 2 // near, 8, N), f32))
        add("far_" + part, pltpu.VMEM((max(far - 1, 1), shard, 8, N), f32))
    add("sum_sem", pltpu.SemaphoreType.DMA((len(sz.parts),)))
    add("in_sem", pltpu.SemaphoreType.DMA((2, G, 2 * sz.blocks)))
    add("k1_sem", pltpu.SemaphoreType.DMA)
    for name, value in zip(SMALL, (k2, k3, ko, b1, b2, b3)):
        add(name, pltpu.VMEM(value.shape, f32))
    add("small_sem", pltpu.SemaphoreType.DMA((len(SMALL),)))
    add("again_sem", pltpu.SemaphoreType.DMA((2, G, 2 * sz.blocks)))
    add("ring_sem", pltpu.SemaphoreType.DMA((2,)))
    add("ring", pltpu.VMEM((2, sz.per_group, sz.block // 4, W, sz.wide), f32))
    add("inside", pltpu.VMEM((sz.images, W, N), f32))
    add("wb", pltpu.VMEM((sz.wide, 9 * n3), bf16))
    add("out_sem", pltpu.SemaphoreType.DMA((G, sz.blocks)))
    add("send", pltpu.SemaphoreType.DMA((E, G, 2)))
    add("recv", pltpu.SemaphoreType.DMA((E, G, 2)))
    add("ar_send", pltpu.SemaphoreType.DMA((len(sz.parts), 6)))
    add("ar_recv", pltpu.SemaphoreType.DMA((len(sz.parts), 6)))
    grouped = ("a0", "act", "carry", "slope1", "slope2", "slope3", "p1", "p2", "q", "d3", "d2")

    def whole_kernel(*args):
        refs = {"io": args[:14]}
        at = 14
        for name, size in names:
            held = args[at : at + size]
            refs[name] = held if name in grouped else held[0]
            at += size
        kernel_a(sz, refs)

    hbm = pl.BlockSpec(memory_space=pl.ANY)
    vmem = pl.BlockSpec(memory_space=pltpu.VMEM)
    smem = pl.BlockSpec(memory_space=pltpu.SMEM)
    return pl.pallas_call(
        whole_kernel,
        out_shape=(
            jax.ShapeDtypeStruct(x.shape, f32),
            jax.ShapeDtypeStruct((G, H, 2 * M, N), bf16),
            jax.ShapeDtypeStruct((U, 8, N), f32),
        ),
        in_specs=[hbm, hbm, smem, smem] + [hbm] * 7,
        out_specs=(hbm, hbm, hbm),
        scratch_shapes=shapes,
        compiler_params=pltpu.CompilerParams(
            collective_id=0, has_side_effects=True, vmem_limit_bytes=63 * 2**20
        ),
        name="block_chain",
    )(x, dy, heights, widths, k1, k2, k3, ko, b1, b2, b3)


def kernel_b(
    sz, rows, x_hbm, g_hbm, a3_hbm, sums_hbm, ko_hbm, bo, out_hbm, grad_hbm, g1, g2, g3, go, s1, s2, s3, so,
    x, grad, a3, sums, ko, wo, in_sem, out_sem,
):
    G, W, M = sz.groups, sz.width, sz.mid
    n3 = 3 * M
    chunks = sz.height // rows

    def copies_in(c):
        at = (slice(None), pl.ds(c * rows, rows))
        pairs = ((a3_hbm, a3), (x_hbm, x), (g_hbm, grad))
        return [pltpu.make_async_copy(s.at[at], d.at[at], in_sem.at[i, c]) for i, (s, d) in enumerate(pairs)]

    def copies_out(c):
        at = (slice(None), pl.ds(c * rows, rows))
        return [
            pltpu.make_async_copy(grad.at[at], grad_hbm.at[at], out_sem.at[0, c]),
            pltpu.make_async_copy(x.at[at], out_hbm.at[at], out_sem.at[1, c]),
        ]

    early = pltpu.make_async_copy(ko_hbm, ko, in_sem.at[0, chunks])
    tail = pltpu.make_async_copy(sums_hbm, sums, in_sem.at[1, chunks])
    early.start()
    for c in range(chunks):
        for copy in copies_in(c):
            copy.start()
    tail.start()
    early.wait()
    hi, lo = halves(ko[...].T * GAIN)
    wo[...] = cat([hi, hi, lo], 1)
    add = bo[...] * GAIN

    def body(c, carry):
        for copy in copies_in(c):
            copy.wait()
        copies_out(c)[0].start()
        for k in range(rows):
            i = c * rows + k
            act = cat([a3[g, i] for g in range(G)], 1)
            branch = dot(wo[...], cat([act, act[:M]], 0)).T
            for n in range(sz.images):
                x[n, i] = x[n, i] + (branch[n * W : (n + 1) * W] + add)
        copies_out(c)[1].start()
        return carry

    lax.fori_loop(0, chunks, body, 0)

    tail.wait()

    def take(at, count):
        return sums[at : at + count].reshape(count * 8, LANES)

    at = sz.parts["taps"][0]
    for h in range(sz.wide // LANES):
        part = take(at, 9 * M // 8)
        at += 9 * M // 8
        for t in range(3):
            for b in range(3):
                lo = (t * 3 + b) * M
                g1[2 - t, 2 - b, :, h * LANES : (h + 1) * LANES] = part[lo : lo + M]
    rest = take(at, M // 8).T
    s1[...] = rest[0:1]
    s2[...] = rest[1:2]
    s3[...] = rest[2:3]
    at = sz.parts["rest"][0]
    for h in range(sz.wide // LANES):
        part = take(at, (M + 16) // 8)
        at += (M + 16) // 8
        go[:, h * LANES : (h + 1) * LANES] = part[:M]
        so[:, h * LANES : (h + 1) * LANES] = part[M : M + 1]
    for ref in (g3, g2):
        big, rest = take(at, n3 // 8), take(at + n3 // 8, n3 // 16)
        at += n3 // 8 + n3 // 16
        rest = cat([rest[:, :M], rest[:, M:]], 0)
        for b in range(3):
            sl = slice(b * M, (b + 1) * M)
            ref[0, b] = big[sl, :M]
            ref[1, b] = big[sl, M:]
            ref[2, b] = rest[sl]

    def finish(c, carry):
        for copy in copies_out(c):
            copy.wait()
        return carry

    lax.fori_loop(0, chunks, finish, 0)


def call_b(sz, x, grad, a3, sums, ko, bo):
    M = sz.mid
    rows = 8
    hbm = pl.BlockSpec(memory_space=pl.ANY)
    vmem = pl.BlockSpec(memory_space=pltpu.VMEM)
    shapes = ((3, 3, M, sz.wide), (3, 3, M, M), (3, 3, M, M), (M, sz.wide), (1, M), (1, M), (1, M), (1, sz.wide))
    return pl.pallas_call(
        functools.partial(kernel_b, sz, rows),
        out_shape=tuple(jax.ShapeDtypeStruct(s, f32) for s in (x.shape, x.shape) + shapes),
        in_specs=[hbm] * 5 + [vmem],
        out_specs=(hbm, hbm) + (vmem,) * 8,
        scratch_shapes=[
            pltpu.VMEM(x.shape, f32),
            pltpu.VMEM(x.shape, f32),
            pltpu.VMEM(a3.shape, bf16),
            pltpu.VMEM(sums.shape, f32),
            pltpu.VMEM(ko.shape, f32),
            pltpu.VMEM((sz.wide, 3 * M), bf16),
            pltpu.SemaphoreType.DMA((3, sz.height // rows + 1)),
            pltpu.SemaphoreType.DMA((2, sz.height // rows)),
        ],
        compiler_params=pltpu.CompilerParams(vmem_limit_bytes=60 * 2**20),
        name="wide_outputs",
    )(x, grad, a3, sums, ko, bo)


def body(rows, cols, x, k1, b1, k2, b2, k3, b3, ko, bo, dy, heights, widths):
    wide, mid = k1.shape[2:]
    sz = Sizes(x.shape, mid, rows, cols)
    k1 = jnp.swapaxes(k1, 2, 3)
    grad, a3, sums = call_a(
        sz, x, dy, heights, widths, k1.reshape(9 * mid, wide), k2, k3, ko, b1[None], b2[None], b3[None]
    )
    out, grad, g1, g2, g3, go, s1, s2, s3, so = call_b(sz, x, grad, a3, sums, ko, bo[None])
    return (
        out,
        grad,
        jnp.swapaxes(g1, 2, 3),
        s1.reshape(mid),
        g2,
        s2.reshape(mid),
        g3,
        s3.reshape(mid),
        go,
        so.reshape(wide),
    )


def solution(mesh):
    tiled = P(None, "rows", "cols", None)
    return jax.shard_map(
        functools.partial(body, mesh.shape["rows"], mesh.shape["cols"]),
        mesh=mesh,
        in_specs=(tiled,) + (P(),) * 8 + (tiled, P(), P()),
        out_specs=(tiled, tiled) + (P(),) * 8,
        check_vma=False,
    )
```

```python
import functools

import jax
import jax.numpy as jnp
from jax import lax
from jax.experimental import pallas as pl
from jax.experimental.pallas import tpu as pltpu
from jax.sharding import PartitionSpec as P

MESH = pl.DeviceIdType.MESH
bf16 = jnp.bfloat16
f32 = jnp.float32
LANES = 128
NN = (((1,), (0,)), ((), ()))
NT = (((1,), (1,)), ((), ()))
GAIN = 1.0 / 64.0
EXCHANGES = 6
GOES = ((0, 1), (0, -1), (1, 0), (-1, 0), (1, 1), (1, -1), (-1, 1), (-1, -1))


SMALL = ("k2", "k3", "ko_in", "b1", "b2", "b3")


def dot(a, b, dims=NN):
    return lax.dot_general(a, b, dims, preferred_element_type=f32)


def halves(v):
    hi = v.astype(bf16)
    return hi, (v - hi.astype(f32)).astype(bf16)


def sigmoid(v):
    return 0.5 + 0.5 * jnp.tanh(0.5 * v)


def cat(parts, axis):
    return jnp.concatenate(parts, axis=axis)


def lane_column(width):
    return lax.broadcasted_iota(jnp.int32, (1, LANES), 1) % width


class Sizes:
    def __init__(self, shape, mid, rows, cols):
        self.images, self.height, self.width, self.wide = shape
        self.mid = mid
        self.rows, self.cols = rows, cols
        self.per_group = LANES // self.width
        self.groups = self.images // self.per_group
        self.block = min(16, self.height)
        self.blocks = self.height // self.block
        self.devices = rows * cols
        self.lows = dict(taps=min(rows, max(16 // (cols // 2), 1)), rest=2)
        half = 3 * mid // 8
        self.counts = dict(
            taps=9 * mid // 8 * (self.wide // LANES) + mid // 8,
            rest=(mid + 16) // 8 * (self.wide // LANES) + 2 * (half + half // 2),
        )
        self.parts, at = {}, 0
        for name, used in self.counts.items():
            shard = -(-used // self.devices)
            self.parts[name] = (at, shard * self.devices, shard)
            at += shard * self.devices
        self.units = at


def kernel_a(sz, refs):
    x_hbm, dy_hbm, heights, widths, k1 = refs["io"][:5]
    grad_hbm, a3_hbm, sums_out = refs["io"][11:]
    k2, k3, ko_in, b1, b2, b3 = [refs[n] for n in SMALL]
    w1, w2, w3, t3, t2, ko, bias = [refs[n] for n in ("w1", "w2", "w3", "t3", "t2", "ko", "bias")]
    G, H, W, M = sz.groups, sz.height, sz.width, sz.mid
    RB, NB = sz.block, sz.blocks
    me_r, me_c = lax.axis_index("rows"), lax.axis_index("cols")
    col = lane_column(W)
    first, last = col == 0, col == W - 1
    ends = first | last
    even = col % 2 == 0
    n3 = 3 * M

    has_up, has_down = me_r > 0, me_r < sz.rows - 1
    has_left, has_right = me_c > 0, me_c < sz.cols - 1

    row_at = {d: lax.rem(me_r + d + sz.rows, sz.rows) if d else me_r for d in (-1, 0, 1)}
    col_at = {d: lax.rem(me_c + d + sz.cols, sz.cols) if d else me_c for d in (-1, 0, 1)}

    def neighbour(dr, dc):
        return row_at[dr], col_at[dc]

    buf = refs["buf"]
    half_rows = RB // 2

    def in_copy(src, which, g, k):
        n0 = g * sz.per_group
        return pltpu.make_async_copy(
            src.at[pl.ds(n0, sz.per_group), pl.ds(k * half_rows, half_rows)],
            buf.at[pl.ds(n0, sz.per_group), pl.ds(k * half_rows, half_rows)],
            refs["in_sem"].at[which, g, k],
        )

    in_copy(x_hbm, 0, 0, 0).start()

    k1_copy = pltpu.make_async_copy(k1, refs["acc1"], refs["k1_sem"])
    k1_copy.start()
    small_copies = [
        pltpu.make_async_copy(src, refs[n], refs["small_sem"].at[i])
        for i, (n, src) in enumerate(zip(SMALL, refs["io"][5:11]))
    ]
    for copy in small_copies:
        copy.start()

    def prepare():
        k1_copy.wait()
        hi, lo = halves(refs["acc1"][...])
        w1[...] = cat([hi, hi, lo], 1)
        for copy in small_copies:
            copy.wait()
        for i, b in enumerate((b1, b2, b3)):
            bias[i] = jnp.broadcast_to(b[...], (LANES, M)).T

    def prepare_rest():
        back = refs["acc1"][...].reshape(3, 3, M, sz.wide)
        for p in range(3):
            hi, lo = halves(cat([back[2 - p, 2 - b].T for b in range(3)], 1))
            refs["wb"][:, 2 * p * n3 : 2 * (p + 1) * n3] = cat([hi, hi], 1)
            refs["wb"][:, (6 + p) * n3 : (7 + p) * n3] = lo
        across = lax.broadcasted_iota(jnp.int32, (W, LANES), 0) + me_c * W
        for n in range(sz.images):
            refs["inside"][n] = jnp.where(across < widths[n], 1.0, 0.0)
        ko[:M], ko[M:] = halves(ko_in[...])
        for k, fwd, back in ((k2, w2, t2), (k3, w3, t3)):
            for p in range(3):
                at = slice(p * M, (p + 1) * M)
                hi, lo = halves(cat([k[p, q].T for q in range(3)], 1))
                fwd[at] = cat([hi, hi, lo], 1)
                hi, lo = halves(cat([k[2 - p, 2 - q] for q in range(3)], 1))
                back[at] = cat([hi, hi, lo], 1)

    core, rest = me_c % 2, me_c // 2
    pair_id = (me_r, me_c + 1 - 2 * core)

    def levels(name):
        low_count = sz.lows[name]
        near, far = sz.cols // 2 * low_count, sz.rows // low_count
        low, far_at = me_r % low_count, me_r // low_count
        near_at = rest * low_count + low
        near_ids = []
        for d in range(1, near):
            k = lax.rem(near_at + d, near)
            near_ids.append((far_at * low_count + k % low_count, (k // low_count) * 2 + core))
        far_ids = [(lax.rem(far_at + d, far) * low_count + low, me_c) for d in range(1, far)]
        return near, far, near_at, far_at, near_ids, far_ids

    barrier = pltpu.get_barrier_semaphore()
    near_ids, far_ids = levels("taps")[4:]
    if far_ids:
        partners = [pair_id] + [neighbour(dr, dc) for dr, dc in GOES] + near_ids + far_ids
        partners += [dev for ids in levels("rest")[4:] for dev in ids]
    else:
        partners = near_ids + [neighbour(dr, dc) for dr, dc in GOES if dc]

    def greet():
        for dev in partners:
            pl.semaphore_signal(barrier, inc=1, device_id=dev, device_id_type=MESH)

    def message(e, g, slot):
        dr, dc = GOES[slot]
        at = (e % 2, g)
        if slot < 2:
            src, dst = refs["msg"].at[at], refs["sideway"].at[(*at, slot)]
        elif slot < 4:
            src = refs["rowmsg"].at[(*at, 3 - slot)]
            dst = refs["updown"].at[(*at, pl.ds((slot - 2) * M, M))]
        else:
            src = refs["cormsg"].at[(*at, 1 if dr > 0 else 0)]
            dst = refs["updown"].at[(*at, pl.ds(2 * M + 8 * (slot - 4), 8))]
        kind = 0 if slot < 2 else 1
        return pltpu.make_async_remote_copy(
            src_ref=src,
            dst_ref=dst,
            send_sem=refs["send"].at[e, g, kind],
            recv_sem=refs["recv"].at[e, g, kind],
            device_id=neighbour(dr, dc),
            device_id_type=MESH,
        )

    def landed(e, g, kind, sem):
        held = refs["updown" if kind else "sideway"].at[e % 2, g]
        pltpu.make_async_copy(held, held, refs[sem].at[e, g, kind]).wait()

    def send(e, g, top, bottom, top_rim, bottom_rim):
        for slot in (0, 1):
            message(e, g, slot).start()
        refs["rowmsg"][e % 2, g, 0] = top
        refs["rowmsg"][e % 2, g, 1] = bottom
        for slot in (2, 3):
            message(e, g, slot).start()
        refs["cormsg"][e % 2, g, 0] = pack_corner(top_rim)
        refs["cormsg"][e % 2, g, 1] = pack_corner(bottom_rim)
        for slot in (4, 5, 6, 7):
            message(e, g, slot).start()

    def reuse(e, g):
        if e >= 2:
            for kind in range(2):
                landed(e - 2, g, kind, "send")

    def receive(e, g, kind):
        landed(e, g, kind, "recv")

    def pack(held, value, u):
        moved = pltpu.roll(value, lax.rem(LANES + 1 + 2 * u, LANES), 1)
        return jnp.where(col // 2 == u, moved, held)

    def pack_corner(value):
        held = jnp.zeros((8, LANES), f32)
        for k in range(M // 8):
            held = jnp.where(col // 2 == k, pltpu.roll(value[8 * k : 8 * k + 8], 1 + 2 * k, 1), held)
        return held

    def beyond(e, g, lower):
        row = refs["updown"][e % 2, g, pl.ds(M if lower else 0, M)]
        at = 2 if lower else 0
        there = has_down if lower else has_up
        left = jnp.where(there & has_left, corner_left(refs["updown"][e % 2, g, pl.ds(2 * M + 8 * at, 8)]), 0.0)
        right = jnp.where(there & has_right, corner_right(refs["updown"][e % 2, g, pl.ds(2 * M + 8 * (at + 1), 8)]), 0.0)
        return jnp.where(there, row, 0.0), jnp.where(first, left, right)

    def meet(e, g):
        left = jnp.where(has_left, refs["sideway"][e % 2, g, 0], 0.0)
        right = jnp.where(has_right, refs["sideway"][e % 2, g, 1], 0.0)
        refs["met"][g] = jnp.where(even, left, pltpu.roll(right, (2 * W - 2) % LANES, 1))

    def from_sides(held, u):
        return pltpu.roll(held, LANES - W - 2 * u, 1)

    def corner_left(held):
        return cat([pltpu.roll(held, LANES - W - 2 * k, 1) for k in range(M // 8)], 0)

    def corner_right(held):
        return cat([pltpu.roll(held, W - 2 - 2 * k, 1) for k in range(M // 8)], 0)

    def nothing():
        pass

    def run(*phases, steps=NB, flat=False):
        for before, _, _ in phases:
            before()

        def step(b, carry):
            for _, body, _ in phases:
                body(b)
            return carry

        if flat:
            for b in range(steps):
                step(b, 0)
        else:
            lax.fori_loop(0, steps, step, 0)
        for _, _, after in phases:
            after()

    def conv_first(g):
        a0, z, carry = refs["a0"][g], refs["slope3"][g], refs["carry"][g]

        def before():
            carry[...] = jnp.zeros_like(carry)
            refs["msg"][0, g] = jnp.zeros((M, LANES), f32)

        def emit(row, s, held):
            s0, s1, s2 = s[:M], s[M : 2 * M], s[2 * M :]
            value = s1 + jnp.where(first, 0.0, pltpu.roll(s0, 1, 1))
            value = value + jnp.where(last, 0.0, pltpu.roll(s2, LANES - 1, 1))
            z[row + 1] = value
            rim = jnp.where(first, s2, s0)
            return rim, pack(held, rim, row)

        def body(b):
            held = refs["msg"][0, g]
            c0, c1 = carry[0], carry[1]
            for m in range(RB // 2):
                r = b * RB + 2 * m
                if 2 * m % half_rows == 0:
                    in_copy(x_hbm, 0, g, 2 * b + 2 * m // half_rows).wait()
                pair = []
                for i in range(2):
                    v = cat([buf[g * sz.per_group + s, r + i] for s in range(sz.per_group)], 0)
                    hi, lo = halves(v * sigmoid(v))
                    both = cat([hi, lo], 1)
                    a0[r + i] = both
                    pair.append(both)
                rhs = cat(pair, 0)
                y = dot(w1[...], cat([rhs, rhs[:, : sz.wide]], 1), NT)
                ya, yb = y[:, :LANES], y[:, LANES:]
                rim, held = emit(r - 1, c0 + ya[2 * n3 :], held)
                if m == 0:
                    refs["rim"][g, jnp.minimum(b, 1)] = rim
                _, held = emit(r, c1 + ya[n3 : 2 * n3] + yb[2 * n3 :], held)
                c0, c1 = ya[:n3] + yb[n3 : 2 * n3], yb[:n3]
            carry[0] = c0
            carry[1] = c1
            refs["msg"][0, g] = held

        def after():
            _, held = emit(H - 1, carry[0], refs["msg"][0, g])
            rim, _ = emit(H, carry[1], held)
            refs["msg"][0, g] = held
            for k in range(2 * NB):
                in_copy(dy_hbm, 1, g, k).start()
            send(0, g, z[0], z[H + 1], refs["rim"][g, 0], rim)

        return before, body, after

    def after_first(g):
        z, act, slope = refs["slope3"][g], refs["act"][g], refs["slope1"][g]
        def before():
            receive(0, g, 0)
            meet(0, g)
            refs["msg"][1, g] = jnp.zeros((M, LANES), f32)

        def emit(r, v, held):
            v = v + bias[0]
            sig = sigmoid(v)
            a = v * sig
            slope[r] = sig + a * (1.0 - sig)
            act[r] = a
            return pack(held, a, r)

        def with_sides(r):
            return z[r + 1] + jnp.where(ends, from_sides(refs["met"][g], r), 0.0)

        def body(b):
            held = refs["msg"][1, g]
            for k in range(RB):
                r = b * RB + k
                held = emit(r, with_sides(r), held)
            refs["msg"][1, g] = held

        def after():
            receive(0, g, 1)
            held = refs["msg"][1, g]
            for r, lower in ((0, False), (H - 1, True)):
                row, sides = beyond(0, g, lower)
                held = emit(r, with_sides(r) + row + jnp.where(ends, sides, 0.0), held)
            refs["msg"][1, g] = held
            send(1, g, act[0], act[H - 1], act[0], act[H - 1])

        return before, body, after

    def spread(e, g, dst):
        act = refs["act"][g]

        def before():
            receive(e, g, 0)
            meet(e, g)

        def store(row, v, left, right):
            before = jnp.where(first, left, pltpu.roll(v, 1, 1))
            behind = jnp.where(last, right, pltpu.roll(v, LANES - 1, 1))
            for at, part in enumerate((before, v, behind)):
                hi, lo = halves(part)
                dst[row, at * M : (at + 1) * M] = hi
                dst[row, n3 + at * M : n3 + (at + 1) * M] = lo

        def body(b):
            both = refs["met"][g]
            for k in range(RB):
                r = b * RB + k
                sides = from_sides(both, r)
                store(r + 1, act[r], sides, sides)

        def after():
            receive(e, g, 1)
            for at, lower in ((0, False), (H + 1, True)):
                row, sides = beyond(e, g, lower)
                store(at, row, sides, sides)

        return before, body, after

    def conv_mid(g, src, weight, emit, begin, end):
        carry = refs["carry"][g]

        def pair(m):
            rhs = cat([src[2 * m], src[2 * m + 1]], 1)
            y = dot(weight[...], cat([rhs, rhs[:n3]], 0))
            return y[:, :LANES], y[:, LANES:]

        def before():
            ya, yb = pair(0)
            carry[0, :M] = ya[:M] + yb[M : 2 * M]
            carry[1, :M] = yb[:M]

        def body(b):
            state = begin(b)
            c0, c1 = carry[0, :M], carry[1, :M]
            for k in range(RB // 2):
                ya, yb = pair(1 + b * (RB // 2) + k)
                r = b * RB + 2 * k
                state = emit(r, c0 + ya[2 * M :], state)
                state = emit(r + 1, c1 + ya[M : 2 * M] + yb[2 * M :], state)
                c0, c1 = ya[:M] + yb[M : 2 * M], yb[:M]
            carry[0, :M] = c0
            carry[1, :M] = c1
            end(b, state)

        return before, body

    def second(g):
        act, slope = refs["act"][g], refs["slope2"][g]

        def clear():
            reuse(2, g)
            refs["msg"][0, g] = jnp.zeros((M, LANES), f32)

        def emit(r, v, held):
            v = v + bias[1]
            sig = sigmoid(v)
            a = v * sig
            slope[r] = sig + a * (1.0 - sig)
            act[r] = a
            return pack(held, a, r)

        def end(b, held):
            refs["msg"][0, g] = held

        before, body = conv_mid(g, refs["p1"][g], w2, emit, lambda b: refs["msg"][0, g], end)
        return (lambda: (clear(), before())), body, lambda: send(2, g, act[0], act[H - 1], act[0], act[H - 1])

    def a3_copy(g, b):
        return pltpu.make_async_copy(
            refs["a3"].at[b % 2], a3_hbm.at[g, pl.ds(b * RB, RB)], refs["out_sem"].at[g, b]
        )

    def third(g):
        a3, slope = refs["a3"], refs["slope3"][g]

        def emit(r, v, state):
            v = v + bias[2]
            sig = sigmoid(v)
            a = v * sig
            slope[r] = sig + a * (1.0 - sig)
            hi, lo = halves(a)
            k = r - state * RB
            a3[state % 2, k, :M] = hi
            a3[state % 2, k, M:] = lo
            return state

        def begin(b):
            if NB > 2:

                @pl.when(b >= 2)
                def _():
                    a3_copy(g, b - 2).wait()

            return b

        before, body = conv_mid(g, refs["p2"][g], w3, emit, begin, lambda b, s: a3_copy(g, b).start())

        def after():
            for k in range(max(NB - 2, 0), NB):
                a3_copy(g, k).wait()

        return before, body, after

    ring_rows = half_rows // 2
    ring_count = H // ring_rows

    def again(g, k):
        at = (pl.ds(g * sz.per_group, sz.per_group), pl.ds(k * half_rows, half_rows))
        return (
            pltpu.make_async_copy(x_hbm.at[at], buf.at[at], refs["again_sem"].at[0, g, k]),
            pltpu.make_async_copy(buf.at[at], grad_hbm.at[at], refs["again_sem"].at[1, g, k]),
        )

    def cotangent(t, slot):
        t = lax.rem(t, G * ring_count)
        at = (
            pl.ds(t // ring_count * sz.per_group, sz.per_group),
            pl.ds(lax.rem(t, ring_count) * ring_rows, ring_rows),
        )
        return pltpu.make_async_copy(dy_hbm.at[at], refs["ring"].at[slot], refs["ring_sem"].at[slot])

    def masked(value, s, n, r):
        keep = refs["inside"][n] * jnp.where(me_r * H + r < heights[n], 1.0, 0.0)
        return value * cat([keep] * (sz.wide // LANES), 1)

    def input_grad(g):
        q, wb = refs["q"][g], refs["wb"]

        def body(b):
            again(g, b)[0].wait()
            for m in range(half_rows // 2):
                r = b * half_rows + 2 * m
                t = g * ring_count + 2 * b + 2 * m // ring_rows
                slot, at_row = 2 * m // ring_rows, 2 * m % ring_rows
                if at_row == 0:
                    cotangent(t, slot).wait()
                dy = refs["ring"].at[slot]
                three = [cat([q[r + s], q[r + 1 + s]], 1) for s in range(3)]
                y = dot(wb[...], cat(three + [t3[:n3] for t3 in three], 0)).T
                for i in range(2):
                    for s in range(sz.per_group):
                        n = g * sz.per_group + s
                        at = i * LANES + s * W
                        v = buf[n, r + i]
                        sig = sigmoid(v)
                        slope = sig * (1.0 + v * (1.0 - sig))
                        buf[n, r + i] = masked(dy[s, at_row + i], s, n, r + i) + y[at : at + W] * slope
                if at_row == ring_rows - 2:
                    cotangent(t + 2, slot).start()
            again(g, b)[1].start()

        return nothing, body, nothing

    def emit_grad(e, g, own, total, slope):
        act = refs["act"][g]

        def emit(r, v, state):
            held, summed = state
            d = v * slope[r]
            act[r] = d
            if own is not None:
                hi, lo = halves(d)
                own[r + 1, :M] = hi
                own[r + 1, M:] = lo
            return pack(held, d, r), summed + d

        def begin(b):
            return refs["msg"][e % 2, g], total[...]

        def end(b, state):
            refs["msg"][e % 2, g] = state[0]
            total[...] = state[1]

        def clear():
            reuse(e, g)
            refs["msg"][e % 2, g] = jnp.zeros((M, LANES), f32)

        return emit, begin, end, clear

    def out_layer(g):
        a3, act = refs["a3"], refs["act"][g]
        emit, begin, end, clear = emit_grad(3, g, refs["d3"][g], refs["total"].at[2], refs["slope3"][g])
        ones = jnp.ones((16, 2 * LANES), bf16)

        def body(b):
            for h in range(2):
                in_copy(dy_hbm, 1, g, 2 * b + h).wait()
            state = begin(b)
            upper, lower = refs["acc_o1"][...], refs["acc_o2"][...]
            for m in range(RB // 2):
                r = b * RB + 2 * m
                parts = []
                for i in range(2):
                    for s in range(sz.per_group):
                        n = g * sz.per_group + s
                        parts.append(masked(buf[n, r + i], s, n, r + i) * GAIN)
                hi, lo = halves(cat(parts, 0))
                y1 = dot(ko[...], hi, NT)
                y2 = dot(ko[:M], lo, NT)
                y = y1[:M] + y1[M:] + y2
                state = emit(r, y[:, :LANES], state)
                state = emit(r + 1, y[:, LANES:], state)
                act3 = cat([a3[b % 2, 2 * m], a3[b % 2, 2 * m + 1]], 1)
                upper = upper + dot(cat([act3, ones], 0), hi)
                lower = lower + dot(cat([act3[:M], ones], 0), lo)
            refs["acc_o1"][...] = upper
            refs["acc_o2"][...] = lower
            end(b, state)

        def after():
            send(3, g, act[0], act[H - 1], act[0], act[H - 1])
            for k in range(2 * NB):
                again(g, k)[0].start()
            if g == 0:
                for slot in range(2):
                    cotangent(slot, slot).start()

        return clear, body, after

    def back_layer(e, g, weight, own, total, slope):
        act = refs["act"][g]
        emit, begin, end, clear = emit_grad(e, g, own, total, slope)
        before, body = conv_mid(g, refs["q"][g], weight, emit, begin, end)
        return (lambda: (clear(), before())), body, lambda: send(e, g, act[0], act[H - 1], act[0], act[H - 1])

    def mid_kernel_grad(g, src, own, acc):
        def terms(rows, own_rows):
            left = cat(rows, 1)
            right = [cat(two, 1) for two in own_rows]
            hi = cat([two[:M] for two in right], 0)
            lo = cat([two[M:] for two in right], 0)
            return cat([left[:n3], left[:n3], left[n3:]], 1), cat([hi, lo, hi], 1)

        def body(b):
            ls, rs = [], []
            for m in range(RB // 2):
                r = b * RB + 2 * m
                l, rr = terms(
                    [src[r + 1], src[r + 2]], [[own[r + 2 - p], own[r + 3 - p]] for p in range(3)]
                )
                ls.append(l)
                rs.append(rr)
            acc[...] += dot(cat(ls, 1), cat(rs, 1), NT)

        def after():
            none = jnp.zeros((2 * M, LANES), bf16)
            l, rr = terms([src[0], src[H + 1]], [[own[1], none], [none, none], [none, own[H]]])
            acc[...] += dot(l, rr, NT)

        return nothing, body, after

    def first_kernel_grad(g):
        a0, q, acc = refs["a0"][g], refs["q"][g], refs["acc1"]

        def body(b):
            ls, rs = [], []
            for m in range(half_rows // 2):
                r = b * half_rows + 2 * m
                three = [cat([q[r + s], q[r + 1 + s]], 1) for s in range(3)]
                hi = cat([t[:n3] for t in three], 0)
                lo = cat([t[n3:] for t in three], 0)
                ls.append(cat([hi, hi, lo], 1))
                two = cat([a0[r], a0[r + 1]], 0)
                rs.append(cat([two[:, : sz.wide], two[:, sz.wide :], two[:, : sz.wide]], 0))
            for m in range(0, half_rows // 2, 2):
                acc[...] += dot(cat(ls[m : m + 2], 1), cat(rs[m : m + 2], 0))

        return nothing, body, nothing

    def reducer(name):
        base, units, shard = sz.parts[name]
        near, far, near_at, far_at, near_ids, far_ids = levels(name)
        half, quarter = units // 2, units // 2 // near
        ar, whole = refs["ar"], refs["ar_all"]
        sems = list(sz.parts).index(name)
        pair_buf = refs["pair_" + name]
        near_buf = refs["near_" + name]
        far_buf = refs["far_" + name]
        used = [0]

        def ship(src, dst, dev):
            pltpu.make_async_remote_copy(
                src_ref=src,
                dst_ref=dst,
                send_sem=refs["ar_send"].at[sems, used[0]],
                recv_sem=refs["ar_recv"].at[sems, used[0]],
                device_id=dev,
                device_id_type=MESH,
            ).start()

        def land(held):
            for sem in ("ar_recv", "ar_send"):
                pltpu.make_async_copy(held, held, refs[sem].at[sems, used[0]]).wait()
            used[0] += 1

        mine_half = base + core * half
        mine_quarter = mine_half + near_at * quarter
        mine = mine_quarter + far_at * shard

        def fill(blocks):
            at = base
            for block in blocks:
                rows = block.shape[0] // 8
                ar[at : at + rows] = block.reshape(rows, 8, LANES)
                at += rows
            if at < base + units:
                ar[at : base + units] = jnp.zeros((base + units - at, 8, LANES), f32)
            ship(ar.at[pl.ds(base + (1 - core) * half, half)], pair_buf, pair_id)

        def to_near():
            land(pair_buf)
            ar[pl.ds(mine_half, half)] += pair_buf[...]
            for d, dev in enumerate(near_ids, 1):
                to = lax.rem(near_at + d, near)
                ship(ar.at[pl.ds(mine_half + to * quarter, quarter)], near_buf.at[near - 1 - d], dev)

        def to_far():
            land(near_buf)
            got = ar[pl.ds(mine_quarter, quarter)]
            for d in range(near - 1):
                got = got + near_buf[d]
            ar[pl.ds(mine_quarter, quarter)] = got
            for d, dev in enumerate(far_ids, 1):
                to = lax.rem(far_at + d, far)
                ship(ar.at[pl.ds(mine_quarter + to * shard, shard)], far_buf.at[far - 1 - d], dev)

        def spread_far():
            land(far_buf)
            got = ar[pl.ds(mine, shard)]
            for d in range(far - 1):
                got = got + far_buf[d]
            whole[pl.ds(mine, shard)] = got
            for dev in far_ids:
                ship(whole.at[pl.ds(mine, shard)], whole.at[pl.ds(mine, shard)], dev)

        def spread_near():
            land(far_buf)
            at = pl.ds(mine_quarter, quarter)
            for dev in near_ids:
                ship(whole.at[at], whole.at[at], dev)

        def spread_pair():
            land(near_buf)
            at = pl.ds(mine_half, half)
            ship(whole.at[at], whole.at[at], pair_id)

        def done():
            land(pair_buf)
            sums = pltpu.make_async_copy(
                whole.at[pl.ds(base, units)], sums_out.at[pl.ds(base, units)], refs["sum_sem"].at[sems]
            )
            sums.start()
            return sums

        def near_only():
            land(near_buf)
            got = ar[pl.ds(mine, shard)]
            for d in range(near - 1):
                got = got + near_buf[d]
            whole[pl.ds(mine, shard)] = got
            for dev in near_ids:
                ship(whole.at[pl.ds(mine, shard)], whole.at[pl.ds(mine, shard)], dev)

        if far == 1:
            return fill, iter((to_near, near_only, spread_pair, done))
        return fill, iter((to_near, to_far, spread_far, spread_near, spread_pair, done))

    for name in ("acc2", "acc3", "acc_o1", "acc_o2", "total"):
        refs[name][...] = jnp.zeros_like(refs[name])
    none = jnp.zeros((2 * M, LANES), bf16)
    for g in range(G):
        for name in ("d2", "d3"):
            refs[name][g][0] = none
            refs[name][g][H + 1] = none

    every = range(G)
    moving, ended = {}, []

    def advance(*names):
        for name in names:
            if name not in moving:
                continue
            copy = next(moving[name])()
            if copy is not None:
                ended.append(copy)
                del moving[name]

    def reduce(name, blocks):
        fill, moving[name] = reducer(name)
        fill(blocks)

    def wide_blocks(value):
        return [value[:, h * LANES : (h + 1) * LANES] for h in range(sz.wide // LANES)]

    def mid_blocks(acc):
        value = acc[...]
        rest = value[:, LANES:]
        return [value[:, :LANES], cat([rest[: n3 // 2], rest[n3 // 2 :]], 1)]

    greet()
    prepare()
    for g in every:
        for k in range(2 * NB):
            if (g, k) != (0, 0):
                in_copy(x_hbm, 0, g, k).start()
    for g in every:
        before, body, after = conv_first(g)
        if g == 0:
            run((before, body, nothing))
            pl.semaphore_wait(barrier, len(partners))
            after()
        else:
            run((before, body, after))
    for g in every:
        run(after_first(g))
        if g == 0:
            prepare_rest()
            refs["acc1"][...] = jnp.zeros_like(refs["acc1"])
    for g in every:
        run(spread(1, g, refs["p1"][g]))
        run(second(g), flat=True)
    for g in every:
        run(spread(2, g, refs["p2"][g]))
        run(third(g), out_layer(g))
    for g in every:
        run(spread(3, g, refs["q"][g]), mid_kernel_grad(g, refs["p2"][g], refs["d3"][g], refs["acc3"]))
        run(back_layer(4, g, t3, refs["d2"][g], refs["total"].at[1], refs["slope2"][g]), flat=True)
    for g in every:
        run(spread(4, g, refs["q"][g]), mid_kernel_grad(g, refs["p1"][g], refs["d2"][g], refs["acc2"]))
        if g == G - 1:
            upper, lower = refs["acc_o1"][...], refs["acc_o2"][...]
            outs = cat([upper[:M] + upper[M : 2 * M] + lower[:M], upper[2 * M :] + lower[M:]], 0)
            reduce("rest", wide_blocks(outs) + mid_blocks(refs["acc3"]) + mid_blocks(refs["acc2"]))
        run(back_layer(5, g, t2, None, refs["total"].at[0], refs["slope1"][g]), flat=True)
    advance("rest")
    lane = lax.broadcasted_iota(jnp.int32, (1, LANES), 1)
    sums = [jnp.sum(refs["total"][i], axis=1, keepdims=True) for i in range(3)]
    biases = jnp.where(lane == 0, sums[0], jnp.where(lane == 1, sums[1], sums[2]))
    for g in every:
        run(spread(5, g, refs["q"][g]), flat=True)
        run(first_kernel_grad(g), steps=2 * NB)
        if g < G - 1:
            advance("rest")
    reduce("taps", wide_blocks(refs["acc1"]) + [biases])
    advance("rest", "taps")
    for g in every:
        run(input_grad(g), steps=2 * NB)
        advance("rest", "taps")
    while moving:
        advance(*list(moving))

    for copy in ended:
        copy.wait()
    for slot in range(2):
        cotangent(slot, slot).wait()
    for g in every:
        for k in range(2 * NB):
            again(g, k)[1].wait()
    for g in every:
        for e in range(EXCHANGES - 2, EXCHANGES):
            for kind in range(2):
                landed(e, g, kind, "send")


def call_a(sz, x, dy, heights, widths, k1, k2, k3, ko, b1, b2, b3):
    G, H, W, M, N = sz.groups, sz.height, sz.width, sz.mid, LANES
    n3 = 3 * M
    names, shapes = [], []

    def add(name, *what):
        names.append((name, len(what)))
        shapes.extend(what)

    def per_group(name, shape, dtype):
        add(name, *[pltpu.VMEM(shape, dtype) for _ in range(G)])

    add("buf", pltpu.VMEM((sz.images, H, W, sz.wide), f32))
    per_group("a0", (H, N, 2 * sz.wide), bf16)
    per_group("act", (H, M, N), f32)
    per_group("carry", (2, n3, N), f32)
    for name in ("slope1", "slope2"):
        per_group(name, (H, M, N), f32)
    per_group("slope3", (H + 2, M, N), f32)
    for name in ("p1", "p2", "q"):
        per_group(name, (H + 2, 2 * n3, N), bf16)
    for name in ("d3", "d2"):
        per_group(name, (H + 2, 2 * M, N), bf16)
    add("a3", pltpu.VMEM((2, sz.block, 2 * M, N), bf16))
    add("w1", pltpu.VMEM((9 * M, 3 * sz.wide), bf16))
    for name in ("w2", "w3", "t2", "t3"):
        add(name, pltpu.VMEM((n3, 3 * n3), bf16))
    add("ko", pltpu.VMEM((2 * M, sz.wide), bf16))
    add("met", pltpu.VMEM((G, M, N), f32))
    add("bias", pltpu.VMEM((3, M, N), f32))
    E = EXCHANGES
    add("rim", pltpu.VMEM((G, 2, M, N), f32))
    add("msg", pltpu.VMEM((2, G, M, N), f32))
    add("rowmsg", pltpu.VMEM((2, G, 2, M, N), f32))
    add("cormsg", pltpu.VMEM((2, G, 2, 8, N), f32))
    add("sideway", pltpu.VMEM((2, G, 2, M, N), f32))
    add("updown", pltpu.VMEM((2, G, 2 * M + 32, N), f32))
    add("acc1", pltpu.VMEM((9 * M, sz.wide), f32))
    add("acc2", pltpu.VMEM((n3, n3), f32))
    add("acc3", pltpu.VMEM((n3, n3), f32))
    add("acc_o1", pltpu.VMEM((2 * M + 16, sz.wide), f32))
    add("acc_o2", pltpu.VMEM((M + 16, sz.wide), f32))
    add("total", pltpu.VMEM((3, M, N), f32))
    U = sz.units
    add("ar", pltpu.VMEM((U, 8, N), f32))
    add("ar_all", pltpu.VMEM((U, 8, N), f32))
    for part, (_, units, shard) in sz.parts.items():
        near = sz.cols // 2 * sz.lows[part]
        far = sz.rows // sz.lows[part]
        add("pair_" + part, pltpu.VMEM((units // 2, 8, N), f32))
        add("near_" + part, pltpu.VMEM((max(near - 1, 1), units // 2 // near, 8, N), f32))
        add("far_" + part, pltpu.VMEM((max(far - 1, 1), shard, 8, N), f32))
    add("sum_sem", pltpu.SemaphoreType.DMA((len(sz.parts),)))
    add("in_sem", pltpu.SemaphoreType.DMA((2, G, 2 * sz.blocks)))
    add("k1_sem", pltpu.SemaphoreType.DMA)
    for name, value in zip(SMALL, (k2, k3, ko, b1, b2, b3)):
        add(name, pltpu.VMEM(value.shape, f32))
    add("small_sem", pltpu.SemaphoreType.DMA((len(SMALL),)))
    add("again_sem", pltpu.SemaphoreType.DMA((2, G, 2 * sz.blocks)))
    add("ring_sem", pltpu.SemaphoreType.DMA((2,)))
    add("ring", pltpu.VMEM((2, sz.per_group, sz.block // 4, W, sz.wide), f32))
    add("inside", pltpu.VMEM((sz.images, W, N), f32))
    add("wb", pltpu.VMEM((sz.wide, 9 * n3), bf16))
    add("out_sem", pltpu.SemaphoreType.DMA((G, sz.blocks)))
    add("send", pltpu.SemaphoreType.DMA((E, G, 2)))
    add("recv", pltpu.SemaphoreType.DMA((E, G, 2)))
    add("ar_send", pltpu.SemaphoreType.DMA((len(sz.parts), 6)))
    add("ar_recv", pltpu.SemaphoreType.DMA((len(sz.parts), 6)))
    grouped = ("a0", "act", "carry", "slope1", "slope2", "slope3", "p1", "p2", "q", "d3", "d2")

    def whole_kernel(*args):
        refs = {"io": args[:14]}
        at = 14
        for name, size in names:
            held = args[at : at + size]
            refs[name] = held if name in grouped else held[0]
            at += size
        kernel_a(sz, refs)

    hbm = pl.BlockSpec(memory_space=pl.ANY)
    vmem = pl.BlockSpec(memory_space=pltpu.VMEM)
    smem = pl.BlockSpec(memory_space=pltpu.SMEM)
    return pl.pallas_call(
        whole_kernel,
        out_shape=(
            jax.ShapeDtypeStruct(x.shape, f32),
            jax.ShapeDtypeStruct((G, H, 2 * M, N), bf16),
            jax.ShapeDtypeStruct((U, 8, N), f32),
        ),
        in_specs=[hbm, hbm, smem, smem] + [hbm] * 7,
        out_specs=(hbm, hbm, hbm),
        scratch_shapes=shapes,
        compiler_params=pltpu.CompilerParams(
            collective_id=0, has_side_effects=True, vmem_limit_bytes=63 * 2**20
        ),
        name="block_chain",
    )(x, dy, heights, widths, k1, k2, k3, ko, b1, b2, b3)


def kernel_b(
    sz, rows, x_hbm, g_hbm, a3_hbm, sums_hbm, ko_hbm, bo, out_hbm, grad_hbm, g1_hbm, g2_hbm, g3_hbm, go_hbm, s1, s2, s3, so,
    x, grad, a3, sums, ko, wo, g1, g2, g3, go, in_sem, out_sem, sums_sem,
):
    G, W, M = sz.groups, sz.width, sz.mid
    n3 = 3 * M
    chunks = sz.height // rows

    def copies_in(c):
        at = (slice(None), pl.ds(c * rows, rows))
        pairs = ((a3_hbm, a3), (x_hbm, x), (g_hbm, grad))
        return [pltpu.make_async_copy(s.at[at], d.at[at], in_sem.at[i, c]) for i, (s, d) in enumerate(pairs)]

    def copies_out(c):
        at = (slice(None), pl.ds(c * rows, rows))
        return [
            pltpu.make_async_copy(grad.at[at], grad_hbm.at[at], out_sem.at[0, c]),
            pltpu.make_async_copy(x.at[at], out_hbm.at[at], out_sem.at[1, c]),
        ]

    early = pltpu.make_async_copy(ko_hbm, ko, sums_sem.at[0])
    sums_in = pltpu.make_async_copy(sums_hbm, sums, sums_sem.at[1])
    sums_out = [
        pltpu.make_async_copy(s, d, sums_sem.at[2 + i])
        for i, (s, d) in enumerate(((g1, g1_hbm), (g2, g2_hbm), (g3, g3_hbm), (go, go_hbm)))
    ]
    early.start()
    for c in range(chunks):
        for copy in copies_in(c):
            copy.start()
        if c == 0:
            sums_in.start()
    early.wait()
    hi, lo = halves(ko[...].T * GAIN)
    wo[...] = cat([hi, hi, lo], 1)
    add = bo[...] * GAIN

    def body(c, carry):
        a3_in, x_in, grad_in = copies_in(c)
        grad_out, x_out = copies_out(c)
        a3_in.wait()
        x_in.wait()
        for k in range(rows):
            i = c * rows + k
            act = cat([a3[g, i] for g in range(G)], 1)
            branch = dot(wo[...], cat([act, act[:M]], 0)).T
            for n in range(sz.images):
                x[n, i] = x[n, i] + (branch[n * W : (n + 1) * W] + add)
        x_out.start()
        grad_in.wait()
        grad_out.start()
        return carry

    def take(at, count):
        return sums[at : at + count].reshape(count * 8, LANES)

    lax.fori_loop(0, chunks - 1, body, 0)

    sums_in.wait()
    at = sz.parts["taps"][0]
    for h in range(sz.wide // LANES):
        part = take(at, 9 * M // 8)
        at += 9 * M // 8
        for t in range(3):
            for b in range(3):
                lo = (t * 3 + b) * M
                g1[2 - t, 2 - b, :, h * LANES : (h + 1) * LANES] = part[lo : lo + M]
    rest = take(at, M // 8).T
    s1[...] = rest[0:1]
    s2[...] = rest[1:2]
    s3[...] = rest[2:3]
    at = sz.parts["rest"][0]
    for h in range(sz.wide // LANES):
        part = take(at, (M + 16) // 8)
        at += (M + 16) // 8
        go[:, h * LANES : (h + 1) * LANES] = part[:M]
        so[:, h * LANES : (h + 1) * LANES] = part[M : M + 1]
    for ref in (g3, g2):
        big, rest = take(at, n3 // 8), take(at + n3 // 8, n3 // 16)
        at += n3 // 8 + n3 // 16
        rest = cat([rest[:, :M], rest[:, M:]], 0)
        for b in range(3):
            sl = slice(b * M, (b + 1) * M)
            ref[0, b] = big[sl, :M]
            ref[1, b] = big[sl, M:]
            ref[2, b] = rest[sl]
    for copy in sums_out:
        copy.start()

    lax.fori_loop(chunks - 1, chunks, body, 0)

    def finish(c, carry):
        for copy in copies_out(c):
            copy.wait()
        return carry

    lax.fori_loop(0, chunks, finish, 0)
    for copy in sums_out:
        copy.wait()


def call_b(sz, x, grad, a3, sums, ko, bo):
    M = sz.mid
    rows = 8
    hbm = pl.BlockSpec(memory_space=pl.ANY)
    vmem = pl.BlockSpec(memory_space=pltpu.VMEM)
    grads = ((3, 3, M, sz.wide), (3, 3, M, M), (3, 3, M, M), (M, sz.wide))
    small = ((1, M), (1, M), (1, M), (1, sz.wide))
    return pl.pallas_call(
        functools.partial(kernel_b, sz, rows),
        out_shape=tuple(jax.ShapeDtypeStruct(s, f32) for s in (x.shape, x.shape) + grads + small),
        in_specs=[hbm] * 5 + [vmem],
        out_specs=(hbm,) * 6 + (vmem,) * 4,
        scratch_shapes=[
            pltpu.VMEM(x.shape, f32),
            pltpu.VMEM(x.shape, f32),
            pltpu.VMEM(a3.shape, bf16),
            pltpu.VMEM(sums.shape, f32),
            pltpu.VMEM(ko.shape, f32),
            pltpu.VMEM((sz.wide, 3 * M), bf16),
        ]
        + [pltpu.VMEM(s, f32) for s in grads]
        + [
            pltpu.SemaphoreType.DMA((3, sz.height // rows)),
            pltpu.SemaphoreType.DMA((2, sz.height // rows)),
            pltpu.SemaphoreType.DMA((6,)),
        ],
        compiler_params=pltpu.CompilerParams(vmem_limit_bytes=60 * 2**20),
        name="wide_outputs",
    )(x, grad, a3, sums, ko, bo)


def body(rows, cols, x, k1, b1, k2, b2, k3, b3, ko, bo, dy, heights, widths):
    wide, mid = k1.shape[2:]
    sz = Sizes(x.shape, mid, rows, cols)
    k1 = jnp.swapaxes(k1, 2, 3)
    grad, a3, sums = call_a(
        sz, x, dy, heights, widths, k1.reshape(9 * mid, wide), k2, k3, ko, b1[None], b2[None], b3[None]
    )
    out, grad, g1, g2, g3, go, s1, s2, s3, so = call_b(sz, x, grad, a3, sums, ko, bo[None])
    return (
        out,
        grad,
        jnp.swapaxes(g1, 2, 3),
        s1.reshape(mid),
        g2,
        s2.reshape(mid),
        g3,
        s3.reshape(mid),
        go,
        so.reshape(wide),
    )


def solution(mesh):
    tiled = P(None, "rows", "cols", None)
    return jax.shard_map(
        functools.partial(body, mesh.shape["rows"], mesh.shape["cols"]),
        mesh=mesh,
        in_specs=(tiled,) + (P(),) * 8 + (tiled, P(), P()),
        out_specs=(tiled, tiled) + (P(),) * 8,
        check_vma=False,
    )
```

```python
import functools

import jax
import jax.numpy as jnp
from jax import lax
from jax.experimental import pallas as pl
from jax.experimental.pallas import tpu as pltpu
from jax.sharding import PartitionSpec as P

MESH = pl.DeviceIdType.MESH
bf16 = jnp.bfloat16
f32 = jnp.float32
LANES = 128
NN = (((1,), (0,)), ((), ()))
NT = (((1,), (1,)), ((), ()))
GAIN = 1.0 / 64.0
EXCHANGES = 6
GOES = ((0, 1), (0, -1), (1, 0), (-1, 0), (1, 1), (1, -1), (-1, 1), (-1, -1))


SMALL = ("k2", "k3", "ko_in", "b1", "b2", "b3")


def dot(a, b, dims=NN):
    return lax.dot_general(a, b, dims, preferred_element_type=f32)


def halves(v):
    hi = v.astype(bf16)
    return hi, (v - hi.astype(f32)).astype(bf16)


def sigmoid(v):
    return 0.5 + 0.5 * jnp.tanh(0.5 * v)


def cat(parts, axis):
    return jnp.concatenate(parts, axis=axis)


def lane_column(width):
    return lax.broadcasted_iota(jnp.int32, (1, LANES), 1) % width


class Sizes:
    def __init__(self, shape, mid, rows, cols):
        self.images, self.height, self.width, self.wide = shape
        self.mid = mid
        self.rows, self.cols = rows, cols
        self.per_group = LANES // self.width
        self.groups = self.images // self.per_group
        self.block = min(16, self.height)
        self.blocks = self.height // self.block
        self.devices = rows * cols
        self.lows = dict(taps=min(rows, max(16 // (cols // 2), 1)), rest=2)
        half = 3 * mid // 8
        self.counts = dict(
            taps=9 * mid // 8 * (self.wide // LANES) + mid // 8,
            rest=(mid + 16) // 8 * (self.wide // LANES) + 2 * (half + half // 2),
        )
        self.parts, at = {}, 0
        for name, used in self.counts.items():
            shard = -(-used // self.devices)
            self.parts[name] = (at, shard * self.devices, shard)
            at += shard * self.devices
        self.units = at


def kernel_a(sz, refs):
    x_hbm, dy_hbm, heights, widths, k1 = refs["io"][:5]
    grad_hbm, a3_hbm, sums_out = refs["io"][11:]
    k2, k3, ko_in, b1, b2, b3 = [refs[n] for n in SMALL]
    w1, w2, w3, t3, t2, ko, bias = [refs[n] for n in ("w1", "w2", "w3", "t3", "t2", "ko", "bias")]
    G, H, W, M = sz.groups, sz.height, sz.width, sz.mid
    RB, NB = sz.block, sz.blocks
    me_r, me_c = lax.axis_index("rows"), lax.axis_index("cols")
    col = lane_column(W)
    first, last = col == 0, col == W - 1
    ends = first | last
    even = col % 2 == 0
    n3 = 3 * M

    has_up, has_down = me_r > 0, me_r < sz.rows - 1
    has_left, has_right = me_c > 0, me_c < sz.cols - 1

    row_at = {d: lax.rem(me_r + d + sz.rows, sz.rows) if d else me_r for d in (-1, 0, 1)}
    col_at = {d: lax.rem(me_c + d + sz.cols, sz.cols) if d else me_c for d in (-1, 0, 1)}

    def neighbour(dr, dc):
        return row_at[dr], col_at[dc]

    buf = refs["buf"]
    half_rows = RB // 2

    def in_copy(src, which, g, k):
        n0 = g * sz.per_group
        return pltpu.make_async_copy(
            src.at[pl.ds(n0, sz.per_group), pl.ds(k * half_rows, half_rows)],
            buf.at[pl.ds(n0, sz.per_group), pl.ds(k * half_rows, half_rows)],
            refs["in_sem"].at[which, g, k],
        )

    in_copy(x_hbm, 0, 0, 0).start()

    k1_copy = pltpu.make_async_copy(k1, refs["acc1"], refs["k1_sem"])
    k1_copy.start()
    small_copies = [
        pltpu.make_async_copy(src, refs[n], refs["small_sem"].at[i])
        for i, (n, src) in enumerate(zip(SMALL, refs["io"][5:11]))
    ]
    for copy in small_copies:
        copy.start()

    def prepare():
        k1_copy.wait()
        hi, lo = halves(refs["acc1"][...])
        w1[...] = cat([hi, hi, lo], 1)
        for copy in small_copies:
            copy.wait()
        for i, b in enumerate((b1, b2, b3)):
            bias[i] = jnp.broadcast_to(b[...], (LANES, M)).T

    def prepare_rest():
        back = refs["acc1"][...].reshape(3, 3, M, sz.wide)
        for p in range(3):
            hi, lo = halves(cat([back[2 - p, 2 - b].T for b in range(3)], 1))
            refs["wb"][:, 2 * p * n3 : 2 * (p + 1) * n3] = cat([hi, hi], 1)
            refs["wb"][:, (6 + p) * n3 : (7 + p) * n3] = lo
        across = lax.broadcasted_iota(jnp.int32, (W, LANES), 0) + me_c * W
        for n in range(sz.images):
            refs["inside"][n] = jnp.where(across < widths[n], 1.0, 0.0)
        ko[:M], ko[M:] = halves(ko_in[...])
        for k, fwd, back in ((k2, w2, t2), (k3, w3, t3)):
            for p in range(3):
                at = slice(p * M, (p + 1) * M)
                hi, lo = halves(cat([k[p, q].T for q in range(3)], 1))
                fwd[at], fwd[n3 + p * M : n3 + (p + 1) * M] = hi, lo
                hi, lo = halves(cat([k[2 - p, 2 - q] for q in range(3)], 1))
                back[at], back[n3 + p * M : n3 + (p + 1) * M] = hi, lo

    core, rest = me_c % 2, me_c // 2
    pair_id = (me_r, me_c + 1 - 2 * core)

    def levels(name):
        low_count = sz.lows[name]
        near, far = sz.cols // 2 * low_count, sz.rows // low_count
        low, far_at = me_r % low_count, me_r // low_count
        near_at = rest * low_count + low
        near_ids = []
        for d in range(1, near):
            k = lax.rem(near_at + d, near)
            near_ids.append((far_at * low_count + k % low_count, (k // low_count) * 2 + core))
        far_ids = [(lax.rem(far_at + d, far) * low_count + low, me_c) for d in range(1, far)]
        return near, far, near_at, far_at, near_ids, far_ids

    barrier = pltpu.get_barrier_semaphore()
    near_ids, far_ids = levels("taps")[4:]
    if far_ids:
        partners = [pair_id] + [neighbour(dr, dc) for dr, dc in GOES] + near_ids + far_ids
        partners += [dev for ids in levels("rest")[4:] for dev in ids]
    else:
        partners = near_ids + [neighbour(dr, dc) for dr, dc in GOES if dc]

    def greet():
        for dev in partners:
            pl.semaphore_signal(barrier, inc=1, device_id=dev, device_id_type=MESH)

    def message(e, g, slot):
        dr, dc = GOES[slot]
        at = (e % 2, g)
        if slot < 2:
            src, dst = refs["msg"].at[at], refs["sideway"].at[(*at, slot)]
        elif slot < 4:
            src = refs["rowmsg"].at[(*at, 3 - slot)]
            dst = refs["updown"].at[(*at, pl.ds((slot - 2) * M, M))]
        else:
            src = refs["cormsg"].at[(*at, 1 if dr > 0 else 0)]
            dst = refs["updown"].at[(*at, pl.ds(2 * M + 8 * (slot - 4), 8))]
        kind = 0 if slot < 2 else 1
        return pltpu.make_async_remote_copy(
            src_ref=src,
            dst_ref=dst,
            send_sem=refs["send"].at[e, g, kind],
            recv_sem=refs["recv"].at[e, g, kind],
            device_id=neighbour(dr, dc),
            device_id_type=MESH,
        )

    def landed(e, g, kind, sem):
        held = refs["updown" if kind else "sideway"].at[e % 2, g]
        pltpu.make_async_copy(held, held, refs[sem].at[e, g, kind]).wait()

    def send(e, g, top, bottom, top_rim, bottom_rim):
        for slot in (0, 1):
            message(e, g, slot).start()
        refs["rowmsg"][e % 2, g, 0] = top
        refs["rowmsg"][e % 2, g, 1] = bottom
        for slot in (2, 3):
            message(e, g, slot).start()
        refs["cormsg"][e % 2, g, 0] = pack_corner(top_rim)
        refs["cormsg"][e % 2, g, 1] = pack_corner(bottom_rim)
        for slot in (4, 5, 6, 7):
            message(e, g, slot).start()

    def reuse(e, g):
        if e >= 2:
            for kind in range(2):
                landed(e - 2, g, kind, "send")

    def receive(e, g, kind):
        landed(e, g, kind, "recv")

    def pack(held, value, u):
        moved = pltpu.roll(value, lax.rem(LANES + 1 + 2 * u, LANES), 1)
        return jnp.where(col // 2 == u, moved, held)

    def pack_corner(value):
        held = jnp.zeros((8, LANES), f32)
        for k in range(M // 8):
            held = jnp.where(col // 2 == k, pltpu.roll(value[8 * k : 8 * k + 8], 1 + 2 * k, 1), held)
        return held

    def beyond(e, g, lower):
        row = refs["updown"][e % 2, g, pl.ds(M if lower else 0, M)]
        at = 2 if lower else 0
        there = has_down if lower else has_up
        left = jnp.where(there & has_left, corner_left(refs["updown"][e % 2, g, pl.ds(2 * M + 8 * at, 8)]), 0.0)
        right = jnp.where(there & has_right, corner_right(refs["updown"][e % 2, g, pl.ds(2 * M + 8 * (at + 1), 8)]), 0.0)
        return jnp.where(there, row, 0.0), jnp.where(first, left, right)

    def meet(e, g):
        left = jnp.where(has_left, refs["sideway"][e % 2, g, 0], 0.0)
        right = jnp.where(has_right, refs["sideway"][e % 2, g, 1], 0.0)
        refs["met"][g] = jnp.where(even, left, pltpu.roll(right, (2 * W - 2) % LANES, 1))

    def from_sides(held, u):
        return pltpu.roll(held, LANES - W - 2 * u, 1)

    def corner_left(held):
        return cat([pltpu.roll(held, LANES - W - 2 * k, 1) for k in range(M // 8)], 0)

    def corner_right(held):
        return cat([pltpu.roll(held, W - 2 - 2 * k, 1) for k in range(M // 8)], 0)

    def nothing():
        pass

    def run(*phases, steps=NB, flat=False):
        for before, _, _ in phases:
            before()

        def step(b, carry):
            for _, body, _ in phases:
                body(b)
            return carry

        if flat:
            for b in range(steps):
                step(b, 0)
        else:
            lax.fori_loop(0, steps, step, 0)
        for _, _, after in phases:
            after()

    def conv_first(g):
        a0, z, carry = refs["a0"][g], refs["slope3"][g], refs["carry"][g]

        def before():
            carry[...] = jnp.zeros_like(carry)
            refs["msg"][0, g] = jnp.zeros((M, LANES), f32)

        def emit(row, s, held):
            s0, s1, s2 = s[:M], s[M : 2 * M], s[2 * M :]
            value = s1 + jnp.where(first, 0.0, pltpu.roll(s0, 1, 1))
            value = value + jnp.where(last, 0.0, pltpu.roll(s2, LANES - 1, 1))
            z[row + 1] = value
            rim = jnp.where(first, s2, s0)
            return rim, pack(held, rim, row)

        def body(b):
            held = refs["msg"][0, g]
            c0, c1 = carry[0], carry[1]
            for m in range(RB // 2):
                r = b * RB + 2 * m
                if 2 * m % half_rows == 0:
                    in_copy(x_hbm, 0, g, 2 * b + 2 * m // half_rows).wait()
                pair = []
                for i in range(2):
                    v = cat([buf[g * sz.per_group + s, r + i] for s in range(sz.per_group)], 0)
                    hi, lo = halves(v * sigmoid(v))
                    both = cat([hi, lo], 1)
                    a0[r + i] = both
                    pair.append(both)
                rhs = cat(pair, 0)
                y = dot(w1[...], cat([rhs, rhs[:, : sz.wide]], 1), NT)
                ya, yb = y[:, :LANES], y[:, LANES:]
                rim, held = emit(r - 1, c0 + ya[2 * n3 :], held)
                if m == 0:
                    refs["rim"][g, jnp.minimum(b, 1)] = rim
                _, held = emit(r, c1 + ya[n3 : 2 * n3] + yb[2 * n3 :], held)
                c0, c1 = ya[:n3] + yb[n3 : 2 * n3], yb[:n3]
            carry[0] = c0
            carry[1] = c1
            refs["msg"][0, g] = held

        def after():
            _, held = emit(H - 1, carry[0], refs["msg"][0, g])
            rim, _ = emit(H, carry[1], held)
            refs["msg"][0, g] = held
            for k in range(2 * NB):
                in_copy(dy_hbm, 1, g, k).start()
            send(0, g, z[0], z[H + 1], refs["rim"][g, 0], rim)

        return before, body, after

    def after_first(g):
        z, act, slope = refs["slope3"][g], refs["act"][g], refs["slope1"][g]
        def before():
            receive(0, g, 0)
            meet(0, g)
            refs["msg"][1, g] = jnp.zeros((M, LANES), f32)

        def emit(r, v, held):
            v = v + bias[0]
            sig = sigmoid(v)
            a = v * sig
            slope[r] = sig + a * (1.0 - sig)
            act[r] = a
            return pack(held, a, r)

        def with_sides(r):
            return z[r + 1] + jnp.where(ends, from_sides(refs["met"][g], r), 0.0)

        def body(b):
            held = refs["msg"][1, g]
            for k in range(RB):
                r = b * RB + k
                held = emit(r, with_sides(r), held)
            refs["msg"][1, g] = held

        def after():
            receive(0, g, 1)
            held = refs["msg"][1, g]
            for r, lower in ((0, False), (H - 1, True)):
                row, sides = beyond(0, g, lower)
                held = emit(r, with_sides(r) + row + jnp.where(ends, sides, 0.0), held)
            refs["msg"][1, g] = held
            send(1, g, act[0], act[H - 1], act[0], act[H - 1])

        return before, body, after

    def spread(e, g, dst):
        act = refs["act"][g]

        def before():
            receive(e, g, 0)
            meet(e, g)

        def store(row, v, left, right):
            before = jnp.where(first, left, pltpu.roll(v, 1, 1))
            behind = jnp.where(last, right, pltpu.roll(v, LANES - 1, 1))
            for at, part in enumerate((before, v, behind)):
                hi, lo = halves(part)
                dst[row, at * M : (at + 1) * M] = hi
                dst[row, n3 + at * M : n3 + (at + 1) * M] = lo

        def body(b):
            both = refs["met"][g]
            for k in range(RB):
                r = b * RB + k
                sides = from_sides(both, r)
                store(r + 1, act[r], sides, sides)

        def after():
            receive(e, g, 1)
            for at, lower in ((0, False), (H + 1, True)):
                row, sides = beyond(e, g, lower)
                store(at, row, sides, sides)

        return before, body, after

    def conv_mid(g, src, weight, emit, begin, end):
        carry = refs["carry"][g]

        def pair(m):
            rhs = cat([src[2 * m], src[2 * m + 1]], 1)
            y = dot(weight[...], rhs[:n3])
            y = y[:n3] + y[n3:] + dot(weight[:n3], rhs[n3:])
            return y[:, :LANES], y[:, LANES:]

        def before():
            ya, yb = pair(0)
            carry[0, :M] = ya[:M] + yb[M : 2 * M]
            carry[1, :M] = yb[:M]

        def body(b):
            state = begin(b)
            c0, c1 = carry[0, :M], carry[1, :M]
            for k in range(RB // 2):
                ya, yb = pair(1 + b * (RB // 2) + k)
                r = b * RB + 2 * k
                state = emit(r, c0 + ya[2 * M :], state)
                state = emit(r + 1, c1 + ya[M : 2 * M] + yb[2 * M :], state)
                c0, c1 = ya[:M] + yb[M : 2 * M], yb[:M]
            carry[0, :M] = c0
            carry[1, :M] = c1
            end(b, state)

        return before, body

    def second(g):
        act, slope = refs["act"][g], refs["slope2"][g]

        def clear():
            reuse(2, g)
            refs["msg"][0, g] = jnp.zeros((M, LANES), f32)

        def emit(r, v, held):
            v = v + bias[1]
            sig = sigmoid(v)
            a = v * sig
            slope[r] = sig + a * (1.0 - sig)
            act[r] = a
            return pack(held, a, r)

        def end(b, held):
            refs["msg"][0, g] = held

        before, body = conv_mid(g, refs["p1"][g], w2, emit, lambda b: refs["msg"][0, g], end)
        return (lambda: (clear(), before())), body, lambda: send(2, g, act[0], act[H - 1], act[0], act[H - 1])

    def a3_copy(g, b):
        return pltpu.make_async_copy(
            refs["a3"].at[b % 2], a3_hbm.at[g, pl.ds(b * RB, RB)], refs["out_sem"].at[g, b]
        )

    def third(g):
        a3, slope = refs["a3"], refs["slope3"][g]

        def emit(r, v, state):
            v = v + bias[2]
            sig = sigmoid(v)
            a = v * sig
            slope[r] = sig + a * (1.0 - sig)
            hi, lo = halves(a)
            k = r - state * RB
            a3[state % 2, k, :M] = hi
            a3[state % 2, k, M:] = lo
            return state

        def begin(b):
            if NB > 2:

                @pl.when(b >= 2)
                def _():
                    a3_copy(g, b - 2).wait()

            return b

        before, body = conv_mid(g, refs["p2"][g], w3, emit, begin, lambda b, s: a3_copy(g, b).start())

        def after():
            for k in range(max(NB - 2, 0), NB):
                a3_copy(g, k).wait()

        return before, body, after

    ring_rows = half_rows // 2
    ring_count = H // ring_rows

    def again(g, k):
        at = (pl.ds(g * sz.per_group, sz.per_group), pl.ds(k * half_rows, half_rows))
        return (
            pltpu.make_async_copy(x_hbm.at[at], buf.at[at], refs["again_sem"].at[0, g, k]),
            pltpu.make_async_copy(buf.at[at], grad_hbm.at[at], refs["again_sem"].at[1, g, k]),
        )

    def cotangent(t, slot):
        t = lax.rem(t, G * ring_count)
        at = (
            pl.ds(t // ring_count * sz.per_group, sz.per_group),
            pl.ds(lax.rem(t, ring_count) * ring_rows, ring_rows),
        )
        return pltpu.make_async_copy(dy_hbm.at[at], refs["ring"].at[slot], refs["ring_sem"].at[slot])

    def masked(value, s, n, r):
        keep = refs["inside"][n] * jnp.where(me_r * H + r < heights[n], 1.0, 0.0)
        return value * cat([keep] * (sz.wide // LANES), 1)

    def input_grad(g):
        q, wb = refs["q"][g], refs["wb"]

        def body(b):
            again(g, b)[0].wait()
            for m in range(half_rows // 2):
                r = b * half_rows + 2 * m
                t = g * ring_count + 2 * b + 2 * m // ring_rows
                slot, at_row = 2 * m // ring_rows, 2 * m % ring_rows
                if at_row == 0:
                    cotangent(t, slot).wait()
                dy = refs["ring"].at[slot]
                three = [cat([q[r + s], q[r + 1 + s]], 1) for s in range(3)]
                y = dot(wb[...], cat(three + [t3[:n3] for t3 in three], 0)).T
                for i in range(2):
                    for s in range(sz.per_group):
                        n = g * sz.per_group + s
                        at = i * LANES + s * W
                        v = buf[n, r + i]
                        sig = sigmoid(v)
                        slope = sig * (1.0 + v * (1.0 - sig))
                        buf[n, r + i] = masked(dy[s, at_row + i], s, n, r + i) + y[at : at + W] * slope
                if at_row == ring_rows - 2:
                    cotangent(t + 2, slot).start()
            again(g, b)[1].start()

        return nothing, body, nothing

    def emit_grad(e, g, own, total, slope):
        act = refs["act"][g]

        def emit(r, v, state):
            held, summed = state
            d = v * slope[r]
            act[r] = d
            if own is not None:
                hi, lo = halves(d)
                own[r + 1, :M] = hi
                own[r + 1, M:] = lo
            return pack(held, d, r), summed + d

        def begin(b):
            return refs["msg"][e % 2, g], total[...]

        def end(b, state):
            refs["msg"][e % 2, g] = state[0]
            total[...] = state[1]

        def clear():
            reuse(e, g)
            refs["msg"][e % 2, g] = jnp.zeros((M, LANES), f32)

        return emit, begin, end, clear

    def out_layer(g):
        a3, act = refs["a3"], refs["act"][g]
        emit, begin, end, clear = emit_grad(3, g, refs["d3"][g], refs["total"].at[2], refs["slope3"][g])
        ones = jnp.ones((16, 2 * LANES), bf16)

        def body(b):
            for h in range(2):
                in_copy(dy_hbm, 1, g, 2 * b + h).wait()
            state = begin(b)
            upper, lower = refs["acc_o1"][...], refs["acc_o2"][...]
            for m in range(RB // 2):
                r = b * RB + 2 * m
                parts = []
                for i in range(2):
                    for s in range(sz.per_group):
                        n = g * sz.per_group + s
                        parts.append(masked(buf[n, r + i], s, n, r + i) * GAIN)
                hi, lo = halves(cat(parts, 0))
                y1 = dot(ko[...], hi, NT)
                y2 = dot(ko[:M], lo, NT)
                y = y1[:M] + y1[M:] + y2
                state = emit(r, y[:, :LANES], state)
                state = emit(r + 1, y[:, LANES:], state)
                act3 = cat([a3[b % 2, 2 * m], a3[b % 2, 2 * m + 1]], 1)
                upper = upper + dot(cat([act3, ones], 0), hi)
                lower = lower + dot(cat([act3[:M], ones], 0), lo)
            refs["acc_o1"][...] = upper
            refs["acc_o2"][...] = lower
            end(b, state)

        def after():
            send(3, g, act[0], act[H - 1], act[0], act[H - 1])
            for k in range(2 * NB):
                again(g, k)[0].start()
            if g == 0:
                for slot in range(2):
                    cotangent(slot, slot).start()

        return clear, body, after

    def back_layer(e, g, weight, own, total, slope):
        act = refs["act"][g]
        emit, begin, end, clear = emit_grad(e, g, own, total, slope)
        before, body = conv_mid(g, refs["q"][g], weight, emit, begin, end)
        return (lambda: (clear(), before())), body, lambda: send(e, g, act[0], act[H - 1], act[0], act[H - 1])

    def mid_kernel_grad(g, src, own, acc):
        def terms(rows, own_rows):
            left = cat(rows, 1)
            right = [cat(two, 1) for two in own_rows]
            hi = cat([two[:M] for two in right], 0)
            lo = cat([two[M:] for two in right], 0)
            return cat([left[:n3], left[:n3], left[n3:]], 1), cat([hi, lo, hi], 1)

        def body(b):
            ls, rs = [], []
            for m in range(RB // 2):
                r = b * RB + 2 * m
                l, rr = terms(
                    [src[r + 1], src[r + 2]], [[own[r + 2 - p], own[r + 3 - p]] for p in range(3)]
                )
                ls.append(l)
                rs.append(rr)
            acc[...] += dot(cat(ls, 1), cat(rs, 1), NT)

        def after():
            none = jnp.zeros((2 * M, LANES), bf16)
            l, rr = terms([src[0], src[H + 1]], [[own[1], none], [none, none], [none, own[H]]])
            acc[...] += dot(l, rr, NT)

        return nothing, body, after

    def first_kernel_grad(g):
        a0, q, acc = refs["a0"][g], refs["q"][g], refs["acc1"]

        def body(b):
            ls, rs = [], []
            for m in range(half_rows // 2):
                r = b * half_rows + 2 * m
                three = [cat([q[r + s], q[r + 1 + s]], 1) for s in range(3)]
                hi = cat([t[:n3] for t in three], 0)
                lo = cat([t[n3:] for t in three], 0)
                ls.append(cat([hi, hi, lo], 1))
                two = cat([a0[r], a0[r + 1]], 0)
                rs.append(cat([two[:, : sz.wide], two[:, sz.wide :], two[:, : sz.wide]], 0))
            for m in range(0, half_rows // 2, 2):
                acc[...] += dot(cat(ls[m : m + 2], 1), cat(rs[m : m + 2], 0))

        return nothing, body, nothing

    def reducer(name):
        base, units, shard = sz.parts[name]
        near, far, near_at, far_at, near_ids, far_ids = levels(name)
        half, quarter = units // 2, units // 2 // near
        ar, whole = refs["ar"], refs["ar_all"]
        sems = list(sz.parts).index(name)
        pair_buf = refs["pair_" + name]
        near_buf = refs["near_" + name]
        far_buf = refs["far_" + name]
        used = [0]

        def ship(src, dst, dev):
            pltpu.make_async_remote_copy(
                src_ref=src,
                dst_ref=dst,
                send_sem=refs["ar_send"].at[sems, used[0]],
                recv_sem=refs["ar_recv"].at[sems, used[0]],
                device_id=dev,
                device_id_type=MESH,
            ).start()

        def land(held):
            for sem in ("ar_recv", "ar_send"):
                pltpu.make_async_copy(held, held, refs[sem].at[sems, used[0]]).wait()
            used[0] += 1

        mine_half = base + core * half
        mine_quarter = mine_half + near_at * quarter
        mine = mine_quarter + far_at * shard

        def fill(blocks):
            at = base
            for block in blocks:
                rows = block.shape[0] // 8
                ar[at : at + rows] = block.reshape(rows, 8, LANES)
                at += rows
            if at < base + units:
                ar[at : base + units] = jnp.zeros((base + units - at, 8, LANES), f32)
            ship(ar.at[pl.ds(base + (1 - core) * half, half)], pair_buf, pair_id)

        def to_near():
            land(pair_buf)
            ar[pl.ds(mine_half, half)] += pair_buf[...]
            for d, dev in enumerate(near_ids, 1):
                to = lax.rem(near_at + d, near)
                ship(ar.at[pl.ds(mine_half + to * quarter, quarter)], near_buf.at[near - 1 - d], dev)

        def to_far():
            land(near_buf)
            got = ar[pl.ds(mine_quarter, quarter)]
            for d in range(near - 1):
                got = got + near_buf[d]
            ar[pl.ds(mine_quarter, quarter)] = got
            for d, dev in enumerate(far_ids, 1):
                to = lax.rem(far_at + d, far)
                ship(ar.at[pl.ds(mine_quarter + to * shard, shard)], far_buf.at[far - 1 - d], dev)

        def spread_far():
            land(far_buf)
            got = ar[pl.ds(mine, shard)]
            for d in range(far - 1):
                got = got + far_buf[d]
            whole[pl.ds(mine, shard)] = got
            for dev in far_ids:
                ship(whole.at[pl.ds(mine, shard)], whole.at[pl.ds(mine, shard)], dev)

        def spread_near():
            land(far_buf)
            at = pl.ds(mine_quarter, quarter)
            for dev in near_ids:
                ship(whole.at[at], whole.at[at], dev)

        def spread_pair():
            land(near_buf)
            at = pl.ds(mine_half, half)
            ship(whole.at[at], whole.at[at], pair_id)

        def done():
            land(pair_buf)
            sums = pltpu.make_async_copy(
                whole.at[pl.ds(base, units)], sums_out.at[pl.ds(base, units)], refs["sum_sem"].at[sems]
            )
            sums.start()
            return sums

        def near_only():
            land(near_buf)
            got = ar[pl.ds(mine, shard)]
            for d in range(near - 1):
                got = got + near_buf[d]
            whole[pl.ds(mine, shard)] = got
            for dev in near_ids:
                ship(whole.at[pl.ds(mine, shard)], whole.at[pl.ds(mine, shard)], dev)

        if far == 1:
            return fill, iter((to_near, near_only, spread_pair, done))
        return fill, iter((to_near, to_far, spread_far, spread_near, spread_pair, done))

    for name in ("acc2", "acc3", "acc_o1", "acc_o2", "total"):
        refs[name][...] = jnp.zeros_like(refs[name])
    none = jnp.zeros((2 * M, LANES), bf16)
    for g in range(G):
        for name in ("d2", "d3"):
            refs[name][g][0] = none
            refs[name][g][H + 1] = none

    every = range(G)
    moving, ended = {}, []

    def advance(*names):
        for name in names:
            if name not in moving:
                continue
            copy = next(moving[name])()
            if copy is not None:
                ended.append(copy)
                del moving[name]

    def reduce(name, blocks):
        fill, moving[name] = reducer(name)
        fill(blocks)

    def wide_blocks(value):
        return [value[:, h * LANES : (h + 1) * LANES] for h in range(sz.wide // LANES)]

    def mid_blocks(acc):
        value = acc[...]
        rest = value[:, LANES:]
        return [value[:, :LANES], cat([rest[: n3 // 2], rest[n3 // 2 :]], 1)]

    greet()
    prepare()
    for g in every:
        for k in range(2 * NB):
            if (g, k) != (0, 0):
                in_copy(x_hbm, 0, g, k).start()
    for g in every:
        before, body, after = conv_first(g)
        if g == 0:
            run((before, body, nothing))
            pl.semaphore_wait(barrier, len(partners))
            after()
        else:
            run((before, body, after))
    for g in every:
        run(after_first(g))
        if g == 0:
            prepare_rest()
            refs["acc1"][...] = jnp.zeros_like(refs["acc1"])
    for g in every:
        run(spread(1, g, refs["p1"][g]))
        run(second(g), flat=True)
    for g in every:
        run(spread(2, g, refs["p2"][g]))
        run(third(g), out_layer(g))
    for g in every:
        run(spread(3, g, refs["q"][g]), mid_kernel_grad(g, refs["p2"][g], refs["d3"][g], refs["acc3"]))
        run(back_layer(4, g, t3, refs["d2"][g], refs["total"].at[1], refs["slope2"][g]), flat=True)
    for g in every:
        run(spread(4, g, refs["q"][g]), mid_kernel_grad(g, refs["p1"][g], refs["d2"][g], refs["acc2"]))
        if g == G - 1:
            upper, lower = refs["acc_o1"][...], refs["acc_o2"][...]
            outs = cat([upper[:M] + upper[M : 2 * M] + lower[:M], upper[2 * M :] + lower[M:]], 0)
            reduce("rest", wide_blocks(outs) + mid_blocks(refs["acc3"]) + mid_blocks(refs["acc2"]))
        run(back_layer(5, g, t2, None, refs["total"].at[0], refs["slope1"][g]), flat=True)
    advance("rest")
    lane = lax.broadcasted_iota(jnp.int32, (1, LANES), 1)
    sums = [jnp.sum(refs["total"][i], axis=1, keepdims=True) for i in range(3)]
    biases = jnp.where(lane == 0, sums[0], jnp.where(lane == 1, sums[1], sums[2]))
    for g in every:
        run(spread(5, g, refs["q"][g]), flat=True)
        run(first_kernel_grad(g), steps=2 * NB)
        if g < G - 1:
            advance("rest")
    reduce("taps", wide_blocks(refs["acc1"]) + [biases])
    advance("rest", "taps")
    for g in every:
        run(input_grad(g), steps=2 * NB)
        advance("rest", "taps")
    while moving:
        advance(*list(moving))

    for copy in ended:
        copy.wait()
    for slot in range(2):
        cotangent(slot, slot).wait()
    for g in every:
        for k in range(2 * NB):
            again(g, k)[1].wait()
    for g in every:
        for e in range(EXCHANGES - 2, EXCHANGES):
            for kind in range(2):
                landed(e, g, kind, "send")


def call_a(sz, x, dy, heights, widths, k1, k2, k3, ko, b1, b2, b3):
    G, H, W, M, N = sz.groups, sz.height, sz.width, sz.mid, LANES
    n3 = 3 * M
    names, shapes = [], []

    def add(name, *what):
        names.append((name, len(what)))
        shapes.extend(what)

    def per_group(name, shape, dtype):
        add(name, *[pltpu.VMEM(shape, dtype) for _ in range(G)])

    add("buf", pltpu.VMEM((sz.images, H, W, sz.wide), f32))
    per_group("a0", (H, N, 2 * sz.wide), bf16)
    per_group("act", (H, M, N), f32)
    per_group("carry", (2, n3, N), f32)
    for name in ("slope1", "slope2"):
        per_group(name, (H, M, N), f32)
    per_group("slope3", (H + 2, M, N), f32)
    for name in ("p1", "p2", "q"):
        per_group(name, (H + 2, 2 * n3, N), bf16)
    for name in ("d3", "d2"):
        per_group(name, (H + 2, 2 * M, N), bf16)
    add("a3", pltpu.VMEM((2, sz.block, 2 * M, N), bf16))
    add("w1", pltpu.VMEM((9 * M, 3 * sz.wide), bf16))
    for name in ("w2", "w3", "t2", "t3"):
        add(name, pltpu.VMEM((2 * n3, n3), bf16))
    add("ko", pltpu.VMEM((2 * M, sz.wide), bf16))
    add("met", pltpu.VMEM((G, M, N), f32))
    add("bias", pltpu.VMEM((3, M, N), f32))
    E = EXCHANGES
    add("rim", pltpu.VMEM((G, 2, M, N), f32))
    add("msg", pltpu.VMEM((2, G, M, N), f32))
    add("rowmsg", pltpu.VMEM((2, G, 2, M, N), f32))
    add("cormsg", pltpu.VMEM((2, G, 2, 8, N), f32))
    add("sideway", pltpu.VMEM((2, G, 2, M, N), f32))
    add("updown", pltpu.VMEM((2, G, 2 * M + 32, N), f32))
    add("acc1", pltpu.VMEM((9 * M, sz.wide), f32))
    add("acc2", pltpu.VMEM((n3, n3), f32))
    add("acc3", pltpu.VMEM((n3, n3), f32))
    add("acc_o1", pltpu.VMEM((2 * M + 16, sz.wide), f32))
    add("acc_o2", pltpu.VMEM((M + 16, sz.wide), f32))
    add("total", pltpu.VMEM((3, M, N), f32))
    U = sz.units
    add("ar", pltpu.VMEM((U, 8, N), f32))
    add("ar_all", pltpu.VMEM((U, 8, N), f32))
    for part, (_, units, shard) in sz.parts.items():
        near = sz.cols // 2 * sz.lows[part]
        far = sz.rows // sz.lows[part]
        add("pair_" + part, pltpu.VMEM((units // 2, 8, N), f32))
        add("near_" + part, pltpu.VMEM((max(near - 1, 1), units // 2 // near, 8, N), f32))
        add("far_" + part, pltpu.VMEM((max(far - 1, 1), shard, 8, N), f32))
    add("sum_sem", pltpu.SemaphoreType.DMA((len(sz.parts),)))
    add("in_sem", pltpu.SemaphoreType.DMA((2, G, 2 * sz.blocks)))
    add("k1_sem", pltpu.SemaphoreType.DMA)
    for name, value in zip(SMALL, (k2, k3, ko, b1, b2, b3)):
        add(name, pltpu.VMEM(value.shape, f32))
    add("small_sem", pltpu.SemaphoreType.DMA((len(SMALL),)))
    add("again_sem", pltpu.SemaphoreType.DMA((2, G, 2 * sz.blocks)))
    add("ring_sem", pltpu.SemaphoreType.DMA((2,)))
    add("ring", pltpu.VMEM((2, sz.per_group, sz.block // 4, W, sz.wide), f32))
    add("inside", pltpu.VMEM((sz.images, W, N), f32))
    add("wb", pltpu.VMEM((sz.wide, 9 * n3), bf16))
    add("out_sem", pltpu.SemaphoreType.DMA((G, sz.blocks)))
    add("send", pltpu.SemaphoreType.DMA((E, G, 2)))
    add("recv", pltpu.SemaphoreType.DMA((E, G, 2)))
    add("ar_send", pltpu.SemaphoreType.DMA((len(sz.parts), 6)))
    add("ar_recv", pltpu.SemaphoreType.DMA((len(sz.parts), 6)))
    grouped = ("a0", "act", "carry", "slope1", "slope2", "slope3", "p1", "p2", "q", "d3", "d2")

    def whole_kernel(*args):
        refs = {"io": args[:14]}
        at = 14
        for name, size in names:
            held = args[at : at + size]
            refs[name] = held if name in grouped else held[0]
            at += size
        kernel_a(sz, refs)

    hbm = pl.BlockSpec(memory_space=pl.ANY)
    vmem = pl.BlockSpec(memory_space=pltpu.VMEM)
    smem = pl.BlockSpec(memory_space=pltpu.SMEM)
    return pl.pallas_call(
        whole_kernel,
        out_shape=(
            jax.ShapeDtypeStruct(x.shape, f32),
            jax.ShapeDtypeStruct((G, H, 2 * M, N), bf16),
            jax.ShapeDtypeStruct((U, 8, N), f32),
        ),
        in_specs=[hbm, hbm, smem, smem] + [hbm] * 7,
        out_specs=(hbm, hbm, hbm),
        scratch_shapes=shapes,
        compiler_params=pltpu.CompilerParams(
            collective_id=0, has_side_effects=True, vmem_limit_bytes=63 * 2**20
        ),
        name="block_chain",
    )(x, dy, heights, widths, k1, k2, k3, ko, b1, b2, b3)


def kernel_b(
    sz, rows, x_hbm, g_hbm, a3_hbm, sums_hbm, ko_hbm, bo, out_hbm, grad_hbm, g1_hbm, g2_hbm, g3_hbm, go_hbm, s1, s2, s3, so,
    x, grad, a3, sums, ko, wo, g1, g2, g3, go, in_sem, out_sem, sums_sem,
):
    G, W, M = sz.groups, sz.width, sz.mid
    n3 = 3 * M
    chunks = sz.height // rows

    def copies_in(c):
        at = (slice(None), pl.ds(c * rows, rows))
        pairs = ((a3_hbm, a3), (x_hbm, x), (g_hbm, grad))
        return [pltpu.make_async_copy(s.at[at], d.at[at], in_sem.at[i, c]) for i, (s, d) in enumerate(pairs)]

    def copies_out(c):
        at = (slice(None), pl.ds(c * rows, rows))
        return [
            pltpu.make_async_copy(grad.at[at], grad_hbm.at[at], out_sem.at[0, c]),
            pltpu.make_async_copy(x.at[at], out_hbm.at[at], out_sem.at[1, c]),
        ]

    early = pltpu.make_async_copy(ko_hbm, ko, sums_sem.at[0])
    sums_in = pltpu.make_async_copy(sums_hbm, sums, sums_sem.at[1])
    sums_out = [
        pltpu.make_async_copy(s, d, sums_sem.at[2 + i])
        for i, (s, d) in enumerate(((g1, g1_hbm), (g2, g2_hbm), (g3, g3_hbm), (go, go_hbm)))
    ]
    early.start()
    for c in range(chunks):
        for copy in copies_in(c):
            copy.start()
        if c == 0:
            sums_in.start()
    early.wait()
    hi, lo = halves(ko[...].T * GAIN)
    wo[...] = cat([hi, hi, lo], 1)
    add = bo[...] * GAIN

    def body(c, carry):
        a3_in, x_in, grad_in = copies_in(c)
        grad_out, x_out = copies_out(c)
        a3_in.wait()
        x_in.wait()
        for k in range(rows):
            i = c * rows + k
            act = cat([a3[g, i] for g in range(G)], 1)
            branch = dot(wo[...], cat([act, act[:M]], 0)).T
            for n in range(sz.images):
                x[n, i] = x[n, i] + (branch[n * W : (n + 1) * W] + add)
        x_out.start()
        grad_in.wait()
        grad_out.start()
        return carry

    def take(at, count):
        return sums[at : at + count].reshape(count * 8, LANES)

    lax.fori_loop(0, chunks - 1, body, 0)

    sums_in.wait()
    at = sz.parts["taps"][0]
    for h in range(sz.wide // LANES):
        part = take(at, 9 * M // 8)
        at += 9 * M // 8
        for t in range(3):
            for b in range(3):
                lo = (t * 3 + b) * M
                g1[2 - t, 2 - b, :, h * LANES : (h + 1) * LANES] = part[lo : lo + M]
    rest = take(at, M // 8).T
    s1[...] = rest[0:1]
    s2[...] = rest[1:2]
    s3[...] = rest[2:3]
    at = sz.parts["rest"][0]
    for h in range(sz.wide // LANES):
        part = take(at, (M + 16) // 8)
        at += (M + 16) // 8
        go[:, h * LANES : (h + 1) * LANES] = part[:M]
        so[:, h * LANES : (h + 1) * LANES] = part[M : M + 1]
    for ref in (g3, g2):
        big, rest = take(at, n3 // 8), take(at + n3 // 8, n3 // 16)
        at += n3 // 8 + n3 // 16
        rest = cat([rest[:, :M], rest[:, M:]], 0)
        for b in range(3):
            sl = slice(b * M, (b + 1) * M)
            ref[0, b] = big[sl, :M]
            ref[1, b] = big[sl, M:]
            ref[2, b] = rest[sl]
    for copy in sums_out:
        copy.start()

    lax.fori_loop(chunks - 1, chunks, body, 0)

    def finish(c, carry):
        for copy in copies_out(c):
            copy.wait()
        return carry

    lax.fori_loop(0, chunks, finish, 0)
    for copy in sums_out:
        copy.wait()


def call_b(sz, x, grad, a3, sums, ko, bo):
    M = sz.mid
    rows = 8
    hbm = pl.BlockSpec(memory_space=pl.ANY)
    vmem = pl.BlockSpec(memory_space=pltpu.VMEM)
    grads = ((3, 3, M, sz.wide), (3, 3, M, M), (3, 3, M, M), (M, sz.wide))
    small = ((1, M), (1, M), (1, M), (1, sz.wide))
    return pl.pallas_call(
        functools.partial(kernel_b, sz, rows),
        out_shape=tuple(jax.ShapeDtypeStruct(s, f32) for s in (x.shape, x.shape) + grads + small),
        in_specs=[hbm] * 5 + [vmem],
        out_specs=(hbm,) * 6 + (vmem,) * 4,
        scratch_shapes=[
            pltpu.VMEM(x.shape, f32),
            pltpu.VMEM(x.shape, f32),
            pltpu.VMEM(a3.shape, bf16),
            pltpu.VMEM(sums.shape, f32),
            pltpu.VMEM(ko.shape, f32),
            pltpu.VMEM((sz.wide, 3 * M), bf16),
        ]
        + [pltpu.VMEM(s, f32) for s in grads]
        + [
            pltpu.SemaphoreType.DMA((3, sz.height // rows)),
            pltpu.SemaphoreType.DMA((2, sz.height // rows)),
            pltpu.SemaphoreType.DMA((6,)),
        ],
        compiler_params=pltpu.CompilerParams(vmem_limit_bytes=60 * 2**20),
        name="wide_outputs",
    )(x, grad, a3, sums, ko, bo)


def body(rows, cols, x, k1, b1, k2, b2, k3, b3, ko, bo, dy, heights, widths):
    wide, mid = k1.shape[2:]
    sz = Sizes(x.shape, mid, rows, cols)
    k1 = jnp.swapaxes(k1, 2, 3)
    grad, a3, sums = call_a(
        sz, x, dy, heights, widths, k1.reshape(9 * mid, wide), k2, k3, ko, b1[None], b2[None], b3[None]
    )
    out, grad, g1, g2, g3, go, s1, s2, s3, so = call_b(sz, x, grad, a3, sums, ko, bo[None])
    return (
        out,
        grad,
        jnp.swapaxes(g1, 2, 3),
        s1.reshape(mid),
        g2,
        s2.reshape(mid),
        g3,
        s3.reshape(mid),
        go,
        so.reshape(wide),
    )


def solution(mesh):
    tiled = P(None, "rows", "cols", None)
    return jax.shard_map(
        functools.partial(body, mesh.shape["rows"], mesh.shape["cols"]),
        mesh=mesh,
        in_specs=(tiled,) + (P(),) * 8 + (tiled, P(), P()),
        out_specs=(tiled, tiled) + (P(),) * 8,
        check_vma=False,
    )
```

```python
import functools

import jax
import jax.numpy as jnp
from jax import lax
from jax.experimental import pallas as pl
from jax.experimental.pallas import tpu as pltpu
from jax.sharding import PartitionSpec as P

MESH = pl.DeviceIdType.MESH
bf16 = jnp.bfloat16
f32 = jnp.float32
LANES = 128
NN = (((1,), (0,)), ((), ()))
NT = (((1,), (1,)), ((), ()))
GAIN = 1.0 / 64.0
EXCHANGES = 6
GOES = ((0, 1), (0, -1), (1, 0), (-1, 0), (1, 1), (1, -1), (-1, 1), (-1, -1))


SMALL = ("k2", "k3", "ko_in", "b1", "b2", "b3")


def dot(a, b, dims=NN):
    return lax.dot_general(a, b, dims, preferred_element_type=f32)


def halves(v):
    hi = v.astype(bf16)
    return hi, (v - hi.astype(f32)).astype(bf16)


def sigmoid(v):
    return 0.5 + 0.5 * jnp.tanh(0.5 * v)


def cat(parts, axis):
    return jnp.concatenate(parts, axis=axis)


def lane_column(width):
    return lax.broadcasted_iota(jnp.int32, (1, LANES), 1) % width


class Sizes:
    def __init__(self, shape, mid, rows, cols):
        self.images, self.height, self.width, self.wide = shape
        self.mid = mid
        self.rows, self.cols = rows, cols
        self.per_group = LANES // self.width
        self.groups = self.images // self.per_group
        self.block = min(16, self.height)
        self.blocks = self.height // self.block
        self.devices = rows * cols
        self.lows = dict(taps=min(rows, max(16 // (cols // 2), 1)), rest=2)
        half = 3 * mid // 8
        self.counts = dict(
            taps=9 * mid // 8 * (self.wide // LANES) + mid // 8,
            rest=(mid + 16) // 8 * (self.wide // LANES) + 2 * (half + half // 2),
        )
        self.parts, at = {}, 0
        for name, used in self.counts.items():
            shard = -(-used // self.devices)
            self.parts[name] = (at, shard * self.devices, shard)
            at += shard * self.devices
        self.units = at


def kernel_a(sz, refs):
    x_hbm, dy_hbm, heights, widths, k1 = refs["io"][:5]
    grad_hbm, a3_hbm, sums_out = refs["io"][11:]
    k2, k3, ko_in, b1, b2, b3 = [refs[n] for n in SMALL]
    w1, w2, w3, t3, t2, ko, bias = [refs[n] for n in ("w1", "w2", "w3", "t3", "t2", "ko", "bias")]
    G, H, W, M = sz.groups, sz.height, sz.width, sz.mid
    RB, NB = sz.block, sz.blocks
    me_r, me_c = lax.axis_index("rows"), lax.axis_index("cols")
    col = lane_column(W)
    first, last = col == 0, col == W - 1
    ends = first | last
    even = col % 2 == 0
    n3 = 3 * M

    has_up, has_down = me_r > 0, me_r < sz.rows - 1
    has_left, has_right = me_c > 0, me_c < sz.cols - 1

    row_at = {d: lax.rem(me_r + d + sz.rows, sz.rows) if d else me_r for d in (-1, 0, 1)}
    col_at = {d: lax.rem(me_c + d + sz.cols, sz.cols) if d else me_c for d in (-1, 0, 1)}

    def neighbour(dr, dc):
        return row_at[dr], col_at[dc]

    buf = refs["buf"]
    half_rows = RB // 2

    def in_copy(src, which, g, k):
        n0 = g * sz.per_group
        return pltpu.make_async_copy(
            src.at[pl.ds(n0, sz.per_group), pl.ds(k * half_rows, half_rows)],
            buf.at[pl.ds(n0, sz.per_group), pl.ds(k * half_rows, half_rows)],
            refs["in_sem"].at[which, g, k],
        )

    in_copy(x_hbm, 0, 0, 0).start()

    k1_copy = pltpu.make_async_copy(k1, refs["acc1"], refs["k1_sem"])
    k1_copy.start()
    small_copies = [
        pltpu.make_async_copy(src, refs[n], refs["small_sem"].at[i])
        for i, (n, src) in enumerate(zip(SMALL, refs["io"][5:11]))
    ]
    for copy in small_copies:
        copy.start()

    def prepare():
        k1_copy.wait()
        hi, lo = halves(refs["acc1"][...])
        w1[...] = cat([hi, hi, lo], 1)
        for copy in small_copies:
            copy.wait()
        for i, b in enumerate((b1, b2, b3)):
            bias[i] = jnp.broadcast_to(b[...], (LANES, M)).T

    def prepare_rest():
        back = refs["acc1"][...].reshape(3, 3, M, sz.wide)
        for p in range(3):
            hi, lo = halves(cat([back[2 - p, 2 - b].T for b in range(3)], 1))
            refs["wb"][:, 2 * p * n3 : 2 * (p + 1) * n3] = cat([hi, hi], 1)
            refs["wb"][:, (6 + p) * n3 : (7 + p) * n3] = lo
        across = lax.broadcasted_iota(jnp.int32, (W, LANES), 0) + me_c * W
        for n in range(sz.images):
            refs["inside"][n] = jnp.where(across < widths[n], 1.0, 0.0)
        ko[:M], ko[M:] = halves(ko_in[...])
        for k, fwd, back in ((k2, w2, t2), (k3, w3, t3)):
            for p in range(3):
                at = slice(p * M, (p + 1) * M)
                hi, lo = halves(cat([k[p, q].T for q in range(3)], 1))
                fwd[at], fwd[n3 + p * M : n3 + (p + 1) * M] = hi, lo
                hi, lo = halves(cat([k[2 - p, 2 - q] for q in range(3)], 1))
                back[at], back[n3 + p * M : n3 + (p + 1) * M] = hi, lo

    core, rest = me_c % 2, me_c // 2
    pair_id = (me_r, me_c + 1 - 2 * core)

    def levels(name):
        low_count = sz.lows[name]
        near, far = sz.cols // 2 * low_count, sz.rows // low_count
        low, far_at = me_r % low_count, me_r // low_count
        near_at = rest * low_count + low
        near_ids = []
        for d in range(1, near):
            k = lax.rem(near_at + d, near)
            near_ids.append((far_at * low_count + k % low_count, (k // low_count) * 2 + core))
        far_ids = [(lax.rem(far_at + d, far) * low_count + low, me_c) for d in range(1, far)]
        return near, far, near_at, far_at, near_ids, far_ids

    barrier = pltpu.get_barrier_semaphore()
    near_ids, far_ids = levels("taps")[4:]
    if far_ids:
        partners = [pair_id] + [neighbour(dr, dc) for dr, dc in GOES] + near_ids + far_ids
        partners += [dev for ids in levels("rest")[4:] for dev in ids]
    else:
        partners = near_ids + [neighbour(dr, dc) for dr, dc in GOES if dc]

    def greet():
        for dev in partners:
            pl.semaphore_signal(barrier, inc=1, device_id=dev, device_id_type=MESH)

    def message(e, g, slot):
        dr, dc = GOES[slot]
        at = (e % 2, g)
        if slot < 2:
            src, dst = refs["msg"].at[at], refs["sideway"].at[(*at, slot)]
        elif slot < 4:
            src = refs["rowmsg"].at[(*at, 3 - slot)]
            dst = refs["updown"].at[(*at, pl.ds((slot - 2) * M, M))]
        else:
            src = refs["cormsg"].at[(*at, 1 if dr > 0 else 0)]
            dst = refs["updown"].at[(*at, pl.ds(2 * M + 8 * (slot - 4), 8))]
        kind = 0 if slot < 2 else 1
        return pltpu.make_async_remote_copy(
            src_ref=src,
            dst_ref=dst,
            send_sem=refs["send"].at[e, g, kind],
            recv_sem=refs["recv"].at[e, g, kind],
            device_id=neighbour(dr, dc),
            device_id_type=MESH,
        )

    def landed(e, g, kind, sem):
        held = refs["updown" if kind else "sideway"].at[e % 2, g]
        pltpu.make_async_copy(held, held, refs[sem].at[e, g, kind]).wait()

    def send(e, g, top, bottom, top_rim, bottom_rim):
        for slot in (0, 1):
            message(e, g, slot).start()
        refs["rowmsg"][e % 2, g, 0] = top
        refs["rowmsg"][e % 2, g, 1] = bottom
        for slot in (2, 3):
            message(e, g, slot).start()
        refs["cormsg"][e % 2, g, 0] = pack_corner(top_rim)
        refs["cormsg"][e % 2, g, 1] = pack_corner(bottom_rim)
        for slot in (4, 5, 6, 7):
            message(e, g, slot).start()

    def reuse(e, g):
        if e >= 2:
            for kind in range(2):
                landed(e - 2, g, kind, "send")

    def receive(e, g, kind):
        landed(e, g, kind, "recv")

    def pack(held, value, u):
        moved = pltpu.roll(value, lax.rem(LANES + 1 + 2 * u, LANES), 1)
        return jnp.where(col // 2 == u, moved, held)

    def pack_corner(value):
        held = jnp.zeros((8, LANES), f32)
        for k in range(M // 8):
            held = jnp.where(col // 2 == k, pltpu.roll(value[8 * k : 8 * k + 8], 1 + 2 * k, 1), held)
        return held

    def beyond(e, g, lower):
        row = refs["updown"][e % 2, g, pl.ds(M if lower else 0, M)]
        at = 2 if lower else 0
        there = has_down if lower else has_up
        left = jnp.where(there & has_left, corner_left(refs["updown"][e % 2, g, pl.ds(2 * M + 8 * at, 8)]), 0.0)
        right = jnp.where(there & has_right, corner_right(refs["updown"][e % 2, g, pl.ds(2 * M + 8 * (at + 1), 8)]), 0.0)
        return jnp.where(there, row, 0.0), jnp.where(first, left, right)

    def meet(e, g):
        left = jnp.where(has_left, refs["sideway"][e % 2, g, 0], 0.0)
        right = jnp.where(has_right, refs["sideway"][e % 2, g, 1], 0.0)
        refs["met"][g] = jnp.where(even, left, pltpu.roll(right, (2 * W - 2) % LANES, 1))

    def from_sides(held, u):
        return pltpu.roll(held, LANES - W - 2 * u, 1)

    def corner_left(held):
        return cat([pltpu.roll(held, LANES - W - 2 * k, 1) for k in range(M // 8)], 0)

    def corner_right(held):
        return cat([pltpu.roll(held, W - 2 - 2 * k, 1) for k in range(M // 8)], 0)

    def nothing():
        pass

    def run(*phases, steps=NB, flat=False):
        for before, _, _ in phases:
            before()

        def step(b, carry):
            for _, body, _ in phases:
                body(b)
            return carry

        if flat:
            for b in range(steps):
                step(b, 0)
        else:
            lax.fori_loop(0, steps, step, 0)
        for _, _, after in phases:
            after()

    def conv_first(g):
        a0, z, carry = refs["a0"][g], refs["slope3"][g], refs["carry"][g]

        def before():
            carry[...] = jnp.zeros_like(carry)
            refs["msg"][0, g] = jnp.zeros((M, LANES), f32)

        def emit(row, s, held):
            s0, s1, s2 = s[:M], s[M : 2 * M], s[2 * M :]
            value = s1 + jnp.where(first, 0.0, pltpu.roll(s0, 1, 1))
            value = value + jnp.where(last, 0.0, pltpu.roll(s2, LANES - 1, 1))
            z[row + 1] = value
            rim = jnp.where(first, s2, s0)
            return rim, pack(held, rim, row)

        def body(b):
            held = refs["msg"][0, g]
            c0, c1 = carry[0], carry[1]
            for m in range(RB // 2):
                r = b * RB + 2 * m
                if 2 * m % half_rows == 0:
                    in_copy(x_hbm, 0, g, 2 * b + 2 * m // half_rows).wait()
                pair = []
                for i in range(2):
                    v = cat([buf[g * sz.per_group + s, r + i] for s in range(sz.per_group)], 0)
                    hi, lo = halves(v * sigmoid(v))
                    both = cat([hi, lo], 1)
                    a0[r + i] = both
                    pair.append(both)
                rhs = cat(pair, 0)
                y = dot(w1[...], cat([rhs, rhs[:, : sz.wide]], 1), NT)
                ya, yb = y[:, :LANES], y[:, LANES:]
                rim, held = emit(r - 1, c0 + ya[2 * n3 :], held)
                if m == 0:
                    refs["rim"][g, jnp.minimum(b, 1)] = rim
                _, held = emit(r, c1 + ya[n3 : 2 * n3] + yb[2 * n3 :], held)
                c0, c1 = ya[:n3] + yb[n3 : 2 * n3], yb[:n3]
            carry[0] = c0
            carry[1] = c1
            refs["msg"][0, g] = held

        def after():
            _, held = emit(H - 1, carry[0], refs["msg"][0, g])
            rim, _ = emit(H, carry[1], held)
            refs["msg"][0, g] = held
            for k in range(2 * NB):
                in_copy(dy_hbm, 1, g, k).start()
            send(0, g, z[0], z[H + 1], refs["rim"][g, 0], rim)

        return before, body, after

    def after_first(g):
        z, act, slope = refs["slope3"][g], refs["act"][g], refs["slope1"][g]
        def before():
            receive(0, g, 0)
            meet(0, g)
            refs["msg"][1, g] = jnp.zeros((M, LANES), f32)

        def emit(r, v, held):
            v = v + bias[0]
            sig = sigmoid(v)
            a = v * sig
            slope[r] = sig + a * (1.0 - sig)
            act[r] = a
            return pack(held, a, r)

        def with_sides(r):
            return z[r + 1] + jnp.where(ends, from_sides(refs["met"][g], r), 0.0)

        def body(b):
            held = refs["msg"][1, g]
            for k in range(RB):
                r = b * RB + k
                held = emit(r, with_sides(r), held)
            refs["msg"][1, g] = held

        def after():
            receive(0, g, 1)
            held = refs["msg"][1, g]
            for r, lower in ((0, False), (H - 1, True)):
                row, sides = beyond(0, g, lower)
                held = emit(r, with_sides(r) + row + jnp.where(ends, sides, 0.0), held)
            refs["msg"][1, g] = held
            send(1, g, act[0], act[H - 1], act[0], act[H - 1])

        return before, body, after

    def spread(e, g, dst):
        act = refs["act"][g]

        def before():
            receive(e, g, 0)
            meet(e, g)

        def store(row, v, left, right):
            before = jnp.where(first, left, pltpu.roll(v, 1, 1))
            behind = jnp.where(last, right, pltpu.roll(v, LANES - 1, 1))
            for at, part in enumerate((before, v, behind)):
                hi, lo = halves(part)
                dst[row, at * M : (at + 1) * M] = hi
                dst[row, n3 + at * M : n3 + (at + 1) * M] = lo

        def body(b):
            both = refs["met"][g]
            for k in range(RB):
                r = b * RB + k
                sides = from_sides(both, r)
                store(r + 1, act[r], sides, sides)

        def after():
            receive(e, g, 1)
            for at, lower in ((0, False), (H + 1, True)):
                row, sides = beyond(e, g, lower)
                store(at, row, sides, sides)

        return before, body, after

    def conv_mid(g, src, weight, emit, begin, end):
        carry = refs["carry"][g]

        def pair(m):
            rhs = cat([src[2 * m], src[2 * m + 1]], 1)
            y = dot(weight[...], rhs[:n3])
            y = y[:n3] + y[n3:] + dot(weight[:n3], rhs[n3:])
            return y[:, :LANES], y[:, LANES:]

        def before():
            ya, yb = pair(0)
            carry[0, :M] = ya[:M] + yb[M : 2 * M]
            carry[1, :M] = yb[:M]

        def body(b):
            state = begin(b)
            c0, c1 = carry[0, :M], carry[1, :M]
            for k in range(RB // 2):
                ya, yb = pair(1 + b * (RB // 2) + k)
                r = b * RB + 2 * k
                state = emit(r, c0 + ya[2 * M :], state)
                state = emit(r + 1, c1 + ya[M : 2 * M] + yb[2 * M :], state)
                c0, c1 = ya[:M] + yb[M : 2 * M], yb[:M]
            carry[0, :M] = c0
            carry[1, :M] = c1
            end(b, state)

        return before, body

    def second(g):
        act, slope = refs["act"][g], refs["slope2"][g]

        def clear():
            reuse(2, g)
            refs["msg"][0, g] = jnp.zeros((M, LANES), f32)

        def emit(r, v, held):
            v = v + bias[1]
            sig = sigmoid(v)
            a = v * sig
            slope[r] = sig + a * (1.0 - sig)
            act[r] = a
            return pack(held, a, r)

        def end(b, held):
            refs["msg"][0, g] = held

        before, body = conv_mid(g, refs["p1"][g], w2, emit, lambda b: refs["msg"][0, g], end)
        return (lambda: (clear(), before())), body, lambda: send(2, g, act[0], act[H - 1], act[0], act[H - 1])

    def a3_copy(g, b):
        return pltpu.make_async_copy(
            refs["a3"].at[b % 2], a3_hbm.at[g, pl.ds(b * RB, RB)], refs["out_sem"].at[g, b]
        )

    def third(g):
        a3, slope = refs["a3"], refs["slope3"][g]

        def emit(r, v, state):
            v = v + bias[2]
            sig = sigmoid(v)
            a = v * sig
            slope[r] = sig + a * (1.0 - sig)
            hi, lo = halves(a)
            k = r - state * RB
            a3[state % 2, k, :M] = hi
            a3[state % 2, k, M:] = lo
            return state

        def begin(b):
            if NB > 2:

                @pl.when(b >= 2)
                def _():
                    a3_copy(g, b - 2).wait()

            return b

        before, body = conv_mid(g, refs["p2"][g], w3, emit, begin, lambda b, s: a3_copy(g, b).start())

        def after():
            for k in range(max(NB - 2, 0), NB):
                a3_copy(g, k).wait()

        return before, body, after

    ring_rows = half_rows // 2
    ring_count = H // ring_rows

    def again(g, k):
        at = (pl.ds(g * sz.per_group, sz.per_group), pl.ds(k * half_rows, half_rows))
        return (
            pltpu.make_async_copy(x_hbm.at[at], buf.at[at], refs["again_sem"].at[0, g, k]),
            pltpu.make_async_copy(buf.at[at], grad_hbm.at[at], refs["again_sem"].at[1, g, k]),
        )

    def cotangent(t, slot):
        t = lax.rem(t, G * ring_count)
        at = (
            pl.ds(t // ring_count * sz.per_group, sz.per_group),
            pl.ds(lax.rem(t, ring_count) * ring_rows, ring_rows),
        )
        return pltpu.make_async_copy(dy_hbm.at[at], refs["ring"].at[slot], refs["ring_sem"].at[slot])

    def masked(value, s, n, r):
        keep = refs["inside"][n] * jnp.where(me_r * H + r < heights[n], 1.0, 0.0)
        return value * cat([keep] * (sz.wide // LANES), 1)

    def input_grad(g):
        q, wb = refs["q"][g], refs["wb"]

        def body(b):
            again(g, b)[0].wait()
            for m in range(half_rows // 2):
                r = b * half_rows + 2 * m
                t = g * ring_count + 2 * b + 2 * m // ring_rows
                slot, at_row = 2 * m // ring_rows, 2 * m % ring_rows
                if at_row == 0:
                    cotangent(t, slot).wait()
                dy = refs["ring"].at[slot]
                three = [cat([q[r + s], q[r + 1 + s]], 1) for s in range(3)]
                y = dot(wb[...], cat(three + [t3[:n3] for t3 in three], 0)).T
                for i in range(2):
                    for s in range(sz.per_group):
                        n = g * sz.per_group + s
                        at = i * LANES + s * W
                        v = buf[n, r + i]
                        sig = sigmoid(v)
                        slope = sig * (1.0 + v * (1.0 - sig))
                        buf[n, r + i] = masked(dy[s, at_row + i], s, n, r + i) + y[at : at + W] * slope
                if at_row == ring_rows - 2:
                    cotangent(t + 2, slot).start()
            again(g, b)[1].start()

        return nothing, body, nothing

    def emit_grad(e, g, own, total, slope):
        act = refs["act"][g]

        def emit(r, v, state):
            held, summed = state
            d = v * slope[r]
            act[r] = d
            if own is not None:
                hi, lo = halves(d)
                own[r + 1, :M] = hi
                own[r + 1, M:] = lo
            return pack(held, d, r), summed + d

        def begin(b):
            return refs["msg"][e % 2, g], total[...]

        def end(b, state):
            refs["msg"][e % 2, g] = state[0]
            total[...] = state[1]

        def clear():
            reuse(e, g)
            refs["msg"][e % 2, g] = jnp.zeros((M, LANES), f32)

        return emit, begin, end, clear

    def out_layer(g):
        a3, act = refs["a3"], refs["act"][g]
        emit, begin, end, clear = emit_grad(3, g, refs["d3"][g], refs["total"].at[2], refs["slope3"][g])
        ones = jnp.ones((16, 2 * LANES), bf16)

        def body(b):
            for h in range(2):
                in_copy(dy_hbm, 1, g, 2 * b + h).wait()
            state = begin(b)
            upper, lower = refs["acc_o1"][...], refs["acc_o2"][...]
            for m in range(RB // 2):
                r = b * RB + 2 * m
                parts = []
                for i in range(2):
                    for s in range(sz.per_group):
                        n = g * sz.per_group + s
                        parts.append(masked(buf[n, r + i], s, n, r + i) * GAIN)
                hi, lo = halves(cat(parts, 0))
                y1 = dot(ko[...], hi, NT)
                y2 = dot(ko[:M], lo, NT)
                y = y1[:M] + y1[M:] + y2
                state = emit(r, y[:, :LANES], state)
                state = emit(r + 1, y[:, LANES:], state)
                act3 = cat([a3[b % 2, 2 * m], a3[b % 2, 2 * m + 1]], 1)
                upper = upper + dot(cat([act3, ones], 0), hi)
                lower = lower + dot(cat([act3[:M], ones], 0), lo)
            refs["acc_o1"][...] = upper
            refs["acc_o2"][...] = lower
            end(b, state)

        def after():
            send(3, g, act[0], act[H - 1], act[0], act[H - 1])
            for k in range(2 * NB):
                again(g, k)[0].start()
            if g == 0:
                for slot in range(2):
                    cotangent(slot, slot).start()

        return clear, body, after

    def back_layer(e, g, weight, own, total, slope):
        act = refs["act"][g]
        emit, begin, end, clear = emit_grad(e, g, own, total, slope)
        before, body = conv_mid(g, refs["q"][g], weight, emit, begin, end)
        return (lambda: (clear(), before())), body, lambda: send(e, g, act[0], act[H - 1], act[0], act[H - 1])

    def mid_kernel_grad(g, src, own, acc):
        def terms(rows, own_rows):
            left = cat(rows, 1)
            right = [cat(two, 1) for two in own_rows]
            hi = cat([two[:M] for two in right], 0)
            lo = cat([two[M:] for two in right], 0)
            return cat([left[:n3], left[:n3], left[n3:]], 1), cat([hi, lo, hi], 1)

        def body(b):
            ls, rs = [], []
            for m in range(RB // 2):
                r = b * RB + 2 * m
                l, rr = terms(
                    [src[r + 1], src[r + 2]], [[own[r + 2 - p], own[r + 3 - p]] for p in range(3)]
                )
                ls.append(l)
                rs.append(rr)
            acc[...] += dot(cat(ls, 1), cat(rs, 1), NT)

        def after():
            none = jnp.zeros((2 * M, LANES), bf16)
            l, rr = terms([src[0], src[H + 1]], [[own[1], none], [none, none], [none, own[H]]])
            acc[...] += dot(l, rr, NT)

        return nothing, body, after

    def first_kernel_grad(g):
        a0, q, acc = refs["a0"][g], refs["q"][g], refs["acc1"]

        def body(b):
            ls, rs = [], []
            for m in range(half_rows // 2):
                r = b * half_rows + 2 * m
                three = [cat([q[r + s], q[r + 1 + s]], 1) for s in range(3)]
                hi = cat([t[:n3] for t in three], 0)
                lo = cat([t[n3:] for t in three], 0)
                ls.append(cat([hi, hi, lo], 1))
                two = cat([a0[r], a0[r + 1]], 0)
                rs.append(cat([two[:, : sz.wide], two[:, sz.wide :], two[:, : sz.wide]], 0))
            for m in range(0, half_rows // 2, 2):
                acc[...] += dot(cat(ls[m : m + 2], 1), cat(rs[m : m + 2], 0))

        return nothing, body, nothing

    def reducer(name):
        base, units, shard = sz.parts[name]
        near, far, near_at, far_at, near_ids, far_ids = levels(name)
        half, quarter = units // 2, units // 2 // near
        ar, whole = refs["ar"], refs["ar_all"]
        sems = list(sz.parts).index(name)
        pair_buf = refs["pair_" + name]
        near_buf = refs["near_" + name]
        far_buf = refs["far_" + name]
        used = [0]

        def ship(src, dst, dev):
            pltpu.make_async_remote_copy(
                src_ref=src,
                dst_ref=dst,
                send_sem=refs["ar_send"].at[sems, used[0]],
                recv_sem=refs["ar_recv"].at[sems, used[0]],
                device_id=dev,
                device_id_type=MESH,
            ).start()

        def land(held):
            for sem in ("ar_recv", "ar_send"):
                pltpu.make_async_copy(held, held, refs[sem].at[sems, used[0]]).wait()
            used[0] += 1

        mine_half = base + core * half
        mine_quarter = mine_half + near_at * quarter
        mine = mine_quarter + far_at * shard

        def fill(blocks):
            at = base
            for block in blocks:
                rows = block.shape[0] // 8
                ar[at : at + rows] = block.reshape(rows, 8, LANES)
                at += rows
            if at < base + units:
                ar[at : base + units] = jnp.zeros((base + units - at, 8, LANES), f32)
            ship(ar.at[pl.ds(base + (1 - core) * half, half)], pair_buf, pair_id)

        def to_near():
            land(pair_buf)
            ar[pl.ds(mine_half, half)] += pair_buf[...]
            for d, dev in enumerate(near_ids, 1):
                to = lax.rem(near_at + d, near)
                ship(ar.at[pl.ds(mine_half + to * quarter, quarter)], near_buf.at[near - 1 - d], dev)

        def to_far():
            land(near_buf)
            got = ar[pl.ds(mine_quarter, quarter)]
            for d in range(near - 1):
                got = got + near_buf[d]
            ar[pl.ds(mine_quarter, quarter)] = got
            for d, dev in enumerate(far_ids, 1):
                to = lax.rem(far_at + d, far)
                ship(ar.at[pl.ds(mine_quarter + to * shard, shard)], far_buf.at[far - 1 - d], dev)

        def spread_far():
            land(far_buf)
            got = ar[pl.ds(mine, shard)]
            for d in range(far - 1):
                got = got + far_buf[d]
            whole[pl.ds(mine, shard)] = got
            for dev in far_ids:
                ship(whole.at[pl.ds(mine, shard)], whole.at[pl.ds(mine, shard)], dev)

        def spread_near():
            land(far_buf)
            at = pl.ds(mine_quarter, quarter)
            for dev in near_ids:
                ship(whole.at[at], whole.at[at], dev)

        def leave(h):
            at = pl.ds(base + h * half, half)
            copy = pltpu.make_async_copy(whole.at[at], sums_out.at[at], refs["sum_sem"].at[sems, h])
            copy.start()
            ended.append(copy)

        def spread_pair():
            land(near_buf)
            at = pl.ds(mine_half, half)
            ship(whole.at[at], whole.at[at], pair_id)
            leave(core)

        def done():
            land(pair_buf)
            leave(1 - core)
            return True

        def near_only():
            land(near_buf)
            got = ar[pl.ds(mine, shard)]
            for d in range(near - 1):
                got = got + near_buf[d]
            whole[pl.ds(mine, shard)] = got
            for dev in near_ids:
                ship(whole.at[pl.ds(mine, shard)], whole.at[pl.ds(mine, shard)], dev)

        if far == 1:
            return fill, iter((to_near, near_only, spread_pair, done))
        return fill, iter((to_near, to_far, spread_far, spread_near, spread_pair, done))

    for name in ("acc2", "acc3", "acc_o1", "acc_o2", "total"):
        refs[name][...] = jnp.zeros_like(refs[name])
    none = jnp.zeros((2 * M, LANES), bf16)
    for g in range(G):
        for name in ("d2", "d3"):
            refs[name][g][0] = none
            refs[name][g][H + 1] = none

    every = range(G)
    moving, ended = {}, []

    def advance(*names):
        for name in names:
            if name not in moving:
                continue
            copy = next(moving[name])()
            if copy is not None:
                del moving[name]

    def reduce(name, blocks):
        fill, moving[name] = reducer(name)
        fill(blocks)

    def wide_blocks(value):
        return [value[:, h * LANES : (h + 1) * LANES] for h in range(sz.wide // LANES)]

    def mid_blocks(acc):
        value = acc[...]
        rest = value[:, LANES:]
        return [value[:, :LANES], cat([rest[: n3 // 2], rest[n3 // 2 :]], 1)]

    greet()
    prepare()
    for g in every:
        for k in range(2 * NB):
            if (g, k) != (0, 0):
                in_copy(x_hbm, 0, g, k).start()
    for g in every:
        before, body, after = conv_first(g)
        if g == 0:
            run((before, body, nothing))
            pl.semaphore_wait(barrier, len(partners))
            after()
        else:
            run((before, body, after))
    for g in every:
        run(after_first(g))
        if g == 0:
            prepare_rest()
            refs["acc1"][...] = jnp.zeros_like(refs["acc1"])
    for g in every:
        run(spread(1, g, refs["p1"][g]))
        run(second(g), flat=True)
    for g in every:
        run(spread(2, g, refs["p2"][g]))
        run(third(g), out_layer(g))
    for g in every:
        run(spread(3, g, refs["q"][g]), mid_kernel_grad(g, refs["p2"][g], refs["d3"][g], refs["acc3"]))
        run(back_layer(4, g, t3, refs["d2"][g], refs["total"].at[1], refs["slope2"][g]), flat=True)
    for g in every:
        run(spread(4, g, refs["q"][g]), mid_kernel_grad(g, refs["p1"][g], refs["d2"][g], refs["acc2"]))
        if g == G - 1:
            upper, lower = refs["acc_o1"][...], refs["acc_o2"][...]
            outs = cat([upper[:M] + upper[M : 2 * M] + lower[:M], upper[2 * M :] + lower[M:]], 0)
            reduce("rest", wide_blocks(outs) + mid_blocks(refs["acc3"]) + mid_blocks(refs["acc2"]))
        run(back_layer(5, g, t2, None, refs["total"].at[0], refs["slope1"][g]), flat=True)
    advance("rest")
    lane = lax.broadcasted_iota(jnp.int32, (1, LANES), 1)
    sums = [jnp.sum(refs["total"][i], axis=1, keepdims=True) for i in range(3)]
    biases = jnp.where(lane == 0, sums[0], jnp.where(lane == 1, sums[1], sums[2]))
    for g in every:
        run(spread(5, g, refs["q"][g]), flat=True)
        run(first_kernel_grad(g), steps=2 * NB)
        if g < G - 1:
            advance("rest")
    reduce("taps", wide_blocks(refs["acc1"]) + [biases])
    advance("rest", "taps")
    for g in every:
        run(input_grad(g), steps=2 * NB)
        advance("rest", "taps")
    while moving:
        advance(*list(moving))

    for copy in ended:
        copy.wait()
    for slot in range(2):
        cotangent(slot, slot).wait()
    for g in every:
        for k in range(2 * NB):
            again(g, k)[1].wait()
    for g in every:
        for e in range(EXCHANGES - 2, EXCHANGES):
            for kind in range(2):
                landed(e, g, kind, "send")


def call_a(sz, x, dy, heights, widths, k1, k2, k3, ko, b1, b2, b3):
    G, H, W, M, N = sz.groups, sz.height, sz.width, sz.mid, LANES
    n3 = 3 * M
    names, shapes = [], []

    def add(name, *what):
        names.append((name, len(what)))
        shapes.extend(what)

    def per_group(name, shape, dtype):
        add(name, *[pltpu.VMEM(shape, dtype) for _ in range(G)])

    add("buf", pltpu.VMEM((sz.images, H, W, sz.wide), f32))
    per_group("a0", (H, N, 2 * sz.wide), bf16)
    per_group("act", (H, M, N), f32)
    per_group("carry", (2, n3, N), f32)
    for name in ("slope1", "slope2"):
        per_group(name, (H, M, N), f32)
    per_group("slope3", (H + 2, M, N), f32)
    for name in ("p1", "p2", "q"):
        per_group(name, (H + 2, 2 * n3, N), bf16)
    for name in ("d3", "d2"):
        per_group(name, (H + 2, 2 * M, N), bf16)
    add("a3", pltpu.VMEM((2, sz.block, 2 * M, N), bf16))
    add("w1", pltpu.VMEM((9 * M, 3 * sz.wide), bf16))
    for name in ("w2", "w3", "t2", "t3"):
        add(name, pltpu.VMEM((2 * n3, n3), bf16))
    add("ko", pltpu.VMEM((2 * M, sz.wide), bf16))
    add("met", pltpu.VMEM((G, M, N), f32))
    add("bias", pltpu.VMEM((3, M, N), f32))
    E = EXCHANGES
    add("rim", pltpu.VMEM((G, 2, M, N), f32))
    add("msg", pltpu.VMEM((2, G, M, N), f32))
    add("rowmsg", pltpu.VMEM((2, G, 2, M, N), f32))
    add("cormsg", pltpu.VMEM((2, G, 2, 8, N), f32))
    add("sideway", pltpu.VMEM((2, G, 2, M, N), f32))
    add("updown", pltpu.VMEM((2, G, 2 * M + 32, N), f32))
    add("acc1", pltpu.VMEM((9 * M, sz.wide), f32))
    add("acc2", pltpu.VMEM((n3, n3), f32))
    add("acc3", pltpu.VMEM((n3, n3), f32))
    add("acc_o1", pltpu.VMEM((2 * M + 16, sz.wide), f32))
    add("acc_o2", pltpu.VMEM((M + 16, sz.wide), f32))
    add("total", pltpu.VMEM((3, M, N), f32))
    U = sz.units
    add("ar", pltpu.VMEM((U, 8, N), f32))
    add("ar_all", pltpu.VMEM((U, 8, N), f32))
    for part, (_, units, shard) in sz.parts.items():
        near = sz.cols // 2 * sz.lows[part]
        far = sz.rows // sz.lows[part]
        add("pair_" + part, pltpu.VMEM((units // 2, 8, N), f32))
        add("near_" + part, pltpu.VMEM((max(near - 1, 1), units // 2 // near, 8, N), f32))
        add("far_" + part, pltpu.VMEM((max(far - 1, 1), shard, 8, N), f32))
    add("sum_sem", pltpu.SemaphoreType.DMA((len(sz.parts), 2)))
    add("in_sem", pltpu.SemaphoreType.DMA((2, G, 2 * sz.blocks)))
    add("k1_sem", pltpu.SemaphoreType.DMA)
    for name, value in zip(SMALL, (k2, k3, ko, b1, b2, b3)):
        add(name, pltpu.VMEM(value.shape, f32))
    add("small_sem", pltpu.SemaphoreType.DMA((len(SMALL),)))
    add("again_sem", pltpu.SemaphoreType.DMA((2, G, 2 * sz.blocks)))
    add("ring_sem", pltpu.SemaphoreType.DMA((2,)))
    add("ring", pltpu.VMEM((2, sz.per_group, sz.block // 4, W, sz.wide), f32))
    add("inside", pltpu.VMEM((sz.images, W, N), f32))
    add("wb", pltpu.VMEM((sz.wide, 9 * n3), bf16))
    add("out_sem", pltpu.SemaphoreType.DMA((G, sz.blocks)))
    add("send", pltpu.SemaphoreType.DMA((E, G, 2)))
    add("recv", pltpu.SemaphoreType.DMA((E, G, 2)))
    add("ar_send", pltpu.SemaphoreType.DMA((len(sz.parts), 6)))
    add("ar_recv", pltpu.SemaphoreType.DMA((len(sz.parts), 6)))
    grouped = ("a0", "act", "carry", "slope1", "slope2", "slope3", "p1", "p2", "q", "d3", "d2")

    def whole_kernel(*args):
        refs = {"io": args[:14]}
        at = 14
        for name, size in names:
            held = args[at : at + size]
            refs[name] = held if name in grouped else held[0]
            at += size
        kernel_a(sz, refs)

    hbm = pl.BlockSpec(memory_space=pl.ANY)
    vmem = pl.BlockSpec(memory_space=pltpu.VMEM)
    smem = pl.BlockSpec(memory_space=pltpu.SMEM)
    return pl.pallas_call(
        whole_kernel,
        out_shape=(
            jax.ShapeDtypeStruct(x.shape, f32),
            jax.ShapeDtypeStruct((G, H, 2 * M, N), bf16),
            jax.ShapeDtypeStruct((U, 8, N), f32),
        ),
        in_specs=[hbm, hbm, smem, smem] + [hbm] * 7,
        out_specs=(hbm, hbm, hbm),
        scratch_shapes=shapes,
        compiler_params=pltpu.CompilerParams(
            collective_id=0, has_side_effects=True, vmem_limit_bytes=63 * 2**20
        ),
        name="block_chain",
    )(x, dy, heights, widths, k1, k2, k3, ko, b1, b2, b3)


def kernel_b(
    sz, rows, x_hbm, g_hbm, a3_hbm, sums_hbm, ko_hbm, bo, out_hbm, grad_hbm, g1_hbm, g2_hbm, g3_hbm, go_hbm, s1, s2, s3, so,
    x, grad, a3, sums, ko, wo, g1, g2, g3, go, in_sem, out_sem, sums_sem,
):
    G, W, M = sz.groups, sz.width, sz.mid
    n3 = 3 * M
    chunks = sz.height // rows

    def copies_in(c):
        at = (slice(None), pl.ds(c * rows, rows))
        pairs = ((a3_hbm, a3), (x_hbm, x), (g_hbm, grad))
        return [pltpu.make_async_copy(s.at[at], d.at[at], in_sem.at[i, c]) for i, (s, d) in enumerate(pairs)]

    def copies_out(c):
        at = (slice(None), pl.ds(c * rows, rows))
        return [
            pltpu.make_async_copy(grad.at[at], grad_hbm.at[at], out_sem.at[0, c]),
            pltpu.make_async_copy(x.at[at], out_hbm.at[at], out_sem.at[1, c]),
        ]

    early = pltpu.make_async_copy(ko_hbm, ko, sums_sem.at[0])
    sums_in = pltpu.make_async_copy(sums_hbm, sums, sums_sem.at[1])
    sums_out = [
        pltpu.make_async_copy(s, d, sums_sem.at[2 + i])
        for i, (s, d) in enumerate(((g1, g1_hbm), (g2, g2_hbm), (g3, g3_hbm), (go, go_hbm)))
    ]
    early.start()
    for c in range(chunks):
        for copy in copies_in(c):
            copy.start()
        if c == 0:
            sums_in.start()
    early.wait()
    hi, lo = halves(ko[...].T * GAIN)
    wo[...] = cat([hi, hi, lo], 1)
    add = bo[...] * GAIN

    def body(c, carry):
        a3_in, x_in, grad_in = copies_in(c)
        grad_out, x_out = copies_out(c)
        a3_in.wait()
        x_in.wait()
        for k in range(rows):
            i = c * rows + k
            act = cat([a3[g, i] for g in range(G)], 1)
            branch = dot(wo[...], cat([act, act[:M]], 0)).T
            for n in range(sz.images):
                x[n, i] = x[n, i] + (branch[n * W : (n + 1) * W] + add)
        x_out.start()
        grad_in.wait()
        grad_out.start()
        return carry

    def take(at, count):
        return sums[at : at + count].reshape(count * 8, LANES)

    lax.fori_loop(0, chunks - 1, body, 0)

    sums_in.wait()
    at = sz.parts["taps"][0]
    for h in range(sz.wide // LANES):
        part = take(at, 9 * M // 8)
        at += 9 * M // 8
        for t in range(3):
            for b in range(3):
                lo = (t * 3 + b) * M
                g1[2 - t, 2 - b, :, h * LANES : (h + 1) * LANES] = part[lo : lo + M]
    rest = take(at, M // 8).T
    s1[...] = rest[0:1]
    s2[...] = rest[1:2]
    s3[...] = rest[2:3]
    at = sz.parts["rest"][0]
    for h in range(sz.wide // LANES):
        part = take(at, (M + 16) // 8)
        at += (M + 16) // 8
        go[:, h * LANES : (h + 1) * LANES] = part[:M]
        so[:, h * LANES : (h + 1) * LANES] = part[M : M + 1]
    for ref in (g3, g2):
        big, rest = take(at, n3 // 8), take(at + n3 // 8, n3 // 16)
        at += n3 // 8 + n3 // 16
        rest = cat([rest[:, :M], rest[:, M:]], 0)
        for b in range(3):
            sl = slice(b * M, (b + 1) * M)
            ref[0, b] = big[sl, :M]
            ref[1, b] = big[sl, M:]
            ref[2, b] = rest[sl]
    for copy in sums_out:
        copy.start()

    lax.fori_loop(chunks - 1, chunks, body, 0)

    def finish(c, carry):
        for copy in copies_out(c):
            copy.wait()
        return carry

    lax.fori_loop(0, chunks, finish, 0)
    for copy in sums_out:
        copy.wait()


def call_b(sz, x, grad, a3, sums, ko, bo):
    M = sz.mid
    rows = 8
    hbm = pl.BlockSpec(memory_space=pl.ANY)
    vmem = pl.BlockSpec(memory_space=pltpu.VMEM)
    grads = ((3, 3, M, sz.wide), (3, 3, M, M), (3, 3, M, M), (M, sz.wide))
    small = ((1, M), (1, M), (1, M), (1, sz.wide))
    return pl.pallas_call(
        functools.partial(kernel_b, sz, rows),
        out_shape=tuple(jax.ShapeDtypeStruct(s, f32) for s in (x.shape, x.shape) + grads + small),
        in_specs=[hbm] * 5 + [vmem],
        out_specs=(hbm,) * 6 + (vmem,) * 4,
        scratch_shapes=[
            pltpu.VMEM(x.shape, f32),
            pltpu.VMEM(x.shape, f32),
            pltpu.VMEM(a3.shape, bf16),
            pltpu.VMEM(sums.shape, f32),
            pltpu.VMEM(ko.shape, f32),
            pltpu.VMEM((sz.wide, 3 * M), bf16),
        ]
        + [pltpu.VMEM(s, f32) for s in grads]
        + [
            pltpu.SemaphoreType.DMA((3, sz.height // rows)),
            pltpu.SemaphoreType.DMA((2, sz.height // rows)),
            pltpu.SemaphoreType.DMA((6,)),
        ],
        compiler_params=pltpu.CompilerParams(vmem_limit_bytes=60 * 2**20),
        name="wide_outputs",
    )(x, grad, a3, sums, ko, bo)


def body(rows, cols, x, k1, b1, k2, b2, k3, b3, ko, bo, dy, heights, widths):
    wide, mid = k1.shape[2:]
    sz = Sizes(x.shape, mid, rows, cols)
    k1 = jnp.swapaxes(k1, 2, 3)
    grad, a3, sums = call_a(
        sz, x, dy, heights, widths, k1.reshape(9 * mid, wide), k2, k3, ko, b1[None], b2[None], b3[None]
    )
    out, grad, g1, g2, g3, go, s1, s2, s3, so = call_b(sz, x, grad, a3, sums, ko, bo[None])
    return (
        out,
        grad,
        jnp.swapaxes(g1, 2, 3),
        s1.reshape(mid),
        g2,
        s2.reshape(mid),
        g3,
        s3.reshape(mid),
        go,
        so.reshape(wide),
    )


def solution(mesh):
    tiled = P(None, "rows", "cols", None)
    return jax.shard_map(
        functools.partial(body, mesh.shape["rows"], mesh.shape["cols"]),
        mesh=mesh,
        in_specs=(tiled,) + (P(),) * 8 + (tiled, P(), P()),
        out_specs=(tiled, tiled) + (P(),) * 8,
        check_vma=False,
    )
```
